32 devices in a mesh: img: 8 (over z, y), row: 4 (over x, core).
Axes of the slice: x: 2, y: 2, z: 4, core: 2. Of those that a mesh axis runs over, the one named last changes fastest.
Arguments:
- stem_input: bfloat16 [32, 96, 96, 64], P('img', 'row'), may hold values from -6 to 6
- group: int32 [32], P('img'), may hold values 0 or 1
- conv_in: bfloat16 [64, 64], replicated, may hold values from -0.75 to 0.75
- conv_mid: bfloat16 [64, 9, 64], replicated, may hold values from -0.25 to 0.25
- conv_out: bfloat16 [64, 256], replicated, may hold values from -0.75 to 0.75
- conv_skip: bfloat16 [64, 256], replicated, may hold values from -0.75 to 0.75
- norm_gain: float32 [384], replicated, may hold values from 0.5 to 1.5
- norm_bias: float32 [384], replicated, may hold values from -4 to 4
- patch_weight: bfloat16 [4096, 768], replicated, may hold values from -0.09375 to 0.09375
- patch_bias: float32 [768], replicated, may hold values from -6 to 6
- attn_gain: float32 [768], replicated, may hold values from 0.5 to 1.5
- attn_bias: float32 [768], replicated, may hold values from -4 to 4
- qkv_weight: bfloat16 [768, 2304], replicated, may hold values from -0.21875 to 0.21875
- out_weight: bfloat16 [768, 768], replicated, may hold values from -1.75 to 1.75
- mlp_gain: float32 [768], replicated, may hold values from 0.5 to 1.5
- mlp_bias: float32 [768], replicated, may hold values from -4 to 4
- up_weight: bfloat16 [768, 3072], replicated, may hold values from -0.21875 to 0.21875
- up_bias: float32 [3072], replicated, may hold values from -6 to 6
- down_weight: bfloat16 [3072, 768], replicated, may hold values from -0.109375 to 0.109375
- down_bias: float32 [768], replicated, may hold values from -4 to 4
- cotangent: bfloat16 [32, 576, 768], P('img', 'row'), may hold values from -6 to 6
Outputs:
- block_out: bfloat16 [32, 576, 768], P('img', 'row')
- input_grad: float32 [32, 96, 96, 64], P('img', 'row')
- grad_conv_in: float32 [64, 64], P('row')
- grad_conv_mid: float32 [64, 9, 64], P('row')
- grad_conv_out: float32 [64, 256], P('row')
- grad_conv_skip: float32 [64, 256], P('row')
- grad_norm_gain: float32 [384], P('row')
- grad_norm_bias: float32 [384], P('row')
- grad_patch_weight: float32 [4096, 768], P('row')
- grad_patch_bias: float32 [768], P('row')
- grad_attn_gain: float32 [768], P('row')
- grad_attn_bias: float32 [768], P('row')
- grad_qkv_weight: float32 [768, 2304], P('row')
- grad_out_weight: float32 [768, 768], P('row')
- grad_mlp_gain: float32 [768], P('row')
- grad_mlp_bias: float32 [768], P('row')
- grad_up_weight: float32 [768, 3072], P('row')
- grad_up_bias: float32 [3072], P('row')
- grad_down_weight: float32 [3072, 768], P('row')
- grad_down_bias: float32 [768], P('row')
The draws below stay inside these ranges and needn't reach their ends.
Inputs may be any that keep to these rules, and one draw needn't show every extreme that they name: `group`: 0 marks a 224px image, whose valid cells are the top left 56 x 56 of its map; 1 a 384px image, all 96 x 96 cells valid.
All inputs are finite; a program needn't handle non-finite values. No bound on the sum of `group` on one device may be relied on, other than what follows from the above.
Results may differ from the reference program's by a relative error of at most 0.017.
Values may be sent and summed in bfloat16 or wider, within the bound.
No kernel may reach another device: no remote copies, remote signals or barrier semaphores. Data moves between devices by JAX's collectives and lax.ppermute only.
A program may use at most 256 MiB of HBM per device.

```python
import jax
import jax.numpy as jnp
from jax import lax

C0 = 64
C3 = 256
GROUPS = 32
D = 768
HEADS = 12
HEAD_DIM = 64
FF = 3072
PATCH = 4
FULL = 96
SMALL = 56
IMAGES = 32
TOK = 576


def touch_ends(values, key, smallest, high):
    longest = values.shape.index(max(values.shape))
    spots = []
    for shift in (0, 1):
        where = [jax.random.randint(jax.random.fold_in(key, axis), (), 0, length) for axis, length in enumerate(values.shape)]
        where[longest] = (where[longest] + shift) % values.shape[longest]
        spots.append(tuple(where))
    return values.at[spots[0]].set(smallest).at[spots[1]].set(high)


def shard_levels(own_key, extent, shards, smallest, top_value):
    def one(position, blocks):
        draws = jax.random.uniform(jax.random.fold_in(jax.random.fold_in(own_key, 6), position), (blocks,), jnp.float32, smallest / len(shards), top_value / len(shards))
        return jnp.repeat(jnp.exp(draws), extent[position] // blocks).reshape((-1,) + (1,) * (len(extent) - position - 1))

    factor_of = one(*shards[0])
    for cut in shards[1:]:
        factor_of = factor_of * one(*cut)
    return factor_of


def centred(own_key, dims, spread, bound, cuts=(), dtype=jnp.bfloat16):
    drawn = spread * jax.random.normal(own_key, dims, jnp.float32)
    if cuts:
        drawn = drawn * shard_levels(own_key, dims, cuts, -0.22, 0.18)
    return jnp.clip(drawn, -bound, bound).astype(dtype)


def setup_inputs(seed: int = 0) -> dict:
    key_list = jax.random.split(jax.random.key(seed), 22)
    return {
        "stem_input": centred(key_list[0], (IMAGES, FULL, FULL, C0), 1.0, 6.0, ((0, 8), (1, 4))),
        "group": touch_ends((jax.random.randint(key_list[1], (IMAGES,), 0, 2) < 1).astype(jnp.int32), jax.random.fold_in(key_list[1], 1), 0, 1),
        "conv_in": centred(key_list[2], (C0, C0), C0 ** -0.5, 0.75),
        "conv_mid": centred(key_list[3], (C0, 9, C0), (9 * C0) ** -0.5, 0.25),
        "conv_out": centred(key_list[4], (C0, C3), C0 ** -0.5, 0.75),
        "conv_skip": centred(key_list[5], (C0, C3), C0 ** -0.5, 0.75),
        "norm_gain": jnp.clip(1.0 + 0.1 * jax.random.normal(key_list[6], (2 * C0 + C3,), jnp.float32), 0.5, 1.5),
        "norm_bias": centred(key_list[7], (2 * C0 + C3,), 0.3, 4.0, (), jnp.float32),
        "patch_weight": centred(key_list[8], (PATCH * PATCH * C3, D), (PATCH * PATCH * C3) ** -0.5, 0.09375),
        "patch_bias": centred(key_list[9], (D,), 0.5, 6.0, (), jnp.float32),
        "attn_gain": jnp.clip(1.0 + 0.1 * jax.random.normal(key_list[10], (D,), jnp.float32), 0.5, 1.5),
        "attn_bias": centred(key_list[11], (D,), 0.3, 4.0, (), jnp.float32),
        "qkv_weight": centred(key_list[12], (D, 3 * D), D ** -0.5, 0.21875),
        "out_weight": centred(key_list[13], (D, D), (D // 64) ** -0.5, 1.75),
        "mlp_gain": jnp.clip(1.0 + 0.1 * jax.random.normal(key_list[14], (D,), jnp.float32), 0.5, 1.5),
        "mlp_bias": centred(key_list[15], (D,), 0.3, 4.0, (), jnp.float32),
        "up_weight": centred(key_list[16], (D, FF), D ** -0.5, 0.21875),
        "up_bias": centred(key_list[17], (FF,), 0.5, 6.0, (), jnp.float32),
        "down_weight": centred(key_list[18], (FF, D), FF ** -0.5, 0.109375),
        "down_bias": centred(key_list[19], (D,), 0.3, 4.0, (), jnp.float32),
        "cotangent": centred(key_list[20], (IMAGES, TOK, D), 1.0, 6.0, ((0, 8), (1, 4))),
    }


@jax.custom_vjp
def low(v):
    return lax.optimization_barrier(v.astype(jnp.bfloat16)).astype(jnp.float32)

@jax.custom_vjp
def low_back(v):
    return v

def low_keep(v):
    return (low(v), None)

def low_pass(kept, grad):
    return (grad,)

def back_keep(v):
    return (v, None)

def back_low(kept, grad):
    return (low(grad),)
low.defvjp(low_keep, low_pass)
low_back.defvjp(back_keep, back_low)

def smooth_gelu(values):
    return jax.nn.gelu(values, approximate=False)

def matmul_high(left, right):
    return jnp.dot(left, right, precision=lax.Precision.HIGHEST)

def group_norm(values, cell_mask, count, gain, bias):
    height, width, chans = values.shape
    split = (height * width, GROUPS, chans // GROUPS)
    masked = values * cell_mask[:, :, None]
    first_sum = lax.optimization_barrier(jnp.sum(masked.reshape(split), axis=(0, 2)))
    second_sum = lax.optimization_barrier(jnp.sum((masked * values).reshape(split), axis=(0, 2)))
    mean = first_sum / count
    rstd = lax.rsqrt(second_sum / count - mean * mean + 1e-05)
    normal = ((values.reshape(split) - mean[None, :, None]) * rstd[None, :, None]).reshape(values.shape)
    return normal * gain + bias

def layer_norm(values, gain, bias):
    mean = lax.optimization_barrier(jnp.mean(values, axis=-1, keepdims=True))
    centered = values - mean
    return centered * lax.rsqrt(lax.optimization_barrier(jnp.mean(centered * centered, axis=-1, keepdims=True)) + 1e-05) * gain + bias

def image_forward(image_in, image_side, params):
    conv_in, conv_mid, conv_out, conv_skip, norm_gain, norm_bias, patch_weight, patch_bias, attn_gain, attn_bias, qkv_weight, out_weight, mlp_gain, mlp_bias, up_weight, up_bias, down_weight, down_bias = params
    highest = lax.Precision.HIGHEST
    inside = (jnp.arange(FULL) < image_side).astype(jnp.float32)
    cell_mask = inside[:, None] * inside[None, :]
    cells = (image_side * image_side).astype(jnp.float32)
    mask_chan = cell_mask[:, :, None]
    inputs = image_in * mask_chan
    first_conv = low_back(jnp.einsum('hwc,cd->hwd', inputs, conv_in, precision=highest))
    first_act = low(smooth_gelu(group_norm(first_conv, cell_mask, cells * (C0 // GROUPS), norm_gain[:C0], norm_bias[:C0])) * mask_chan)
    padded = jnp.pad(first_act, ((1, 1), (1, 1), (0, 0)))
    mid_conv = jnp.zeros((FULL, FULL, C0), jnp.float32)
    for offset in range(9):
        shift_row = offset // 3
        shift_col = offset % 3
        mid_conv = mid_conv + jnp.einsum('hwc,cd->hwd', padded[shift_row:shift_row + FULL, shift_col:shift_col + FULL], conv_mid[:, offset, :], precision=highest)
    mid_conv = low_back(mid_conv)
    mid_act = low(smooth_gelu(group_norm(mid_conv, cell_mask, cells * (C0 // GROUPS), norm_gain[C0:2 * C0], norm_bias[C0:2 * C0])) * mask_chan)
    last_conv = low_back(jnp.einsum('hwc,cd->hwd', mid_act, conv_out, precision=highest))
    skip_conv = low_back(jnp.einsum('hwc,cd->hwd', inputs, conv_skip, precision=highest))
    joined = group_norm(last_conv, cell_mask, cells * (C3 // GROUPS), norm_gain[2 * C0:], norm_bias[2 * C0:]) + skip_conv
    stem = low(smooth_gelu(joined) * mask_chan)
    side_tok = FULL // PATCH
    patches = stem.reshape(side_tok, PATCH, side_tok, PATCH, C3).transpose(0, 2, 1, 3, 4).reshape(TOK, PATCH * PATCH * C3)
    hidden = low_back(matmul_high(patches, patch_weight)) + patch_bias
    normed = low(layer_norm(hidden, attn_gain, attn_bias))
    qkv_all = low(low_back(matmul_high(normed, qkv_weight))).reshape(TOK, 3, HEADS, HEAD_DIM)
    query = qkv_all[:, 0]
    key_part = qkv_all[:, 1]
    value_part = qkv_all[:, 2]
    positions = jnp.arange(TOK)
    token_keep = (positions // side_tok < image_side // PATCH) & (positions % side_tok < image_side // PATCH)
    scores = low_back(jnp.einsum('qhe,khe->hqk', query, key_part, precision=highest) * HEAD_DIM ** (-0.5))
    scores = jnp.where(token_keep[None, None, :], scores, -1000000000.0)
    row_top = lax.optimization_barrier(jnp.max(scores, axis=2, keepdims=True))
    expo = jnp.exp(scores - row_top)
    probs = low(expo / lax.optimization_barrier(jnp.sum(expo, axis=2, keepdims=True)))
    mixed = low(low_back(jnp.einsum('hqk,khe->qhe', probs, value_part, precision=highest))).reshape(TOK, D)
    hidden2 = hidden + low_back(matmul_high(mixed, out_weight))
    normed2 = low(layer_norm(hidden2, mlp_gain, mlp_bias))
    pre_act = low_back(matmul_high(normed2, up_weight)) + up_bias
    activ = low(smooth_gelu(pre_act))
    final = hidden2 + low_back(matmul_high(activ, down_weight)) + down_bias
    return final * token_keep.astype(jnp.float32)[:, None]

def reference(stem_input, group, conv_in, conv_mid, conv_out, conv_skip, norm_gain, norm_bias, patch_weight, patch_bias, attn_gain, attn_bias, qkv_weight, out_weight, mlp_gain, mlp_bias, up_weight, up_bias, down_weight, down_bias, cotangent):
    params = tuple((item.astype(jnp.float32) for item in (conv_in, conv_mid, conv_out, conv_skip, norm_gain, norm_bias, patch_weight, patch_bias, attn_gain, attn_bias, qkv_weight, out_weight, mlp_gain, mlp_bias, up_weight, up_bias, down_weight, down_bias)))
    image_all = stem_input.astype(jnp.float32)
    cot_all = cotangent.astype(jnp.float32)

    def per_image(carry, item):
        image_in, image_group, image_cot = item
        image_side = jnp.where(image_group == 1, FULL, SMALL).astype(jnp.int32)
        result, pull = jax.vjp(lambda image_val, param_val: image_forward(image_val, image_side, param_val), image_in, params)
        grad_image, grad_params = pull(image_cot)
        carry = jax.tree.map(lambda summed, added: summed + added, carry, grad_params)
        return (carry, (result.astype(jnp.bfloat16), grad_image))
    zeros = tuple((jnp.zeros_like(item) for item in params))
    sums, (outputs, grad_images) = lax.scan(per_image, zeros, (image_all, group, cot_all))
    return (outputs, grad_images) + tuple(sums)
```

```python
import jax
import jax.numpy as jnp
from jax import lax
from jax.sharding import PartitionSpec as P

GROUPS = 32
HEADS = 12
HEAD_DIM = 64
PATCH = 4
FULL = 96
SMALL = 56
SIDE = FULL // PATCH
TOK = SIDE * SIDE
f32 = jnp.float32
bf16 = jnp.bfloat16


def mm(a, b):
    return lax.dot_general(a, b, (((1,), (0,)), ((), ())), preferred_element_type=f32)


def mm_nt(a, b):
    return lax.dot_general(a, b, (((1,), (1,)), ((), ())), preferred_element_type=f32)


def mm_tn(a, b):
    return lax.dot_general(a, b, (((0,), (0,)), ((), ())), preferred_element_type=f32)


def gelu_both(z):
    cdf = 0.5 * (1.0 + lax.erf(z * 0.7071067811865476))
    pdf = 0.3989422804014327 * jnp.exp(-0.5 * z * z)
    return z * cdf, cdf + z * pdf


def spread4(w):
    return jnp.kron(jnp.eye(PATCH, dtype=w.dtype), w)


def band(taps):
    c, _, d = taps.shape
    zero = jnp.zeros((c, d), taps.dtype)
    mats = []
    for di in range(3):
        rows = []
        for src in (0, 1, 2, 3, -1, 4):
            rows.append(
                [taps[:, 3 * di + src - j + 1] if abs(src - j) <= 1 else zero for j in range(PATCH)]
            )
        mats.append(jnp.block(rows))
    return mats


def fold_band(mats, c, d):
    taps = []
    srcs = (0, 1, 2, 3, -1, 4)
    for di in range(3):
        for dj in range(3):
            total = 0.0
            for j in range(PATCH):
                k = srcs.index(j + dj - 1)
                total = total + mats[di][k * c : (k + 1) * c, j * d : (j + 1) * d]
            taps.append(total)
    return jnp.stack(taps, axis=1)


def fold4(m, c, d):
    return sum(m[j * c : (j + 1) * c, j * d : (j + 1) * d] for j in range(PATCH))


def widen(v):
    c = v.shape[2] // PATCH
    g = v.reshape(PATCH, SIDE, SIDE, PATCH * c)
    up = jnp.pad(g[3:4, :-1], ((0, 0), (1, 0), (0, 0), (0, 0)))
    down = jnp.pad(g[0:1, 1:], ((0, 0), (0, 1), (0, 0), (0, 0)))
    g = jnp.concatenate([up, g, down], axis=0)
    left = jnp.pad(g[:, :, :-1, 3 * c :], ((0, 0), (0, 0), (1, 0), (0, 0)))
    right = jnp.pad(g[:, :, 1:, :c], ((0, 0), (0, 0), (0, 1), (0, 0)))
    g = jnp.concatenate([g, left, right], axis=-1)
    return g.reshape(PATCH + 2, TOK, 6 * c)


def conv3(wide, mats):
    c = wide.shape[2]
    out = 0.0
    for di in range(3):
        out = out + mm(wide[di : di + PATCH].reshape(PATCH * TOK, c), mats[di])
    return out


def group_matrix(chans, lanes):
    lane = jnp.arange(lanes) % chans // (chans // GROUPS)
    return (lane[:, None] == lane[None, :]).astype(f32)


def lane_group_sum(row, gmat):
    return jnp.dot(row, gmat, precision=lax.Precision.HIGHEST)


def gn_stats(v, keep, count, gmat):
    masked = v * keep
    s1 = lane_group_sum(jnp.sum(masked, axis=0, keepdims=True), gmat)
    s2 = lane_group_sum(jnp.sum(masked * v, axis=0, keepdims=True), gmat)
    mean = s1 / count
    rstd = lax.rsqrt(s2 / count - mean * mean + 1e-05)
    return mean, rstd


def gn_back(g, n, rstd, keep, count, gmat, gain):
    c1 = jnp.sum(g, axis=0, keepdims=True)
    c2 = jnp.sum(g * n, axis=0, keepdims=True)
    s1 = lane_group_sum(c1 * gain, gmat) / count
    s2 = lane_group_sum(c2 * gain, gmat) / count
    return rstd * (g * gain - s1 - n * s2) * keep, c2, c1


def ln_stats(h):
    mean = jnp.mean(h, axis=-1, keepdims=True)
    cen = h - mean
    rstd = lax.rsqrt(jnp.mean(cen * cen, axis=-1, keepdims=True) + 1e-05)
    return cen * rstd, rstd


def ln_back(gy, n, rstd, gain):
    gn = gy * gain
    gh = rstd * (
        gn - jnp.mean(gn, axis=-1, keepdims=True) - n * jnp.mean(gn * n, axis=-1, keepdims=True)
    )
    return gh, jnp.sum(gy * n, axis=0), jnp.sum(gy, axis=0)


def per_image(x, side, cot, params):
    (
        conv_in,
        conv_mid,
        conv_out,
        conv_skip,
        norm_gain,
        norm_bias,
        patch_weight,
        patch_bias,
        attn_gain,
        attn_bias,
        qkv_weight,
        out_weight,
        mlp_gain,
        mlp_bias,
        up_weight,
        up_bias,
        down_weight,
        down_bias,
    ) = params
    c0 = conv_in.shape[0]
    c3 = conv_out.shape[1]
    rows = PATCH * TOK
    pos = jnp.arange(TOK)
    limit = side // PATCH
    keep = ((pos // SIDE < limit) & (pos % SIDE < limit)).astype(f32)[:, None]
    keep4 = jnp.tile(keep, (PATCH, 1))
    cells = (side * side).astype(f32)
    x = (x.reshape(rows, PATCH * c0) * keep4.astype(bf16)).astype(bf16)
    g64 = group_matrix(c0, PATCH * c0)
    g256 = group_matrix(c3, PATCH * c3)
    gains = [jnp.tile(v, PATCH)[None] for v in (norm_gain[:c0], norm_gain[c0 : 2 * c0], norm_gain[2 * c0 :])]
    biases = [jnp.tile(v, PATCH)[None] for v in (norm_bias[:c0], norm_bias[c0 : 2 * c0], norm_bias[2 * c0 :])]
    n1count = cells * (c0 // GROUPS)
    n3count = cells * (c3 // GROUPS)
    w_in = spread4(conv_in)
    w_out = spread4(conv_out)
    w_skip = spread4(conv_skip)
    b_fwd = band(conv_mid)
    b_bwd = band(jnp.flip(conv_mid, axis=1).transpose(2, 1, 0))
    v1 = mm(x, w_in)
    m1, r1 = gn_stats(v1, keep4, n1count, g64)
    n1 = (v1 - m1) * r1
    a1, d1 = gelu_both(n1 * gains[0] + biases[0])
    p1 = (a1 * keep4).astype(bf16)
    wide = widen(p1.reshape(PATCH, TOK, PATCH * c0))
    v2 = conv3(wide, b_fwd)
    m2, r2 = gn_stats(v2, keep4, n1count, g64)
    n2 = (v2 - m2) * r2
    a2, d2 = gelu_both(n2 * gains[1] + biases[1])
    p2 = (a2 * keep4).astype(bf16)
    v3 = mm(p2, w_out)
    m3, r3 = gn_stats(v3, keep4, n3count, g256)
    n3 = (v3 - m3) * r3
    z3 = n3 * gains[2] + biases[2] + mm(x, w_skip)
    a3, d3 = gelu_both(z3)
    stem = (a3 * keep4).astype(bf16).reshape(PATCH, TOK, PATCH * c3)
    pw = patch_weight.reshape(PATCH, PATCH * c3, -1)
    hidden = patch_bias
    for i in range(PATCH):
        hidden = hidden + mm(stem[i], pw[i])
    na, ra = ln_stats(hidden)
    normed = (na * attn_gain + attn_bias).astype(bf16)
    qkv = mm(normed, qkv_weight).astype(bf16)
    qkv = qkv.reshape(TOK, 3, HEADS, HEAD_DIM).transpose(1, 2, 0, 3)
    q, k, v = qkv[0], qkv[1], qkv[2]
    scale = HEAD_DIM**-0.5
    scores = jnp.einsum("hqe,hke->hqk", q, k, preferred_element_type=f32) * scale
    scores = jnp.where(keep[:, 0] > 0, scores, -1000000000.0)
    expo = jnp.exp(scores - jnp.max(scores, axis=-1, keepdims=True))
    probs = expo / jnp.sum(expo, axis=-1, keepdims=True)
    probs_low = probs.astype(bf16)
    mixed = jnp.einsum("hqk,hke->hqe", probs_low, v, preferred_element_type=f32).astype(bf16)
    attended = mixed.transpose(1, 0, 2).reshape(TOK, -1)
    hidden2 = hidden + mm(attended, out_weight)
    nm, rm = ln_stats(hidden2)
    normed2 = (nm * mlp_gain + mlp_bias).astype(bf16)
    pre = mm(normed2, up_weight) + up_bias
    act, dact = gelu_both(pre)
    act = act.astype(bf16)
    block_out = ((hidden2 + mm(act, down_weight) + down_bias) * keep).astype(bf16)
    g_final = cot.astype(f32) * keep
    g_low = g_final.astype(bf16)
    grad_down_bias = jnp.sum(g_final, axis=0)
    grad_down = mm_tn(act, g_low)
    g_pre = mm_nt(g_low, down_weight) * dact
    grad_up_bias = jnp.sum(g_pre, axis=0)
    g_pre = g_pre.astype(bf16)
    grad_up = mm_tn(normed2, g_pre)
    g_ln, grad_mlp_gain, grad_mlp_bias = ln_back(mm_nt(g_pre, up_weight), nm, rm, mlp_gain)
    g_h2 = g_final + g_ln
    g_h2_low = g_h2.astype(bf16)
    grad_out = mm_tn(attended, g_h2_low)
    g_att = mm_nt(g_h2_low, out_weight).astype(bf16).reshape(TOK, HEADS, HEAD_DIM).transpose(1, 0, 2)
    g_v = jnp.einsum("hqk,hqe->hke", probs_low, g_att, preferred_element_type=f32)
    g_p = jnp.einsum("hqe,hke->hqk", g_att, v, preferred_element_type=f32)
    g_s = probs * (g_p - jnp.sum(g_p * probs, axis=-1, keepdims=True))
    g_s = g_s.astype(bf16)
    g_q = jnp.einsum("hqk,hke->hqe", g_s, k, preferred_element_type=f32) * scale
    g_k = jnp.einsum("hqk,hqe->hke", g_s, q, preferred_element_type=f32) * scale
    g_qkv = jnp.stack([g_q, g_k, g_v]).astype(bf16).transpose(2, 0, 1, 3).reshape(TOK, -1)
    grad_qkv = mm_tn(normed, g_qkv)
    g_ln, grad_attn_gain, grad_attn_bias = ln_back(mm_nt(g_qkv, qkv_weight), na, ra, attn_gain)
    g_h = g_h2 + g_ln
    grad_patch_bias = jnp.sum(g_h, axis=0)
    g_h = g_h.astype(bf16)
    grad_patch = jnp.concatenate([mm_tn(stem[i], g_h) for i in range(PATCH)], axis=0)
    g_stem = jnp.concatenate([mm_nt(g_h, pw[i]) for i in range(PATCH)], axis=0)
    g_z = g_stem * d3 * keep4
    g_z_low = g_z.astype(bf16)
    grad_skip = fold4(mm_tn(x, g_z_low), c0, c3)
    g_v3, gain3, bias3 = gn_back(g_z, n3, r3, keep4, n3count, g256, gains[2])
    g_v3 = g_v3.astype(bf16)
    grad_cout = fold4(mm_tn(p2, g_v3), c0, c3)
    g_2 = mm_nt(g_v3, w_out) * d2 * keep4
    g_v2, gain2, bias2 = gn_back(g_2, n2, r2, keep4, n1count, g64, gains[1])
    g_v2 = g_v2.astype(bf16)
    grad_mid = fold_band(
        [mm_tn(wide[di : di + PATCH].reshape(rows, 6 * c0), g_v2) for di in range(3)], c0, c0
    )
    g_wide = widen(g_v2.reshape(PATCH, TOK, PATCH * c0))
    g_1 = conv3(g_wide, b_bwd) * d1 * keep4
    g_v1, gain1, bias1 = gn_back(g_1, n1, r1, keep4, n1count, g64, gains[0])
    g_v1 = g_v1.astype(bf16)
    grad_in = fold4(mm_tn(x, g_v1), c0, c0)
    input_grad = (mm_nt(g_v1, w_in) + mm_nt(g_z_low, w_skip)) * keep4

    def lanes(v):
        return jnp.sum(v.reshape(PATCH, -1), axis=0)

    grads = (
        grad_in,
        grad_mid,
        grad_cout,
        grad_skip,
        jnp.concatenate([lanes(gain1), lanes(gain2), lanes(gain3)]),
        jnp.concatenate([lanes(bias1), lanes(bias2), lanes(bias3)]),
        grad_patch,
        grad_patch_bias,
        grad_attn_gain,
        grad_attn_bias,
        grad_qkv,
        grad_out,
        grad_mlp_gain,
        grad_mlp_bias,
        grad_up,
        grad_up_bias,
        grad_down,
        grad_down_bias,
    )
    return block_out, input_grad.reshape(PATCH, TOK, PATCH * c0), grads


def per_device(stem_input, group, *rest):
    params, cot = rest[:-1], rest[-1]
    images, row_count, col_count, c0 = stem_input.shape
    ranks = lax.axis_size("row")
    assert images == ranks
    side = jnp.where(group[lax.axis_index("row")] == 1, FULL, SMALL).astype(jnp.int32)
    strips = row_count // PATCH
    x = stem_input.reshape(images, strips, PATCH, SIDE, PATCH * c0).transpose(0, 2, 1, 3, 4)
    x = lax.all_to_all(x, "row", 0, 0, tiled=True)
    x = x.transpose(1, 0, 2, 3, 4).reshape(PATCH, TOK, PATCH * c0)
    cot_in = lax.all_to_all(cot, "row", 0, 0, tiled=True).reshape(TOK, -1)
    block_out, input_grad, grads = per_image(x, side, cot_in, params)
    block_out = block_out.reshape(images, -1, block_out.shape[-1])
    block_out = lax.all_to_all(block_out, "row", 0, 0, tiled=True)
    ig = input_grad.astype(bf16).reshape(PATCH, ranks, strips, SIDE, PATCH * c0).transpose(1, 0, 2, 3, 4)
    ig = lax.all_to_all(ig, "row", 0, 0, tiled=True)
    ig = ig.transpose(0, 2, 1, 3, 4).reshape(images, row_count, col_count, c0).astype(f32)
    big = [i for i, g in enumerate(grads) if g.size > 100000]
    sums = {}
    for i, s in zip(big, lax.psum([grads[i].astype(bf16) for i in big], ("img", "row"))):
        sums[i] = s
    small = [i for i in range(len(grads)) if i not in big]
    flat = jnp.concatenate([grads[i].reshape(-1) for i in small])
    flat = lax.psum(flat, ("img", "row"))
    at = 0
    for i in small:
        sums[i] = flat[at : at + grads[i].size].reshape(grads[i].shape)
        at += grads[i].size
    rank = lax.axis_index("row")
    shares = []
    for i in range(len(grads)):
        part = grads[i].shape[0] // ranks
        shares.append(lax.dynamic_slice_in_dim(sums[i], rank * part, part, 0).astype(f32))
    return (block_out, ig) + tuple(shares)


def solution(mesh):
    rep = P()
    in_specs = (P("img", "row", None, None), P("img")) + (rep,) * 18 + (P("img", "row", None),)
    dims = (2, 3, 2, 2, 1, 1, 2, 1, 1, 1, 2, 2, 1, 1, 2, 1, 2, 1)
    out_specs = (P("img", "row", None), P("img", "row", None, None)) + tuple(
        P("row", *([None] * (n - 1))) for n in dims
    )
    return jax.shard_map(
        per_device, mesh=mesh, in_specs=in_specs, out_specs=out_specs, check_vma=False
    )
```

```python
import jax
import jax.numpy as jnp
from jax import lax
from jax.experimental import pallas as pl
from jax.experimental.pallas import tpu as pltpu
from jax.sharding import PartitionSpec as P

GROUPS = 32
HEADS = 12
HEAD_DIM = 64
PATCH = 4
FULL = 96
SMALL = 56
SIDE = FULL // PATCH
TOK = SIDE * SIDE
f32 = jnp.float32
bf16 = jnp.bfloat16


def mm(a, b):
    return lax.dot_general(a, b, (((1,), (0,)), ((), ())), preferred_element_type=f32)


def mm_nt(a, b):
    return lax.dot_general(a, b, (((1,), (1,)), ((), ())), preferred_element_type=f32)


def mm_tn(a, b):
    return lax.dot_general(a, b, (((0,), (0,)), ((), ())), preferred_element_type=f32)


def gelu_both(z):
    cdf = 0.5 * (1.0 + lax.erf(z * 0.7071067811865476))
    pdf = 0.3989422804014327 * jnp.exp(-0.5 * z * z)
    return z * cdf, cdf + z * pdf


def spread4(w):
    return jnp.kron(jnp.eye(PATCH, dtype=w.dtype), w)


def band(taps):
    c, _, d = taps.shape
    zero = jnp.zeros((c, d), taps.dtype)
    mats = []
    for di in range(3):
        rows = []
        for src in (0, 1, 2, 3, -1, 4):
            rows.append(
                [taps[:, 3 * di + src - j + 1] if abs(src - j) <= 1 else zero for j in range(PATCH)]
            )
        mats.append(jnp.block(rows))
    return mats


def fold_band(mats, c, d):
    taps = []
    srcs = (0, 1, 2, 3, -1, 4)
    for di in range(3):
        for dj in range(3):
            total = 0.0
            for j in range(PATCH):
                k = srcs.index(j + dj - 1)
                total = total + mats[di][k * c : (k + 1) * c, j * d : (j + 1) * d]
            taps.append(total)
    return jnp.stack(taps, axis=1)


def fold4(m, c, d):
    return sum(m[j * c : (j + 1) * c, j * d : (j + 1) * d] for j in range(PATCH))


def widen(v):
    c = v.shape[2] // PATCH
    g = v.reshape(PATCH, SIDE, SIDE, PATCH * c)
    up = jnp.pad(g[3:4, :-1], ((0, 0), (1, 0), (0, 0), (0, 0)))
    down = jnp.pad(g[0:1, 1:], ((0, 0), (0, 1), (0, 0), (0, 0)))
    g = jnp.concatenate([up, g, down], axis=0)
    left = jnp.pad(g[:, :, :-1, 3 * c :], ((0, 0), (0, 0), (1, 0), (0, 0)))
    right = jnp.pad(g[:, :, 1:, :c], ((0, 0), (0, 0), (0, 1), (0, 0)))
    g = jnp.concatenate([g, left, right], axis=-1)
    return g.reshape(PATCH + 2, TOK, 6 * c)


def conv3(wide, mats):
    c = wide.shape[2]
    out = 0.0
    for di in range(3):
        out = out + mm(wide[di : di + PATCH].reshape(PATCH * TOK, c), mats[di])
    return out


def group_matrix(chans, lanes):
    lane = jnp.arange(lanes) % chans // (chans // GROUPS)
    return (lane[:, None] == lane[None, :]).astype(f32)


def lane_group_sum(row, gmat):
    return jnp.dot(row, gmat, precision=lax.Precision.HIGHEST)


def gn_stats(v, keep, count, gmat):
    masked = v * keep
    s1 = lane_group_sum(jnp.sum(masked, axis=0, keepdims=True), gmat)
    s2 = lane_group_sum(jnp.sum(masked * v, axis=0, keepdims=True), gmat)
    mean = s1 / count
    rstd = lax.rsqrt(s2 / count - mean * mean + 1e-05)
    return mean, rstd


def gn_back(g, n, rstd, keep, count, gmat, gain):
    c1 = jnp.sum(g, axis=0, keepdims=True)
    c2 = jnp.sum(g * n, axis=0, keepdims=True)
    s1 = lane_group_sum(c1 * gain, gmat) / count
    s2 = lane_group_sum(c2 * gain, gmat) / count
    return rstd * (g * gain - s1 - n * s2) * keep, c2, c1


def ln_stats(h):
    mean = jnp.mean(h, axis=-1, keepdims=True)
    cen = h - mean
    rstd = lax.rsqrt(jnp.mean(cen * cen, axis=-1, keepdims=True) + 1e-05)
    return cen * rstd, rstd


def ln_back(gy, n, rstd, gain):
    gn = gy * gain
    gh = rstd * (
        gn - jnp.mean(gn, axis=-1, keepdims=True) - n * jnp.mean(gn * n, axis=-1, keepdims=True)
    )
    return gh, jnp.sum(gy * n, axis=0), jnp.sum(gy, axis=0)


def attend_kernel(keep_ref, q_ref, k_ref, v_ref, o_ref, l_ref):
    scale = HEAD_DIM**-0.5
    valid = keep_ref[...] > 0
    outs = []
    for h in range(2):
        lanes = slice(h * HEAD_DIM, (h + 1) * HEAD_DIM)
        q, k, v = q_ref[:, lanes], k_ref[:, lanes], v_ref[:, lanes]
        s = jnp.where(valid, mm_nt(k, q) * scale, -1000000000.0)
        top = jnp.max(s, axis=0, keepdims=True)
        e = jnp.exp(s - top)
        total = jnp.sum(e, axis=0, keepdims=True)
        outs.append(mm_tn(v, e.astype(bf16)) / total)
        l_ref[0, h : h + 1, :] = top + jnp.log(total)
    o_ref[...] = jnp.concatenate(outs, axis=0).T.astype(bf16)

def attend(qkv, keep):
    tok, width3 = qkv.shape
    pairs = HEADS // 2
    two = 2 * HEAD_DIM
    def spec(kind):
        return pl.BlockSpec((tok, two), lambda h: (0, kind * pairs + h))
    return pl.pallas_call(
        attend_kernel, grid=(pairs,),
        in_specs=[pl.BlockSpec((tok, 1), lambda h: (0, 0)), spec(0), spec(1), spec(2)],
        out_specs=[spec(0), pl.BlockSpec((1, 2, tok), lambda h: (h, 0, 0))],
        out_shape=[jax.ShapeDtypeStruct((tok, width3 // 3), bf16), jax.ShapeDtypeStruct((pairs, 2, tok), f32)],
        compiler_params=pltpu.CompilerParams(vmem_limit_bytes=40*1024*1024),
        name="attend",
    )(keep, qkv, qkv, qkv)

def attend_back_kernel(keep_ref, q_ref, k_ref, v_ref, g_ref, l_ref, gq_ref, gk_ref, gv_ref):
    scale = HEAD_DIM**-0.5
    valid = keep_ref[...] > 0
    gqs, gks, gvs = [], [], []
    for h in range(2):
        lanes = slice(h * HEAD_DIM, (h + 1) * HEAD_DIM)
        q, k, v, g = q_ref[:, lanes], k_ref[:, lanes], v_ref[:, lanes], g_ref[:, lanes]
        s = jnp.where(valid, mm_nt(k, q) * scale, -1000000000.0)
        p = jnp.exp(s - l_ref[0, h : h + 1, :])
        gp = mm_nt(v, g)
        dot = jnp.sum(gp * p, axis=0, keepdims=True)
        gs = (p * (gp - dot)).astype(bf16)
        gvs.append(mm(p.astype(bf16), g))
        gks.append(mm(gs, q) * scale)
        gqs.append(mm_tn(k, gs) * scale)
    gq_ref[...] = jnp.concatenate(gqs, axis=0).T.astype(bf16)
    gk_ref[...] = jnp.concatenate(gks, axis=1).astype(bf16)
    gv_ref[...] = jnp.concatenate(gvs, axis=1).astype(bf16)

def attend_back(qkv, keep, g, logs):
    tok, width3 = qkv.shape
    pairs = HEADS // 2
    two = 2 * HEAD_DIM
    def spec(kind):
        return pl.BlockSpec((tok, two), lambda h: (0, kind * pairs + h))
    o = jax.ShapeDtypeStruct((tok, width3 // 3), bf16)
    return pl.pallas_call(
        attend_back_kernel, grid=(pairs,),
        in_specs=[pl.BlockSpec((tok, 1), lambda h: (0, 0)), spec(0), spec(1), spec(2), spec(0), pl.BlockSpec((1, 2, tok), lambda h: (h, 0, 0))],
        out_specs=[spec(0)] * 3,
        out_shape=[o, o, o],
        compiler_params=pltpu.CompilerParams(vmem_limit_bytes=40*1024*1024),
        name="attend_back",
    )(keep, qkv, qkv, qkv, g, logs)


def per_image(x, side, cot, params, flows):
    (
        conv_in,
        conv_mid,
        conv_out,
        conv_skip,
        norm_gain,
        norm_bias,
        patch_weight,
        patch_bias,
        attn_gain,
        attn_bias,
        qkv_weight,
        out_weight,
        mlp_gain,
        mlp_bias,
        up_weight,
        up_bias,
        down_weight,
        down_bias,
    ) = params
    c0 = conv_in.shape[0]
    c3 = conv_out.shape[1]
    rows = PATCH * TOK
    pos = jnp.arange(TOK)
    limit = side // PATCH
    keep = ((pos // SIDE < limit) & (pos % SIDE < limit)).astype(f32)[:, None]
    keep4 = jnp.tile(keep, (PATCH, 1))
    cells = (side * side).astype(f32)
    x = (x.reshape(rows, PATCH * c0) * keep4.astype(bf16)).astype(bf16)
    g64 = group_matrix(c0, PATCH * c0)
    g256 = group_matrix(c3, PATCH * c3)
    gains = [jnp.tile(v, PATCH)[None] for v in (norm_gain[:c0], norm_gain[c0 : 2 * c0], norm_gain[2 * c0 :])]
    biases = [jnp.tile(v, PATCH)[None] for v in (norm_bias[:c0], norm_bias[c0 : 2 * c0], norm_bias[2 * c0 :])]
    n1count = cells * (c0 // GROUPS)
    n3count = cells * (c3 // GROUPS)
    w_in = spread4(conv_in)
    w_out = spread4(conv_out)
    w_skip = spread4(conv_skip)
    b_fwd = band(conv_mid)
    b_bwd = band(jnp.flip(conv_mid, axis=1).transpose(2, 1, 0))
    v1 = mm(x, w_in)
    m1, r1 = gn_stats(v1, keep4, n1count, g64)
    n1 = (v1 - m1) * r1
    a1, d1 = gelu_both(n1 * gains[0] + biases[0])
    p1 = (a1 * keep4).astype(bf16)
    wide = widen(p1.reshape(PATCH, TOK, PATCH * c0))
    v2 = conv3(wide, b_fwd)
    m2, r2 = gn_stats(v2, keep4, n1count, g64)
    n2 = (v2 - m2) * r2
    a2, d2 = gelu_both(n2 * gains[1] + biases[1])
    p2 = (a2 * keep4).astype(bf16)
    v3 = mm(p2, w_out)
    m3, r3 = gn_stats(v3, keep4, n3count, g256)
    n3 = (v3 - m3) * r3
    z3 = n3 * gains[2] + biases[2] + mm(x, w_skip)
    a3, d3 = gelu_both(z3)
    stem = (a3 * keep4).astype(bf16).reshape(PATCH, TOK, PATCH * c3)
    pw = patch_weight.reshape(PATCH, PATCH * c3, -1)
    hidden = patch_bias
    for i in range(PATCH):
        hidden = hidden + mm(stem[i], pw[i])
    na, ra = ln_stats(hidden)
    normed = (na * attn_gain + attn_bias).astype(bf16)
    qkv = mm(normed, qkv_weight).astype(bf16)
    attended, logs = attend(qkv, keep)
    hidden2 = hidden + mm(attended, out_weight)
    nm, rm = ln_stats(hidden2)
    normed2 = (nm * mlp_gain + mlp_bias).astype(bf16)
    pre = mm(normed2, up_weight) + up_bias
    act, dact = gelu_both(pre)
    act = act.astype(bf16)
    block_out = ((hidden2 + mm(act, down_weight) + down_bias) * keep).astype(bf16)
    g_final = cot.astype(f32) * keep
    g_low = g_final.astype(bf16)
    grad_down_bias = jnp.sum(g_final, axis=0)
    g_low = flows.begin("down", mm_tn(act, g_low), g_low)
    g_pre = mm_nt(g_low, down_weight) * dact
    grad_up_bias = jnp.sum(g_pre, axis=0)
    g_pre = g_pre.astype(bf16)
    g_pre = flows.begin("up", mm_tn(normed2, g_pre), g_pre)
    g_pre = flows.pump(g_pre, "up")
    g_ln, grad_mlp_gain, grad_mlp_bias = ln_back(mm_nt(g_pre, up_weight), nm, rm, mlp_gain)
    g_h2 = g_final + g_ln
    g_h2_low = g_h2.astype(bf16)
    grad_out = mm_tn(attended, g_h2_low)
    g_att = mm_nt(g_h2_low, out_weight).astype(bf16)
    g_att = flows.pump(g_att, "att")
    g_qkv = jnp.concatenate(attend_back(qkv, keep, g_att, logs), axis=1)
    g_qkv = flows.pump(g_qkv, "qkv")
    grad_qkv = mm_tn(normed, g_qkv)
    g_qkv = flows.begin("qkv", jnp.concatenate([grad_qkv, grad_out], axis=1), g_qkv)
    g_qkv = flows.pump(g_qkv, "ln")
    g_ln, grad_attn_gain, grad_attn_bias = ln_back(mm_nt(g_qkv, qkv_weight), na, ra, attn_gain)
    g_h = g_h2 + g_ln
    grad_patch_bias = jnp.sum(g_h, axis=0)
    g_h = g_h.astype(bf16)
    grad_patch = jnp.concatenate([mm_tn(stem[i], g_h) for i in range(PATCH)], axis=0)
    g_h = flows.begin("patch", grad_patch, g_h)
    g_h = flows.pump(g_h, "patch")
    g_stem = jnp.concatenate([mm_nt(g_h, pw[i]) for i in range(PATCH)], axis=0)
    g_stem = flows.pump(g_stem, "stem")
    g_z = g_stem * d3 * keep4
    g_z_low = g_z.astype(bf16)
    grad_skip = fold4(mm_tn(x, g_z_low), c0, c3)
    g_z = flows.pump(g_z, "z")
    g_v3, gain3, bias3 = gn_back(g_z, n3, r3, keep4, n3count, g256, gains[2])
    g_v3 = flows.pump(g_v3.astype(bf16), "v3")
    grad_cout = fold4(mm_tn(p2, g_v3), c0, c3)
    g_2 = mm_nt(g_v3, w_out) * d2 * keep4
    g_v2, gain2, bias2 = gn_back(g_2, n2, r2, keep4, n1count, g64, gains[1])
    g_v2 = flows.pump(g_v2.astype(bf16), "v2")
    grad_mid = fold_band(
        [mm_tn(wide[di : di + PATCH].reshape(rows, 6 * c0), g_v2) for di in range(3)], c0, c0
    )
    g_wide = widen(g_v2.reshape(PATCH, TOK, PATCH * c0))
    g_1 = conv3(g_wide, b_bwd) * d1 * keep4
    g_v1, gain1, bias1 = gn_back(g_1, n1, r1, keep4, n1count, g64, gains[0])
    g_v1 = flows.pump(g_v1.astype(bf16), "v1")
    grad_in = fold4(mm_tn(x, g_v1), c0, c0)
    input_grad = (mm_nt(g_v1, w_in) + mm_nt(g_z_low, w_skip)) * keep4

    def lanes(v):
        return jnp.sum(v.reshape(PATCH, -1), axis=0)

    grads = (
        grad_in,
        grad_mid,
        grad_cout,
        grad_skip,
        jnp.concatenate([lanes(gain1), lanes(gain2), lanes(gain3)]),
        jnp.concatenate([lanes(bias1), lanes(bias2), lanes(bias3)]),
        None,
        grad_patch_bias,
        grad_attn_gain,
        grad_attn_bias,
        None,
        None,
        grad_mlp_gain,
        grad_mlp_bias,
        None,
        grad_up_bias,
        None,
        grad_down_bias,
    )
    return block_out, input_grad.reshape(PATCH, TOK, PATCH * c0), grads


def swap(v, axis, step):
    count = lax.axis_size(axis)
    return lax.ppermute(v, axis, [(i, i ^ step) for i in range(count)])


def plus(a, b):
    return (a.astype(f32) + b.astype(f32)).astype(a.dtype)


def steps_of(axis):
    count = lax.axis_size(axis)
    return [1 << b for b in range(count.bit_length() - 1)]


def tie(x, *others):
    return lax.optimization_barrier((x,) + others)


def flow(whole, order):
    ranks = lax.axis_size("row")
    rank = lax.axis_index("row")
    me = lax.axis_index("img")
    rows = whole.shape[0] // ranks
    cut = whole.reshape(ranks, rows, *whole.shape[1:])
    rels = [int(bin(ranks + r)[:2:-1], 2) for r in range(ranks)]
    v = jnp.stack([lax.dynamic_index_in_dim(cut, rank ^ r, 0, keepdims=False) for r in rels])
    undo = []
    for axis, step in order:
        if axis == "row":
            n = v.shape[0] // 2
            keep, send = v[:n], v[n:]
        else:
            n = v.shape[1] // 2
            odd = (me & step) > 0
            low, high = v[:, :n], v[:, n:]
            send = jnp.where(odd, low, high)
            keep = jnp.where(odd, high, low)
            undo.append(step)
        got = yield send, axis, step
        v = plus(keep, got)
    for step in reversed(undo):
        odd = (me & step) > 0
        got = yield v, "img", step
        v = jnp.concatenate([jnp.where(odd, got, v), jnp.where(odd, v, got)], axis=1)
    yield v[0].astype(f32), None, None


XY = (("row", 1), ("row", 2), ("img", 1), ("img", 2), ("img", 4))


class Flows:
    def __init__(self, plan):
        self.plan = plan
        self.live = {}
        self.out = {}

    def send(self, name, item, x):
        what, axis, step = item
        if axis is None:
            self.out[name] = what
            return x
        x, what = tie(x, what)
        self.live[name][1] = swap(what, axis, step)
        return x

    def begin(self, name, whole, x):
        order = [(a, s) for a in ("row", "img") for s in steps_of(a)]
        gen = flow(whole.astype(bf16), order)
        self.live[name] = [gen, None]
        return self.send(name, next(gen), x)

    def advance(self, name, x):
        gen, got = self.live[name]
        x, got = tie(x, got)
        return self.send(name, gen.send(got), x)

    def pump(self, x, point):
        for name in self.plan.get(point, ()):
            x = self.advance(name, x)
        return x

    def finish(self):
        busy = True
        while busy:
            busy = False
            for name in list(self.live):
                if name not in self.out:
                    gen, got = self.live[name]
                    what, axis, step = gen.send(got)
                    if axis is None:
                        self.out[name] = what
                    else:
                        self.live[name][1] = swap(what, axis, step)
                        busy = True
        return self.out


PLAN = {
    "up": ("down",),
    "att": ("up",),
    "qkv": ("down",),
    "ln": ("up",),
    "patch": ("qkv",),
    "stem": ("down", "patch"),
    "z": ("down", "up"),
    "v3": ("down", "up", "qkv"),
    "v2": ("down", "up", "qkv"),
    "v1": ("down", "up", "qkv"),
}


def img_sum_small(v):
    for step in steps_of("img"):
        v = v + swap(v, "img", step)
    return v


def row_scatter(pieces):
    pieces = list(pieces)
    for step in steps_of("row"):
        for r in range(0, len(pieces), step):
            if r & step:
                pieces[r ^ step] = pieces[r ^ step] + swap(pieces[r], "row", step)
    return pieces[0]


def small_sums(grads, ranks):
    rank = lax.axis_index("row")
    some = [g for g in grads if g is not None]
    flat = jnp.concatenate([g.reshape(ranks, -1) for g in some], axis=1)
    flat = jnp.pad(flat, ((0, 0), (0, -flat.shape[1] % 1024))).reshape(ranks, -1, 128)
    pieces = [lax.dynamic_index_in_dim(flat, rank ^ r, 0, keepdims=False) for r in range(ranks)]
    flat = img_sum_small(row_scatter(pieces)).reshape(-1)
    at = 0
    sums = []
    for g in grads:
        if g is None:
            sums.append(None)
            continue
        n = g.size // ranks
        sums.append(flat[at : at + n].reshape((g.shape[0] // ranks,) + g.shape[1:]))
        at += n
    return sums


def per_device(stem_input, group, *rest):
    params, cot = rest[:-1], rest[-1]
    images, row_count, col_count, c0 = stem_input.shape
    ranks = lax.axis_size("row")
    assert images == ranks
    side = jnp.where(group[lax.axis_index("row")] == 1, FULL, SMALL).astype(jnp.int32)
    strips = row_count // PATCH
    x = stem_input.reshape(images, strips, PATCH, SIDE, PATCH * c0).transpose(0, 2, 1, 3, 4)
    x = lax.all_to_all(x, "row", 0, 0, tiled=True)
    x = x.transpose(1, 0, 2, 3, 4).reshape(PATCH, TOK, PATCH * c0)
    cot_in = lax.all_to_all(cot, "row", 0, 0, tiled=True).reshape(TOK, -1)
    flows = Flows(PLAN)
    block_out, input_grad, grads = per_image(x, side, cot_in, params, flows)
    block_out = block_out.reshape(images, -1, block_out.shape[-1])
    block_out = lax.all_to_all(block_out, "row", 0, 0, tiled=True)
    ig = input_grad.astype(bf16).reshape(PATCH, ranks, strips, SIDE, PATCH * c0).transpose(1, 0, 2, 3, 4)
    ig = lax.all_to_all(ig, "row", 0, 0, tiled=True)
    ig = ig.transpose(0, 2, 1, 3, 4).reshape(images, row_count, col_count, c0).astype(f32)
    shares = small_sums(grads, ranks)
    big = flows.finish()
    width = big["qkv"].shape[1] * 3 // 4
    shares[6] = big["patch"]
    shares[10], shares[11] = big["qkv"][:, :width], big["qkv"][:, width:]
    shares[14], shares[16] = big["up"], big["down"]
    return (block_out, ig) + tuple(shares)


def solution(mesh):
    rep = P()
    in_specs = (P("img", "row", None, None), P("img")) + (rep,) * 18 + (P("img", "row", None),)
    dims = (2, 3, 2, 2, 1, 1, 2, 1, 1, 1, 2, 2, 1, 1, 2, 1, 2, 1)
    out_specs = (P("img", "row", None), P("img", "row", None, None)) + tuple(
        P("row", *([None] * (n - 1))) for n in dims
    )
    return jax.shard_map(
        per_device, mesh=mesh, in_specs=in_specs, out_specs=out_specs, check_vma=False
    )
```

```python
import jax
import jax.numpy as jnp
from jax import lax
from jax.experimental import pallas as pl
from jax.experimental.pallas import tpu as pltpu
from jax.sharding import PartitionSpec as P

GROUPS = 32
HEADS = 12
HEAD_DIM = 64
PATCH = 4
FULL = 96
SMALL = 56
SIDE = FULL // PATCH
TOK = SIDE * SIDE
f32 = jnp.float32
bf16 = jnp.bfloat16


def mm(a, b):
    return lax.dot_general(a, b, (((1,), (0,)), ((), ())), preferred_element_type=f32)


def mm_nt(a, b):
    return lax.dot_general(a, b, (((1,), (1,)), ((), ())), preferred_element_type=f32)


def mm_tn(a, b):
    return lax.dot_general(a, b, (((0,), (0,)), ((), ())), preferred_element_type=f32)


def gelu_both(z):
    cdf = 0.5 + 0.5 * lax.erf(z * 0.7071067811865476)
    bell = jnp.exp(-0.5 * z * z)
    return z * cdf, cdf + z * bell * 0.3989422804014327


SRCS = (0, 1, 2, 3, -1, 4)
VMEM = pl.BlockSpec(memory_space=pltpu.VMEM)
SMEM = pl.BlockSpec(memory_space=pltpu.SMEM)


BIG = pltpu.CompilerParams(vmem_limit_bytes=56 * 1024 * 1024)


def whole(shape):
    return pl.BlockSpec(shape, lambda i: (0,) * len(shape))


def slab(shape):
    return pl.BlockSpec((1,) + tuple(shape[1:]), lambda i: (i,) + (0,) * (len(shape) - 1))


def exact(row, mat):
    return jnp.dot(row, mat, precision=lax.Precision.HIGHEST, preferred_element_type=f32)


def fold(row):
    n = row.shape[1] // PATCH
    return sum(row[:, j * n : (j + 1) * n] for j in range(PATCH))


def tile4(row):
    return jnp.concatenate([row] * PATCH, axis=1)


def tiled(keep, lanes):
    return jnp.concatenate([keep] * (lanes // keep.shape[1]), axis=1)


def back_coefs(sums, gain, inv, gmat, wide):
    if wide:
        pair = jnp.concatenate([fold(r * gain) for r in sums] + [jnp.zeros((6, 256), f32)], axis=0)
        pair = exact(pair, gmat)
        return tile4(pair[0:1]) * inv, tile4(pair[1:2]) * inv
    pair = jnp.concatenate([r * gain for r in sums] + [jnp.zeros((6, 256), f32)], axis=0)
    pair = exact(pair, gmat)
    return pair[0:1] * inv, pair[1:2] * inv


def add_to(ref, value, first):
    @pl.when(first)
    def _():
        ref[...] = value

    @pl.when(jnp.logical_not(first))
    def _():
        ref[...] += value


def colsum(v):
    return jnp.sum(v, axis=0, keepdims=True)


def stem_back1_kernel(
    gh_ref, pw_ref, d3_ref, p2_ref, x_ref, w_ref, st_ref, vec_ref, g256_ref,
    gz_ref, out_ref, skip_ref, acc_ref, sum_ref,
):
    i = pl.program_id(0)
    gz = mm_nt(gh_ref[...], pw_ref[0]) * d3_ref[0].astype(f32)
    n = mm(p2_ref[0], w_ref[...]) * st_ref[0:1] + st_ref[1:2]
    low = gz.astype(bf16)
    gz_ref[0] = low
    add_to(sum_ref, jnp.concatenate([colsum(gz), colsum(gz * n)] + [jnp.zeros((6, gz.shape[1]), f32)], axis=0), i == 0)
    add_to(acc_ref, mm_tn(x_ref[0], low), i == 0)

    @pl.when(i == PATCH - 1)
    def _():
        c1, c2 = sum_ref[0:1], sum_ref[1:2]
        s1, s2 = back_coefs((c1, c2), vec_ref[4:5], vec_ref[7:8], g256_ref[...], True)
        zero = jnp.zeros_like(c1)
        bias, gain = tile4(fold(c1)), tile4(fold(c2))
        out_ref[...] = jnp.concatenate([s1, s2, bias, gain] + [zero] * 4, axis=0)
        c, n = skip_ref.shape
        skip_ref[...] = sum(
            acc_ref[j * c : (j + 1) * c, j * n : (j + 1) * n] for j in range(PATCH)
        )


def stem_back1(g_h, pw, d3, p2, x, w_out, stat, vec, g256):
    lanes = d3.shape[2]
    c = p2.shape[2] // PATCH
    s = jax.ShapeDtypeStruct
    return pl.pallas_call(
        stem_back1_kernel,
        grid=(PATCH,),
        in_specs=[
            whole(g_h.shape), slab(pw.shape), slab(d3.shape), slab(p2.shape), slab(x.shape),
            whole(w_out.shape), whole(stat.shape), whole(vec.shape), whole(g256.shape),
        ],
        out_specs=[slab(d3.shape), whole((8, lanes)), whole((c, lanes // PATCH))],
        out_shape=[s(d3.shape, bf16), s((8, lanes), f32), s((c, lanes // PATCH), f32)],
        scratch_shapes=[pltpu.VMEM((PATCH * c, lanes), f32), pltpu.VMEM((8, lanes), f32)],
        compiler_params=BIG,
        name="stem_back1",
    )(g_h, pw, d3, p2, x, w_out, stat, vec, g256)


def stem_back2_kernel(
    gz_ref, p2_ref, d2_ref, n2_ref, w_ref, st_ref, co_ref, vec_ref, g64_ref, keep_ref,
    g2_ref, out_ref, grad_ref, acc_ref, sum_ref,
):
    i = pl.program_id(0)
    lanes = gz_ref.shape[2]
    keep = tiled(keep_ref[...], lanes)
    rstd, gain, s1, s2 = st_ref[0:1], vec_ref[4:5], co_ref[0:1], co_ref[1:2]
    n = mm(p2_ref[0], w_ref[...]) * rstd + st_ref[1:2]
    gv = (rstd * (gz_ref[0].astype(f32) * gain - s1 - n * s2) * keep).astype(bf16)
    add_to(acc_ref, mm_tn(p2_ref[0], gv), i == 0)
    g2 = mm_nt(gv, w_ref[...]) * d2_ref[0].astype(f32)
    g2_ref[0] = g2
    add_to(sum_ref, jnp.concatenate([colsum(g2), colsum(g2 * n2_ref[0].astype(f32))] + [jnp.zeros((6, g2.shape[1]), f32)], axis=0), i == 0)

    @pl.when(i == PATCH - 1)
    def _():
        narrow = g2_ref.shape[2]
        c1, c2 = sum_ref[0:1], sum_ref[1:2]
        s1, s2 = back_coefs((c1, c2), vec_ref[2:3, :narrow], vec_ref[6:7, :narrow], g64_ref[...], False)
        out_ref[...] = jnp.concatenate([s1, s2, c1, c2] + [jnp.zeros_like(c1)] * 4, axis=0)
        c, n = grad_ref.shape
        grad_ref[...] = sum(
            acc_ref[j * c : (j + 1) * c, j * n : (j + 1) * n] for j in range(PATCH)
        )


def stem_back2(gz, p2, d2, n2, w_out, stat, coef, vec, g64, keep):
    lanes = gz.shape[2]
    narrow = p2.shape[2]
    c = narrow // PATCH
    s = jax.ShapeDtypeStruct
    return pl.pallas_call(
        stem_back2_kernel,
        grid=(PATCH,),
        in_specs=[
            slab(gz.shape), slab(p2.shape), slab(d2.shape), slab(n2.shape), whole(w_out.shape),
            whole(stat.shape), whole(coef.shape), whole(vec.shape), whole(g64.shape), whole(keep.shape),
        ],
        out_specs=[slab(p2.shape), whole((8, narrow)), whole((c, lanes // PATCH))],
        out_shape=[s(p2.shape, f32), s((8, narrow), f32), s((c, lanes // PATCH), f32)],
        scratch_shapes=[pltpu.VMEM((narrow, lanes), f32), pltpu.VMEM((8, narrow), f32)],
        compiler_params=BIG,
        name="stem_back2",
    )(gz, p2, d2, n2, w_out, stat, coef, vec, g64, keep)


def edges(v, edge):
    c = v.shape[1] // PATCH
    toks = v.shape[0]
    left = pltpu.roll(v[:, 3 * c :], 1, 0)
    right = pltpu.roll(v[:, :c], toks - 1, 0)
    return jnp.concatenate([left, right], axis=1) * edge


def fill_wide(wide_ref, i, v, edge):
    lanes = v.shape[1]
    v = jnp.concatenate([v, edges(v, edge)], axis=1)
    wide_ref[i + 1] = v.astype(bf16)
    gap = jnp.zeros((SIDE, v.shape[1]), f32)
    if i == PATCH - 1:
        wide_ref[0] = jnp.concatenate([gap, v[:-SIDE]], axis=0).astype(bf16)
    if i == 0:
        wide_ref[PATCH + 1] = jnp.concatenate([v[SIDE:], gap], axis=0).astype(bf16)


def stem_back3_kernel(
    g2_ref, n2_ref, p1_ref, b_ref, d1_ref, x_ref, w_ref, st1_ref, st2_ref, co_ref, vec_ref, g64_ref,
    keep_ref, edge_ref, g1_ref, out_ref, grad_ref, wide_ref,
):
    narrow = g2_ref.shape[2]
    c = narrow // PATCH
    keep = tiled(keep_ref[...], narrow)
    rstd, gain, s1, s2 = st2_ref[0:1], vec_ref[2:3, :narrow], co_ref[0:1], co_ref[1:2]
    for i in range(PATCH):
        gv = rstd * (g2_ref[i] * gain - s1 - n2_ref[i].astype(f32) * s2) * keep
        fill_wide(wide_ref, i, gv, edge_ref[...])
    for di in range(3):
        total = 0.0
        for i in range(PATCH):
            total = total + mm_tn(p1_ref[i + di], wide_ref[i + 1, :, :narrow])
        for dj in range(3):
            grad_ref[3 * di + dj] = sum(
                total[k * c : (k + 1) * c, j * c : (j + 1) * c]
                for j in range(PATCH)
                for k in (SRCS.index(j + dj - 1),)
            )
    c1 = c2 = 0.0
    for i in range(PATCH):
        g1 = sum(mm_nt(wide_ref[i + di], b_ref[di]) for di in range(3)) * d1_ref[i].astype(f32)
        g1_ref[i] = g1
        n = mm(x_ref[i], w_ref[...]) * st1_ref[0:1] + st1_ref[1:2]
        c1 = c1 + colsum(g1)
        c2 = c2 + colsum(g1 * n)
    s1, s2 = back_coefs((c1, c2), vec_ref[0:1, :narrow], vec_ref[6:7, :narrow], g64_ref[...], False)
    out_ref[...] = jnp.concatenate([s1, s2, c1, c2] + [jnp.zeros_like(c1)] * 4, axis=0)


def stem_back3(g2, n2, p1_wide, b_bwd, d1, x, w_in, stat1, stat2, coef, vec, g64, keep, edge):
    narrow = g2.shape[2]
    c = narrow // PATCH
    s = jax.ShapeDtypeStruct
    vm = VMEM
    return pl.pallas_call(
        stem_back3_kernel,
        in_specs=[vm] * 14,
        out_specs=[vm] * 3,
        out_shape=[s(g2.shape, f32), s((8, narrow), f32), s((9, c, c), f32)],
        scratch_shapes=[pltpu.VMEM((PATCH + 2, TOK, 6 * c), bf16)],
        compiler_params=BIG,
        name="stem_back3",
    )(g2, n2, p1_wide, b_bwd, d1, x, w_in, stat1, stat2, coef, vec, g64, keep, edge)


def stem_back4_kernel(
    g1_ref, x_ref, gz_ref, win_ref, wskip_ref, st_ref, co_ref, vec_ref, keep_ref,
    ig_ref, grad_ref, acc_ref,
):
    i = pl.program_id(0)
    narrow = g1_ref.shape[2]
    keep = tiled(keep_ref[...], narrow)
    rstd, gain, s1, s2 = st_ref[0:1], vec_ref[0:1, :narrow], co_ref[0:1], co_ref[1:2]
    n = mm(x_ref[0], win_ref[...]) * rstd + st_ref[1:2]
    gv = (rstd * (g1_ref[0] * gain - s1 - n * s2) * keep).astype(bf16)
    add_to(acc_ref, mm_tn(x_ref[0], gv), i == 0)
    ig = (mm_nt(gv, win_ref[...]) + mm_nt(gz_ref[0], wskip_ref[...])) * keep
    part = ig_ref.shape[2]
    for k in range(ig_ref.shape[0]):
        ig_ref[k, 0] = ig[k * part : (k + 1) * part].astype(bf16)

    @pl.when(i == PATCH - 1)
    def _():
        c = grad_ref.shape[0]
        grad_ref[...] = sum(
            acc_ref[j * c : (j + 1) * c, j * c : (j + 1) * c] for j in range(PATCH)
        )


def stem_back4(g1, x, gz, w_in, w_skip, stat, coef, vec, keep, ranks):
    narrow = g1.shape[2]
    c = narrow // PATCH
    s = jax.ShapeDtypeStruct
    part = TOK // ranks
    return pl.pallas_call(
        stem_back4_kernel,
        grid=(PATCH,),
        in_specs=[
            slab(g1.shape), slab(x.shape), slab(gz.shape), whole(w_in.shape), whole(w_skip.shape),
            whole(stat.shape), whole(coef.shape), whole(vec.shape), whole(keep.shape),
        ],
        out_specs=[pl.BlockSpec((ranks, 1, part, narrow), lambda i: (0, i, 0, 0)), whole((c, c))],
        out_shape=[s((ranks, PATCH, part, narrow), bf16), s((c, c), f32)],
        scratch_shapes=[pltpu.VMEM((narrow, narrow), f32)],
        compiler_params=BIG,
        name="stem_back4",
    )(g1, x, gz, w_in, w_skip, stat, coef, vec, keep)


def scale_shift(c1, c2, gain, bias, inv, gmat, wide):
    pair = jnp.concatenate([c1, c2], axis=0)
    if wide:
        pair = fold(pair)
    pair = exact(jnp.concatenate([pair, jnp.zeros((6, pair.shape[1]), f32)], axis=0), gmat)
    if wide:
        pair = tile4(pair)
    mean, square = pair[0:1] * inv, pair[1:2] * inv
    rstd = lax.rsqrt(square - mean * mean + 1e-05)
    shift = -mean * rstd
    return rstd, shift, rstd * gain, bias + shift * gain


def stem_front_kernel(
    x_ref, win_ref, bf_ref, wout_ref, vec_ref, g64_ref, g256_ref, keep_ref, edge_ref,
    wide_ref, d1_ref, p2_ref, d2_ref, n2_ref, st1_ref, st2_ref, st3_ref, v_ref,
):
    narrow = x_ref.shape[2]
    keep = tiled(keep_ref[...], narrow)
    inv = vec_ref[6:7, :narrow]
    c1 = c2 = 0.0
    for i in range(PATCH):
        v = mm(x_ref[i], win_ref[...])
        v_ref[i] = v
        c1, c2 = c1 + colsum(v), c2 + colsum(v * v)
    rstd, shift, a, b = scale_shift(c1, c2, vec_ref[0:1, :narrow], vec_ref[1:2, :narrow], inv, g64_ref[...], False)
    st1_ref[...] = jnp.concatenate([rstd, shift], axis=0)
    for i in range(PATCH):
        act, slope = gelu_both(v_ref[i] * a + b)
        d1_ref[i] = (slope * keep).astype(bf16)
        fill_wide(wide_ref, i, act * keep, edge_ref[...])
    c1 = c2 = 0.0
    for i in range(PATCH):
        v = sum(mm(wide_ref[i + di], bf_ref[di]) for di in range(3))
        v_ref[i] = v
        v = v * keep
        c1, c2 = c1 + colsum(v), c2 + colsum(v * v)
    rstd, shift, a, b = scale_shift(c1, c2, vec_ref[2:3, :narrow], vec_ref[3:4, :narrow], inv, g64_ref[...], False)
    st2_ref[...] = jnp.concatenate([rstd, shift], axis=0)
    c1 = c2 = 0.0
    for i in range(PATCH):
        v = v_ref[i]
        act, slope = gelu_both(v * a + b)
        d2_ref[i] = (slope * keep).astype(bf16)
        n2_ref[i] = (v * rstd + shift).astype(bf16)
        low = (act * keep).astype(bf16)
        p2_ref[i] = low
        v = mm(low, wout_ref[...])
        c1, c2 = c1 + colsum(v), c2 + colsum(v * v)
    st3_ref[...] = jnp.concatenate(
        scale_shift(c1, c2, vec_ref[4:5], vec_ref[5:6], vec_ref[7:8], g256_ref[...], True), axis=0
    )


def stem_front(x, w_in, b_fwd, w_out, vec, g64, g256, keep, edge):
    narrow = x.shape[2]
    s = jax.ShapeDtypeStruct
    vm = pl.BlockSpec(memory_space=pltpu.VMEM)
    low = s(x.shape, bf16)
    return pl.pallas_call(
        stem_front_kernel,
        in_specs=[vm] * 9,
        out_specs=[vm] * 8,
        out_shape=[
            s((PATCH + 2, TOK, narrow * 3 // 2), bf16), low, low, low, low,
            s((2, narrow), f32), s((2, narrow), f32), s((4, w_out.shape[1]), f32),
        ],
        scratch_shapes=[pltpu.VMEM(x.shape, f32)],
        compiler_params=BIG,
        name="stem_front",
    )(x, w_in, b_fwd, w_out, vec, g64, g256, keep, edge)


def stem_last_kernel(p2_ref, x_ref, wout_ref, wskip_ref, st_ref, keep_ref, stem_ref, d3_ref):
    keep = tiled(keep_ref[...], wout_ref.shape[1])
    z = mm(p2_ref[0], wout_ref[...]) * st_ref[2:3] + st_ref[3:4] + mm(x_ref[0], wskip_ref[...])
    act, slope = gelu_both(z)
    stem_ref[0] = (act * keep).astype(bf16)
    d3_ref[0] = (slope * keep).astype(bf16)


def stem_last(p2, x, w_out, w_skip, stat, keep):
    lanes = w_out.shape[1]
    shape = p2.shape[:2] + (lanes,)
    o = jax.ShapeDtypeStruct(shape, bf16)
    return pl.pallas_call(
        stem_last_kernel,
        grid=(PATCH,),
        in_specs=[slab(p2.shape), slab(x.shape), whole(w_out.shape), whole(w_skip.shape), whole(stat.shape), whole(keep.shape)],
        out_specs=[slab(shape)] * 2,
        out_shape=[o, o],
        compiler_params=BIG,
        name="stem_last",
    )(p2, x, w_out, w_skip, stat, keep)


def pack_kernel(x_ref, o_ref, wide_ref):
    rows, chans, cols = x_ref.shape[1:]
    for r in range(rows):
        wide_ref[r * cols : (r + 1) * cols, :] = x_ref[0, r].astype(f32).T
    for i in range(PATCH):
        parts = []
        for j in range(PATCH):
            parts.append(
                jnp.concatenate(
                    [
                        wide_ref[pl.ds(r * cols + j, SIDE, stride=PATCH), :]
                        for r in range(i, rows, PATCH)
                    ],
                    axis=0,
                )
            )
        o_ref[0, i] = jnp.concatenate(parts, axis=1).astype(o_ref.dtype)


def pack(x):
    images, rows, cols, chans = x.shape
    x = x.transpose(0, 1, 3, 2)
    shape = (images, PATCH, rows // PATCH * SIDE, PATCH * chans)
    return pl.pallas_call(
        pack_kernel,
        grid=(images,),
        in_specs=[pl.BlockSpec((1, rows, chans, cols), lambda b: (b, 0, 0, 0))],
        out_specs=pl.BlockSpec((1,) + shape[1:], lambda b: (b, 0, 0, 0)),
        out_shape=jax.ShapeDtypeStruct(shape, x.dtype),
        scratch_shapes=[pltpu.VMEM((rows * cols, chans), f32)],
        name="pack",
    )(x)


def unpack_kernel(x_ref, o_ref, row_ref):
    chans = o_ref.shape[2]
    for i in range(PATCH):
        v = x_ref[0, i].astype(f32)
        for p in range(v.shape[0] // SIDE):
            for j in range(PATCH):
                row_ref[PATCH * p + i, pl.ds(j, SIDE, stride=PATCH), :] = v[
                    p * SIDE : (p + 1) * SIDE, j * chans : (j + 1) * chans
                ]
    for r in range(o_ref.shape[1]):
        o_ref[0, r] = row_ref[r].T


def unpack(v):
    images, _, toks, lanes = v.shape
    shape = (images, toks // SIDE * PATCH, lanes // PATCH, SIDE * PATCH)
    return pl.pallas_call(
        unpack_kernel,
        grid=(images,),
        in_specs=[pl.BlockSpec((1,) + v.shape[1:], lambda b: (b, 0, 0, 0))],
        out_specs=pl.BlockSpec((1,) + shape[1:], lambda b: (b, 0, 0, 0)),
        out_shape=jax.ShapeDtypeStruct(shape, f32),
        scratch_shapes=[pltpu.VMEM((shape[1], shape[3], shape[2]), f32)],
        name="unpack",
    )(v).transpose(0, 1, 3, 2)


def prep_kernel(
    rank_ref, group_ref, in_ref, mid_ref, out_ref, skip_ref, gain_ref, bias_ref,
    w_in, w_out, w_skip, b_fwd, b_bwd, g64, g256, vec, keep, edge,
):
    def spread(dst, src):
        dst[...] = jnp.zeros_like(dst)
        c, n = src.shape
        for j in range(PATCH):
            dst[j * c : (j + 1) * c, j * n : (j + 1) * n] = src[...]

    spread(w_in, in_ref)
    spread(w_out, out_ref)
    spread(w_skip, skip_ref)
    b_fwd[...] = jnp.zeros_like(b_fwd)
    b_bwd[...] = jnp.zeros_like(b_bwd)
    c = mid_ref.shape[1]
    for di in range(3):
        for k, src in enumerate(SRCS):
            for j in range(PATCH):
                if abs(src - j) <= 1:
                    dj = src - j + 1
                    b_fwd[di, k * c : (k + 1) * c, j * c : (j + 1) * c] = mid_ref[3 * di + dj]
                    b_bwd[di, j * c : (j + 1) * c, k * c : (k + 1) * c] = mid_ref[8 - 3 * di - dj]
    for ref, chans in ((g64, c), (g256, gain_ref.shape[1] - 2 * c)):
        per = chans // GROUPS
        row = (lax.broadcasted_iota(jnp.int32, ref.shape, 0) & (chans - 1)) // per
        col = (lax.broadcasted_iota(jnp.int32, ref.shape, 1) & (chans - 1)) // per
        ref[...] = jnp.where(row == col, 1.0, 0.0)
    vec[...] = jnp.zeros_like(vec)
    for at, (ref, lo, hi) in enumerate(
        (r, lo, hi)
        for lo, hi in ((0, c), (c, 2 * c), (2 * c, gain_ref.shape[1]))
        for r in (gain_ref, bias_ref)
    ):
        part = jnp.concatenate([ref[:, lo:hi]] * PATCH, axis=1)
        vec[at : at + 1, : part.shape[1]] = part
    limit = jnp.where(group_ref[rank_ref[0]] == 1, FULL // PATCH, SMALL // PATCH)
    inverse = 1.0 / (jnp.full((1, vec.shape[1]), PATCH * PATCH, f32) * (limit * limit).astype(f32))
    vec[6:7] = inverse * (GROUPS / c)
    vec[7:8] = inverse * (GROUPS / (gain_ref.shape[1] - 2 * c))
    t = lax.broadcasted_iota(jnp.int32, keep.shape, 0)
    up = ((t.astype(f32) + 0.5) * (1.0 / SIDE)).astype(jnp.int32)
    t = t - SIDE * up
    keep[...] = jnp.where((up < limit) & (t < limit), 1.0, 0.0)
    left = lax.broadcasted_iota(jnp.int32, edge.shape, 1) < c
    edge[...] = jnp.where(t != jnp.where(left, 0, SIDE - 1), 1.0, 0.0)


def prep(rank, group, conv_in, conv_mid, conv_out, conv_skip, norm_gain, norm_bias):
    c, n = conv_out.shape
    s = jax.ShapeDtypeStruct
    shapes = [
        s((PATCH * c, PATCH * c), bf16),
        s((PATCH * c, PATCH * n), bf16),
        s((PATCH * c, PATCH * n), bf16),
        s((3, 6 * c, PATCH * c), bf16),
        s((3, PATCH * c, 6 * c), bf16),
        s((PATCH * c, PATCH * c), f32),
        s((PATCH * c, PATCH * c), f32),
        s((8, PATCH * n), f32),
        s((TOK, 128), f32),
        s((TOK, 2 * c), f32),
    ]
    return pl.pallas_call(
        prep_kernel,
        in_specs=[SMEM, SMEM] + [VMEM] * 6,
        out_specs=[VMEM] * len(shapes),
        out_shape=shapes,
        name="prep",
    )(
        rank.reshape(1),
        group,
        conv_in,
        conv_mid.transpose(1, 0, 2),
        conv_out,
        conv_skip,
        norm_gain[None],
        norm_bias[None],
    )


def ln_stats(h):
    mean = jnp.mean(h, axis=-1, keepdims=True)
    cen = h - mean
    rstd = lax.rsqrt(jnp.mean(cen * cen, axis=-1, keepdims=True) + 1e-05)
    return cen * rstd, rstd


def ln_back(gy, n, rstd, gain):
    gn = gy * gain
    gh = rstd * (
        gn - jnp.mean(gn, axis=-1, keepdims=True) - n * jnp.mean(gn * n, axis=-1, keepdims=True)
    )
    return gh, jnp.sum(gy * n, axis=0), jnp.sum(gy, axis=0)


def attend_kernel(keep_ref, q_ref, k_ref, v_ref, o_ref, l_ref):
    scale = HEAD_DIM**-0.5
    valid = keep_ref[...] > 0
    outs = []
    for h in range(2):
        lanes = slice(h * HEAD_DIM, (h + 1) * HEAD_DIM)
        q, k, v = q_ref[:, lanes], k_ref[:, lanes], v_ref[:, lanes]
        s = jnp.where(valid, mm_nt(k, q) * scale, -1000000000.0)
        top = jnp.max(s, axis=0, keepdims=True)
        e = jnp.exp(s - top)
        total = jnp.sum(e, axis=0, keepdims=True)
        outs.append(mm_tn(v, e.astype(bf16)) / total)
        l_ref[0, h : h + 1, :] = top + jnp.log(total)
    o_ref[...] = jnp.concatenate(outs, axis=0).T.astype(bf16)

def attend(qkv, keep):
    tok, width3 = qkv.shape
    pairs = HEADS // 2
    two = 2 * HEAD_DIM
    def spec(kind):
        return pl.BlockSpec((tok, two), lambda h: (0, kind * pairs + h))
    return pl.pallas_call(
        attend_kernel, grid=(pairs,),
        in_specs=[pl.BlockSpec((tok, 1), lambda h: (0, 0)), spec(0), spec(1), spec(2)],
        out_specs=[spec(0), pl.BlockSpec((1, 2, tok), lambda h: (h, 0, 0))],
        out_shape=[jax.ShapeDtypeStruct((tok, width3 // 3), bf16), jax.ShapeDtypeStruct((pairs, 2, tok), f32)],
        compiler_params=pltpu.CompilerParams(vmem_limit_bytes=40*1024*1024),
        name="attend",
    )(keep, qkv, qkv, qkv)

def attend_back_kernel(keep_ref, q_ref, k_ref, v_ref, g_ref, l_ref, gq_ref, gk_ref, gv_ref):
    scale = HEAD_DIM**-0.5
    valid = keep_ref[...] > 0
    gqs, gks, gvs = [], [], []
    for h in range(2):
        lanes = slice(h * HEAD_DIM, (h + 1) * HEAD_DIM)
        q, k, v, g = q_ref[:, lanes], k_ref[:, lanes], v_ref[:, lanes], g_ref[:, lanes]
        s = jnp.where(valid, mm_nt(k, q) * scale, -1000000000.0)
        p = jnp.exp(s - l_ref[0, h : h + 1, :])
        gp = mm_nt(v, g)
        dot = jnp.sum(gp * p, axis=0, keepdims=True)
        gs = (p * (gp - dot)).astype(bf16)
        gvs.append(mm(p.astype(bf16), g))
        gks.append(mm(gs, q) * scale)
        gqs.append(mm_tn(k, gs) * scale)
    gq_ref[...] = jnp.concatenate(gqs, axis=0).T.astype(bf16)
    gk_ref[...] = jnp.concatenate(gks, axis=1).astype(bf16)
    gv_ref[...] = jnp.concatenate(gvs, axis=1).astype(bf16)

def attend_back(qkv, keep, g, logs):
    tok, width3 = qkv.shape
    pairs = HEADS // 2
    two = 2 * HEAD_DIM
    def spec(kind):
        return pl.BlockSpec((tok, two), lambda h: (0, kind * pairs + h))
    o = jax.ShapeDtypeStruct((tok, width3 // 3), bf16)
    return pl.pallas_call(
        attend_back_kernel, grid=(pairs,),
        in_specs=[pl.BlockSpec((tok, 1), lambda h: (0, 0)), spec(0), spec(1), spec(2), spec(0), pl.BlockSpec((1, 2, tok), lambda h: (h, 0, 0))],
        out_specs=[spec(0)] * 3,
        out_shape=[o, o, o],
        compiler_params=pltpu.CompilerParams(vmem_limit_bytes=40*1024*1024),
        name="attend_back",
    )(keep, qkv, qkv, qkv, g, logs)


def per_image(x, cot, made, params, flows):
    (
        conv_in,
        conv_mid,
        conv_out,
        conv_skip,
        norm_gain,
        norm_bias,
        patch_weight,
        patch_bias,
        attn_gain,
        attn_bias,
        qkv_weight,
        out_weight,
        mlp_gain,
        mlp_bias,
        up_weight,
        up_bias,
        down_weight,
        down_bias,
    ) = params
    w_in, w_out, w_skip, b_fwd, b_bwd, g64, g256, vec, keep_wide, edge = made
    c0 = conv_in.shape[0]
    c3 = conv_out.shape[1]
    ranks = lax.axis_size("row")
    keep = keep_wide[:, :1]
    x = x * keep.astype(bf16)
    wide, d1, p2, d2, n2, st1, st2, st3 = stem_front(
        x, w_in, b_fwd, w_out, vec, g64, g256, keep_wide, edge
    )
    stem, d3 = stem_last(p2, x, w_out, w_skip, st3, keep_wide)
    pw = patch_weight.reshape(PATCH, PATCH * c3, -1)
    hidden = patch_bias
    for i in range(PATCH):
        hidden = hidden + mm(stem[i], pw[i])
    na, ra = ln_stats(hidden)
    normed = (na * attn_gain + attn_bias).astype(bf16)
    qkv = mm(normed, qkv_weight).astype(bf16)
    attended, logs = attend(qkv, keep)
    hidden2 = hidden + mm(attended, out_weight)
    nm, rm = ln_stats(hidden2)
    normed2 = (nm * mlp_gain + mlp_bias).astype(bf16)
    pre = mm(normed2, up_weight) + up_bias
    act, dact = gelu_both(pre)
    act = act.astype(bf16)
    block_out = ((hidden2 + mm(act, down_weight) + down_bias) * keep).astype(bf16)
    g_final = cot.astype(f32) * keep
    g_low = g_final.astype(bf16)
    grad_down_bias = jnp.sum(g_final, axis=0)
    g_low = flows.begin("down", mm_tn(act, g_low), g_low)
    g_pre = mm_nt(g_low, down_weight) * dact
    grad_up_bias = jnp.sum(g_pre, axis=0)
    g_pre = g_pre.astype(bf16)
    g_pre = flows.begin("up", mm_tn(normed2, g_pre), g_pre)
    g_pre = flows.pump(g_pre, "up")
    g_ln, grad_mlp_gain, grad_mlp_bias = ln_back(mm_nt(g_pre, up_weight), nm, rm, mlp_gain)
    g_h2 = g_final + g_ln
    g_h2_low = g_h2.astype(bf16)
    grad_out = mm_tn(attended, g_h2_low)
    g_att = mm_nt(g_h2_low, out_weight).astype(bf16)
    g_att = flows.pump(g_att, "att")
    g_qkv = jnp.concatenate(attend_back(qkv, keep, g_att, logs), axis=1)
    g_qkv = flows.pump(g_qkv, "qkv")
    grad_qkv = mm_tn(normed, g_qkv)
    g_qkv = flows.begin("qkv", jnp.concatenate([grad_qkv, grad_out], axis=1), g_qkv)
    g_qkv = flows.pump(g_qkv, "ln")
    g_ln, grad_attn_gain, grad_attn_bias = ln_back(mm_nt(g_qkv, qkv_weight), na, ra, attn_gain)
    g_h = g_h2 + g_ln
    grad_patch_bias = jnp.sum(g_h, axis=0)
    g_h = g_h.astype(bf16)
    grad_patch = jnp.concatenate([mm_tn(stem[i], g_h) for i in range(PATCH)], axis=0)
    g_h = flows.begin("patch", grad_patch, g_h)
    g_h = flows.pump(g_h, "patch")
    g_z, co3, grad_skip = stem_back1(g_h, pw, d3, p2, x, w_out, st3, vec, g256)
    g_z = flows.pump(g_z, "z")
    g_2, co2, grad_cout = stem_back2(g_z, p2, d2, n2, w_out, st3, co3, vec, g64, keep_wide)
    g_2 = flows.pump(g_2, "v3")
    g_1, co1, grad_mid = stem_back3(
        g_2, n2, wide, b_bwd, d1, x, w_in, st1, st2, co2, vec, g64, keep_wide, edge
    )
    g_1 = flows.pump(g_1, "v2")
    input_grad, grad_in = stem_back4(g_1, x, g_z, w_in, w_skip, st1, co1, vec, keep_wide, ranks)
    input_grad = flows.pump(input_grad, "v1")

    def lanes(v):
        return jnp.sum(v.reshape(PATCH, -1), axis=0)

    grads = (
        grad_in,
        grad_mid.transpose(1, 0, 2),
        grad_cout,
        grad_skip,
        jnp.concatenate([lanes(co1[3]), lanes(co2[3]), co3[3, :c3]]),
        jnp.concatenate([lanes(co1[2]), lanes(co2[2]), co3[2, :c3]]),
        None,
        grad_patch_bias,
        grad_attn_gain,
        grad_attn_bias,
        None,
        None,
        grad_mlp_gain,
        grad_mlp_bias,
        None,
        grad_up_bias,
        None,
        grad_down_bias,
    )
    return block_out, input_grad, grads


def swap(v, axis, step):
    count = lax.axis_size(axis)
    return lax.ppermute(v, axis, [(i, i ^ step) for i in range(count)])


def plus(a, b):
    return (a.astype(f32) + b.astype(f32)).astype(a.dtype)


def steps_of(axis):
    count = lax.axis_size(axis)
    return [1 << b for b in range(count.bit_length() - 1)]


def tie(x, *others):
    return lax.optimization_barrier((x,) + others)


def flow(whole, order):
    ranks = lax.axis_size("row")
    rank = lax.axis_index("row")
    me = lax.axis_index("img")
    rows = whole.shape[0] // ranks
    cut = whole.reshape(ranks, rows, *whole.shape[1:])
    rels = [int(bin(ranks + r)[:2:-1], 2) for r in range(ranks)]
    v = jnp.stack([lax.dynamic_index_in_dim(cut, rank ^ r, 0, keepdims=False) for r in rels])
    undo = []
    for axis, step in order:
        if axis == "row":
            n = v.shape[0] // 2
            keep, send = v[:n], v[n:]
        else:
            n = v.shape[1] // 2
            odd = (me & step) > 0
            low, high = v[:, :n], v[:, n:]
            send = jnp.where(odd, low, high)
            keep = jnp.where(odd, high, low)
            undo.append(step)
        got = yield send, axis, step
        v = plus(keep, got)
    for step in reversed(undo):
        odd = (me & step) > 0
        got = yield v, "img", step
        v = jnp.concatenate([jnp.where(odd, got, v), jnp.where(odd, v, got)], axis=1)
    yield v[0].astype(f32), None, None


XY = (("row", 1), ("row", 2), ("img", 1), ("img", 2), ("img", 4))


class Flows:
    def __init__(self, plan):
        self.plan = plan
        self.live = {}
        self.out = {}

    def send(self, name, item, x):
        what, axis, step = item
        if axis is None:
            self.out[name] = what
            return x
        x, what = tie(x, what)
        self.live[name][1] = swap(what, axis, step)
        return x

    def begin(self, name, whole, x):
        order = [(a, s) for a in ("row", "img") for s in steps_of(a)]
        gen = flow(whole.astype(bf16), order)
        self.live[name] = [gen, None]
        return self.send(name, next(gen), x)

    def advance(self, name, x):
        gen, got = self.live[name]
        x, got = tie(x, got)
        return self.send(name, gen.send(got), x)

    def pump(self, x, point):
        for name in self.plan.get(point, ()):
            x = self.advance(name, x)
        return x

    def finish(self):
        busy = True
        while busy:
            busy = False
            for name in list(self.live):
                if name not in self.out:
                    gen, got = self.live[name]
                    what, axis, step = gen.send(got)
                    if axis is None:
                        self.out[name] = what
                    else:
                        self.live[name][1] = swap(what, axis, step)
                        busy = True
        return self.out


PLAN = {
    "up": ("down",),
    "att": ("up",),
    "qkv": ("down",),
    "ln": ("up",),
    "patch": ("qkv",),
    "stem": ("down", "patch"),
    "z": ("down", "up"),
    "v3": ("down", "up", "qkv"),
    "v2": ("down", "up", "qkv"),
    "v1": ("down", "up", "qkv"),
}


def img_sum_small(v):
    for step in steps_of("img"):
        v = v + swap(v, "img", step)
    return v


def row_scatter(pieces):
    pieces = list(pieces)
    for step in steps_of("row"):
        for r in range(0, len(pieces), step):
            if r & step:
                pieces[r ^ step] = pieces[r ^ step] + swap(pieces[r], "row", step)
    return pieces[0]


def small_sums(grads, ranks):
    rank = lax.axis_index("row")
    some = [g for g in grads if g is not None]
    flat = jnp.concatenate([g.reshape(ranks, -1) for g in some], axis=1)
    flat = jnp.pad(flat, ((0, 0), (0, -flat.shape[1] % 1024))).reshape(ranks, -1, 128)
    pieces = [lax.dynamic_index_in_dim(flat, rank ^ r, 0, keepdims=False) for r in range(ranks)]
    flat = img_sum_small(row_scatter(pieces)).reshape(-1)
    at = 0
    sums = []
    for g in grads:
        if g is None:
            sums.append(None)
            continue
        n = g.size // ranks
        sums.append(flat[at : at + n].reshape((g.shape[0] // ranks,) + g.shape[1:]))
        at += n
    return sums


def per_device(stem_input, group, *rest):
    params, cot = rest[:-1], rest[-1]
    images, row_count, col_count, c0 = stem_input.shape
    ranks = lax.axis_size("row")
    assert images == ranks
    x = lax.all_to_all(pack(stem_input), "row", 0, 0, tiled=True)
    x = x.transpose(1, 0, 2, 3).reshape(PATCH, TOK, PATCH * c0)
    made = prep(
        lax.axis_index("row"), group, rest[0], rest[1], rest[2], rest[3], rest[4], rest[5]
    )
    x, cot = tie(x, cot)
    cot_in = lax.all_to_all(cot, "row", 0, 0, tiled=True).reshape(TOK, -1)
    flows = Flows(PLAN)
    block_out, input_grad, grads = per_image(x, cot_in, made, params, flows)
    block_out = block_out.reshape(images, -1, block_out.shape[-1])
    block_out = lax.all_to_all(block_out, "row", 0, 0, tiled=True)
    ig = unpack(lax.all_to_all(input_grad, "row", 0, 0, tiled=True))
    shares = small_sums(grads, ranks)
    big = flows.finish()
    width = big["qkv"].shape[1] * 3 // 4
    shares[6] = big["patch"]
    shares[10], shares[11] = big["qkv"][:, :width], big["qkv"][:, width:]
    shares[14], shares[16] = big["up"], big["down"]
    return (block_out, ig) + tuple(shares)


def solution(mesh):
    rep = P()
    in_specs = (P("img", "row", None, None), P("img")) + (rep,) * 18 + (P("img", "row", None),)
    dims = (2, 3, 2, 2, 1, 1, 2, 1, 1, 1, 2, 2, 1, 1, 2, 1, 2, 1)
    out_specs = (P("img", "row", None), P("img", "row", None, None)) + tuple(
        P("row", *([None] * (n - 1))) for n in dims
    )
    return jax.shard_map(
        per_device, mesh=mesh, in_specs=in_specs, out_specs=out_specs, check_vma=False
    )
```

```python
import jax
import jax.numpy as jnp
from jax import lax
from jax.experimental import pallas as pl
from jax.experimental.pallas import tpu as pltpu
from jax.sharding import PartitionSpec as P

GROUPS = 32
HEADS = 12
HEAD_DIM = 64
PATCH = 4
FULL = 96
SMALL = 56
SIDE = FULL // PATCH
TOK = SIDE * SIDE
f32 = jnp.float32
bf16 = jnp.bfloat16


def mm(a, b):
    return lax.dot_general(a, b, (((1,), (0,)), ((), ())), preferred_element_type=f32)


def mm_nt(a, b):
    return lax.dot_general(a, b, (((1,), (1,)), ((), ())), preferred_element_type=f32)


def mm_tn(a, b):
    return lax.dot_general(a, b, (((0,), (0,)), ((), ())), preferred_element_type=f32)


def gelu_both(z):
    cdf = 0.5 + 0.5 * lax.erf(z * 0.7071067811865476)
    bell = jnp.exp(-0.5 * z * z)
    return z * cdf, cdf + z * bell * 0.3989422804014327


SRCS = (0, 1, 2, 3, -1, 4)
VMEM = pl.BlockSpec(memory_space=pltpu.VMEM)
SMEM = pl.BlockSpec(memory_space=pltpu.SMEM)


ANY = pl.BlockSpec(memory_space=pl.ANY)
TIMES = {
    "attend": 10, "attend_back": 15, "stem_front": 11, "stem_last": 11, "stem_back1": 13, "stem_back2": 12,
    "stem_back3": 10, "stem_back4": 8, "wgrad_rows": 6, "wgrad_cols": 6, "wgrad_qkv": 6, "mlp_back1": 4,
    "mlp_back2": 7, "qkv_back": 5, "unpack": 4, "pack": 2, "prep": 4,
}


def cost(name):
    flops = int(TIMES.get(name, 1) * 0.3 * 1.1e9)
    return pl.CostEstimate(flops=flops, bytes_accessed=flops // 1000, transcendentals=0)


class Chain:
    def __init__(self):
        self.tokens = []


def launch(kernel, chain=None, in_specs=None, grid_spec=None, out_specs=None, out_shape=None, **options):
    deps = chain.tokens if chain else []
    extra = [ANY] * len(deps)
    single = not isinstance(out_shape, (list, tuple))
    if single:
        out_shape = [out_shape]
    if grid_spec:
        out_specs = grid_spec["out_specs"]
    if not isinstance(out_specs, (list, tuple)):
        out_specs = [out_specs]
    outs = len(out_shape)
    count = len(in_specs if in_specs else grid_spec["in_specs"])
    count += grid_spec["num_scalar_prefetch"] if grid_spec else 0
    out_shape, out_specs = list(out_shape), list(out_specs)
    if chain:
        out_shape = out_shape + [jax.ShapeDtypeStruct((8, 128), f32)]
        out_specs = out_specs + [pl.BlockSpec((8, 128), lambda *_: (0, 0))]
    if grid_spec:
        spec = dict(grid_spec, in_specs=grid_spec["in_specs"] + extra, out_specs=out_specs)
        options["grid_spec"] = pltpu.PrefetchScalarGridSpec(**spec)
    else:
        options["in_specs"], options["out_specs"] = in_specs + extra, out_specs

    def body(*refs):
        at = count + len(deps) + outs
        if chain:
            refs[at][...] = jnp.zeros((8, 128), f32)
        return kernel(*refs[:count], *refs[count + len(deps) : at], *refs[at + (1 if chain else 0) :])

    run = pl.pallas_call(body, out_shape=out_shape, cost_estimate=cost(options["name"]), **options)

    def call(*operands):
        out = run(*operands, *deps)
        if chain:
            chain.tokens = [out[-1]]
            out = out[:-1]
        return out[0] if single else out

    return call


MID = pltpu.CompilerParams(vmem_limit_bytes=24 * 1024 * 1024)
BIG = pltpu.CompilerParams(vmem_limit_bytes=56 * 1024 * 1024)


def whole(shape):
    return pl.BlockSpec(shape, lambda i: (0,) * len(shape))


def slab(shape):
    return pl.BlockSpec((1,) + tuple(shape[1:]), lambda i: (i,) + (0,) * (len(shape) - 1))


def exact(row, mat):
    return jnp.dot(row, mat, precision=lax.Precision.HIGHEST, preferred_element_type=f32)


def fold(row):
    n = row.shape[1] // PATCH
    return sum(row[:, j * n : (j + 1) * n] for j in range(PATCH))


def tile4(row):
    return jnp.concatenate([row] * PATCH, axis=1)


def tiled(keep, lanes):
    return jnp.concatenate([keep] * (lanes // keep.shape[1]), axis=1)


def back_coefs(sums, gain, inv, gmat, wide):
    if wide:
        pair = jnp.concatenate([fold(r * gain) for r in sums] + [jnp.zeros((6, 256), f32)], axis=0)
        pair = exact(pair, gmat)
        return tile4(pair[0:1]) * inv, tile4(pair[1:2]) * inv
    pair = jnp.concatenate([r * gain for r in sums] + [jnp.zeros((6, 256), f32)], axis=0)
    pair = exact(pair, gmat)
    return pair[0:1] * inv, pair[1:2] * inv


def add_to(ref, value, first):
    @pl.when(first)
    def _():
        ref[...] = value

    @pl.when(jnp.logical_not(first))
    def _():
        ref[...] += value


def colsum(v):
    return jnp.sum(v, axis=0, keepdims=True)


def stem_back1_kernel(
    gh_ref, pw_ref, d3_ref, p2_ref, x_ref, w_ref, st_ref, vec_ref, g256_ref,
    gz_ref, out_ref, skip_ref, acc_ref, sum_ref,
):
    i = pl.program_id(0)
    gz = mm_nt(gh_ref[...], pw_ref[0]) * d3_ref[0].astype(f32)
    n = mm(p2_ref[0], w_ref[...]) * st_ref[0:1] + st_ref[1:2]
    low = gz.astype(bf16)
    gz_ref[0] = low
    add_to(sum_ref, jnp.concatenate([colsum(gz), colsum(gz * n)] + [jnp.zeros((6, gz.shape[1]), f32)], axis=0), i == 0)
    add_to(acc_ref, mm_tn(x_ref[0], low), i == 0)

    @pl.when(i == PATCH - 1)
    def _():
        c1, c2 = sum_ref[0:1], sum_ref[1:2]
        s1, s2 = back_coefs((c1, c2), vec_ref[4:5], vec_ref[7:8], g256_ref[...], True)
        zero = jnp.zeros_like(c1)
        bias, gain = tile4(fold(c1)), tile4(fold(c2))
        out_ref[...] = jnp.concatenate([s1, s2, bias, gain] + [zero] * 4, axis=0)
        c, n = skip_ref.shape
        skip_ref[...] = sum(
            acc_ref[j * c : (j + 1) * c, j * n : (j + 1) * n] for j in range(PATCH)
        )


def stem_back1(g_h, pw, d3, p2, x, w_out, stat, vec, g256, chain=None):
    lanes = d3.shape[2]
    c = p2.shape[2] // PATCH
    s = jax.ShapeDtypeStruct
    return launch(
        stem_back1_kernel,
        grid=(PATCH,),
        in_specs=[
            whole(g_h.shape), slab(pw.shape), slab(d3.shape), slab(p2.shape), slab(x.shape),
            whole(w_out.shape), whole(stat.shape), whole(vec.shape), whole(g256.shape),
        ],
        out_specs=[slab(d3.shape), whole((8, lanes)), whole((c, lanes // PATCH))],
        out_shape=[s(d3.shape, bf16), s((8, lanes), f32), s((c, lanes // PATCH), f32)],
        scratch_shapes=[pltpu.VMEM((PATCH * c, lanes), f32), pltpu.VMEM((8, lanes), f32)],
        compiler_params=BIG,
        chain=chain,
        name="stem_back1",
    )(g_h, pw, d3, p2, x, w_out, stat, vec, g256)


def stem_back2_kernel(
    gz_ref, p2_ref, d2_ref, n2_ref, w_ref, st_ref, co_ref, vec_ref, g64_ref, keep_ref,
    g2_ref, out_ref, grad_ref, acc_ref, sum_ref,
):
    i = pl.program_id(0)
    lanes = gz_ref.shape[2]
    keep = tiled(keep_ref[...], lanes)
    rstd, gain, s1, s2 = st_ref[0:1], vec_ref[4:5], co_ref[0:1], co_ref[1:2]
    n = mm(p2_ref[0], w_ref[...]) * rstd + st_ref[1:2]
    gv = (rstd * (gz_ref[0].astype(f32) * gain - s1 - n * s2) * keep).astype(bf16)
    add_to(acc_ref, mm_tn(p2_ref[0], gv), i == 0)
    g2 = mm_nt(gv, w_ref[...]) * d2_ref[0].astype(f32)
    g2_ref[0] = g2
    add_to(sum_ref, jnp.concatenate([colsum(g2), colsum(g2 * n2_ref[0].astype(f32))] + [jnp.zeros((6, g2.shape[1]), f32)], axis=0), i == 0)

    @pl.when(i == PATCH - 1)
    def _():
        narrow = g2_ref.shape[2]
        c1, c2 = sum_ref[0:1], sum_ref[1:2]
        s1, s2 = back_coefs((c1, c2), vec_ref[2:3, :narrow], vec_ref[6:7, :narrow], g64_ref[...], False)
        out_ref[...] = jnp.concatenate([s1, s2, c1, c2] + [jnp.zeros_like(c1)] * 4, axis=0)
        c, n = grad_ref.shape
        grad_ref[...] = sum(
            acc_ref[j * c : (j + 1) * c, j * n : (j + 1) * n] for j in range(PATCH)
        )


def stem_back2(gz, p2, d2, n2, w_out, stat, coef, vec, g64, keep, chain=None):
    lanes = gz.shape[2]
    narrow = p2.shape[2]
    c = narrow // PATCH
    s = jax.ShapeDtypeStruct
    return launch(
        stem_back2_kernel,
        grid=(PATCH,),
        in_specs=[
            slab(gz.shape), slab(p2.shape), slab(d2.shape), slab(n2.shape), whole(w_out.shape),
            whole(stat.shape), whole(coef.shape), whole(vec.shape), whole(g64.shape), whole(keep.shape),
        ],
        out_specs=[slab(p2.shape), whole((8, narrow)), whole((c, lanes // PATCH))],
        out_shape=[s(p2.shape, f32), s((8, narrow), f32), s((c, lanes // PATCH), f32)],
        scratch_shapes=[pltpu.VMEM((narrow, lanes), f32), pltpu.VMEM((8, narrow), f32)],
        compiler_params=BIG,
        chain=chain,
        name="stem_back2",
    )(gz, p2, d2, n2, w_out, stat, coef, vec, g64, keep)


def edges(v, edge):
    c = v.shape[1] // PATCH
    toks = v.shape[0]
    left = pltpu.roll(v[:, 3 * c :], 1, 0)
    right = pltpu.roll(v[:, :c], toks - 1, 0)
    return jnp.concatenate([left, right], axis=1) * edge


def fill_wide(wide_ref, i, v, edge):
    lanes = v.shape[1]
    v = jnp.concatenate([v, edges(v, edge)], axis=1)
    wide_ref[i + 1] = v.astype(bf16)
    gap = jnp.zeros((SIDE, v.shape[1]), f32)
    if i == PATCH - 1:
        wide_ref[0] = jnp.concatenate([gap, v[:-SIDE]], axis=0).astype(bf16)
    if i == 0:
        wide_ref[PATCH + 1] = jnp.concatenate([v[SIDE:], gap], axis=0).astype(bf16)


def stem_back3_kernel(
    g2_ref, n2_ref, p1_ref, b_ref, d1_ref, x_ref, w_ref, st1_ref, st2_ref, co_ref, vec_ref, g64_ref,
    keep_ref, edge_ref, g1_ref, out_ref, grad_ref, wide_ref,
):
    narrow = g2_ref.shape[2]
    c = narrow // PATCH
    keep = tiled(keep_ref[...], narrow)
    rstd, gain, s1, s2 = st2_ref[0:1], vec_ref[2:3, :narrow], co_ref[0:1], co_ref[1:2]
    for i in range(PATCH):
        gv = rstd * (g2_ref[i] * gain - s1 - n2_ref[i].astype(f32) * s2) * keep
        fill_wide(wide_ref, i, gv, edge_ref[...])
    for di in range(3):
        total = 0.0
        for i in range(PATCH):
            total = total + mm_tn(p1_ref[i + di], wide_ref[i + 1, :, :narrow])
        for dj in range(3):
            grad_ref[3 * di + dj] = sum(
                total[k * c : (k + 1) * c, j * c : (j + 1) * c]
                for j in range(PATCH)
                for k in (SRCS.index(j + dj - 1),)
            )
    c1 = c2 = 0.0
    for i in range(PATCH):
        g1 = sum(mm_nt(wide_ref[i + di], b_ref[di]) for di in range(3)) * d1_ref[i].astype(f32)
        g1_ref[i] = g1
        n = mm(x_ref[i], w_ref[...]) * st1_ref[0:1] + st1_ref[1:2]
        c1 = c1 + colsum(g1)
        c2 = c2 + colsum(g1 * n)
    s1, s2 = back_coefs((c1, c2), vec_ref[0:1, :narrow], vec_ref[6:7, :narrow], g64_ref[...], False)
    out_ref[...] = jnp.concatenate([s1, s2, c1, c2] + [jnp.zeros_like(c1)] * 4, axis=0)


def stem_back3(g2, n2, p1_wide, b_bwd, d1, x, w_in, stat1, stat2, coef, vec, g64, keep, edge, chain=None):
    narrow = g2.shape[2]
    c = narrow // PATCH
    s = jax.ShapeDtypeStruct
    vm = VMEM
    return launch(
        stem_back3_kernel,
        in_specs=[vm] * 14,
        out_specs=[vm] * 3,
        out_shape=[s(g2.shape, f32), s((8, narrow), f32), s((9, c, c), f32)],
        scratch_shapes=[pltpu.VMEM((PATCH + 2, TOK, 6 * c), bf16)],
        compiler_params=BIG,
        chain=chain,
        name="stem_back3",
    )(g2, n2, p1_wide, b_bwd, d1, x, w_in, stat1, stat2, coef, vec, g64, keep, edge)


def stem_back4_kernel(
    rank_ref, g1_ref, x_ref, gz_ref, win_ref, wskip_ref, st_ref, co_ref, vec_ref, keep_ref,
    o0_ref, o1_ref, o2_ref, o3_ref, grad_ref, acc_ref, ig_ref,
):
    i = pl.program_id(0)
    narrow = g1_ref.shape[2]
    keep = tiled(keep_ref[...], narrow)
    rstd, gain, s1, s2 = st_ref[0:1], vec_ref[0:1, :narrow], co_ref[0:1], co_ref[1:2]
    n = mm(x_ref[0], win_ref[...]) * rstd + st_ref[1:2]
    gv = (rstd * (g1_ref[0] * gain - s1 - n * s2) * keep).astype(bf16)
    add_to(acc_ref, mm_tn(x_ref[0], gv), i == 0)
    ig_ref[...] = (mm_nt(gv, win_ref[...]) + mm_nt(gz_ref[0], wskip_ref[...])) * keep
    for k, o_ref in enumerate((o0_ref, o1_ref, o2_ref, o3_ref)):
        toks = o_ref.shape[1]
        at = pl.ds(pl.multiple_of((rank_ref[0] ^ k) * toks, 16), toks)
        o_ref[0] = ig_ref[at, :].astype(bf16)

    @pl.when(i == PATCH - 1)
    def _():
        c = grad_ref.shape[0]
        grad_ref[...] = sum(
            acc_ref[j * c : (j + 1) * c, j * c : (j + 1) * c] for j in range(PATCH)
        )


def stem_back4(rank, g1, x, gz, w_in, w_skip, stat, coef, vec, keep, ranks, chain=None):
    narrow = g1.shape[2]
    c = narrow // PATCH
    part = jax.ShapeDtypeStruct((PATCH, TOK // ranks, narrow), bf16)
    return launch(
        stem_back4_kernel,
        grid=(PATCH,),
        in_specs=[
            SMEM, slab(g1.shape), slab(x.shape), slab(gz.shape), whole(w_in.shape), whole(w_skip.shape),
            whole(stat.shape), whole(coef.shape), whole(vec.shape), whole(keep.shape),
        ],
        out_specs=[slab(part.shape)] * ranks + [whole((c, c))],
        out_shape=[part] * ranks + [jax.ShapeDtypeStruct((c, c), f32)],
        scratch_shapes=[pltpu.VMEM((narrow, narrow), f32), pltpu.VMEM((TOK, narrow), f32)],
        compiler_params=BIG,
        chain=chain,
        name="stem_back4",
    )(rank, g1, x, gz, w_in, w_skip, stat, coef, vec, keep)


def scale_shift(c1, c2, gain, bias, inv, gmat, wide):
    pair = jnp.concatenate([c1, c2], axis=0)
    if wide:
        pair = fold(pair)
    pair = exact(jnp.concatenate([pair, jnp.zeros((6, pair.shape[1]), f32)], axis=0), gmat)
    if wide:
        pair = tile4(pair)
    mean, square = pair[0:1] * inv, pair[1:2] * inv
    rstd = lax.rsqrt(square - mean * mean + 1e-05)
    shift = -mean * rstd
    return rstd, shift, rstd * gain, bias + shift * gain


def stem_front_kernel(
    rank_ref, x0_ref, x1_ref, x2_ref, x3_ref,
    win_ref, bf_ref, wout_ref, vec_ref, g64_ref, g256_ref, keep_ref, edge_ref,
    x_ref, wide_ref, d1_ref, p2_ref, d2_ref, n2_ref, st1_ref, st2_ref, st3_ref, v_ref,
):
    narrow = x_ref.shape[2]
    for k, part_ref in enumerate((x0_ref, x1_ref, x2_ref, x3_ref)):
        toks = part_ref.shape[1]
        at = pl.ds(pl.multiple_of((rank_ref[0] ^ k) * toks, 16), toks)
        mask = tiled(keep_ref[at, :], narrow)
        for i in range(PATCH):
            x_ref[i, at, :] = (part_ref[i].astype(f32) * mask).astype(bf16)
    keep = tiled(keep_ref[...], narrow)
    inv = vec_ref[6:7, :narrow]
    c1 = c2 = 0.0
    for i in range(PATCH):
        v = mm(x_ref[i], win_ref[...])
        v_ref[i] = v
        c1, c2 = c1 + colsum(v), c2 + colsum(v * v)
    rstd, shift, a, b = scale_shift(c1, c2, vec_ref[0:1, :narrow], vec_ref[1:2, :narrow], inv, g64_ref[...], False)
    st1_ref[...] = jnp.concatenate([rstd, shift], axis=0)
    for i in range(PATCH):
        act, slope = gelu_both(v_ref[i] * a + b)
        d1_ref[i] = (slope * keep).astype(bf16)
        fill_wide(wide_ref, i, act * keep, edge_ref[...])
    c1 = c2 = 0.0
    for i in range(PATCH):
        v = sum(mm(wide_ref[i + di], bf_ref[di]) for di in range(3))
        v_ref[i] = v
        v = v * keep
        c1, c2 = c1 + colsum(v), c2 + colsum(v * v)
    rstd, shift, a, b = scale_shift(c1, c2, vec_ref[2:3, :narrow], vec_ref[3:4, :narrow], inv, g64_ref[...], False)
    st2_ref[...] = jnp.concatenate([rstd, shift], axis=0)
    c1 = c2 = 0.0
    for i in range(PATCH):
        v = v_ref[i]
        act, slope = gelu_both(v * a + b)
        d2_ref[i] = (slope * keep).astype(bf16)
        n2_ref[i] = (v * rstd + shift).astype(bf16)
        low = (act * keep).astype(bf16)
        p2_ref[i] = low
        v = mm(low, wout_ref[...])
        c1, c2 = c1 + colsum(v), c2 + colsum(v * v)
    st3_ref[...] = jnp.concatenate(
        scale_shift(c1, c2, vec_ref[4:5], vec_ref[5:6], vec_ref[7:8], g256_ref[...], True), axis=0
    )


def stem_front(rank, parts, w_in, b_fwd, w_out, vec, g64, g256, keep, edge, chain=None):
    narrow = parts[0].shape[2]
    s = jax.ShapeDtypeStruct
    vm = pl.BlockSpec(memory_space=pltpu.VMEM)
    low = s((PATCH, TOK, narrow), bf16)
    return launch(
        stem_front_kernel,
        in_specs=[SMEM] + [vm] * 12,
        out_specs=[vm] * 9,
        out_shape=[
            low, s((PATCH + 2, TOK, narrow * 3 // 2), bf16), low, low, low, low,
            s((2, narrow), f32), s((2, narrow), f32), s((4, w_out.shape[1]), f32),
        ],
        scratch_shapes=[pltpu.VMEM((PATCH, TOK, narrow), f32)],
        compiler_params=BIG,
        chain=chain,
        name="stem_front",
    )(rank, *parts, w_in, b_fwd, w_out, vec, g64, g256, keep, edge)


def stem_last_kernel(p2_ref, x_ref, wout_ref, wskip_ref, st_ref, keep_ref, stem_ref, d3_ref):
    keep = tiled(keep_ref[...], wout_ref.shape[1])
    z = mm(p2_ref[0], wout_ref[...]) * st_ref[2:3] + st_ref[3:4] + mm(x_ref[0], wskip_ref[...])
    act, slope = gelu_both(z)
    stem_ref[0] = (act * keep).astype(bf16)
    d3_ref[0] = (slope * keep).astype(bf16)


def stem_last(p2, x, w_out, w_skip, stat, keep, chain=None):
    lanes = w_out.shape[1]
    shape = p2.shape[:2] + (lanes,)
    o = jax.ShapeDtypeStruct(shape, bf16)
    return launch(
        stem_last_kernel,
        grid=(PATCH,),
        in_specs=[slab(p2.shape), slab(x.shape), whole(w_out.shape), whole(w_skip.shape), whole(stat.shape), whole(keep.shape)],
        out_specs=[slab(shape)] * 2,
        out_shape=[o, o],
        compiler_params=BIG,
        chain=chain,
        name="stem_last",
    )(p2, x, w_out, w_skip, stat, keep)


def pack_kernel(rank_ref, x_ref, *refs):
    outs, wide_ref = refs[:-1], refs[-1]
    rows, chans, cols = x_ref.shape[1:]
    for r in range(rows):
        wide_ref[r * cols : (r + 1) * cols, :] = x_ref[0, r].astype(f32).T
    for k, o_ref in enumerate(outs):

        @pl.when(pl.program_id(0) == k)
        def _():
            for i in range(PATCH):
                parts = []
                for j in range(PATCH):
                    parts.append(
                        jnp.concatenate(
                            [
                                wide_ref[pl.ds(r * cols + j, SIDE, stride=PATCH), :]
                                for r in range(i, rows, PATCH)
                            ],
                            axis=0,
                        )
                    )
                o_ref[i] = jnp.concatenate(parts, axis=1).astype(o_ref.dtype)


def pack(rank, x, chain):
    images, rows, cols, chans = x.shape
    x = x.transpose(0, 1, 3, 2)
    shape = (PATCH, rows // PATCH * SIDE, PATCH * chans)
    return launch(
        pack_kernel,
        grid_spec=dict(
            num_scalar_prefetch=1,
            grid=(images,),
            in_specs=[pl.BlockSpec((1, rows, chans, cols), lambda b, r: (b ^ r[0], 0, 0, 0))],
            out_specs=[pl.BlockSpec(shape, lambda b, r: (0, 0, 0))] * images,
            scratch_shapes=[pltpu.VMEM((rows * cols, chans), f32)],
        ),
        out_shape=[jax.ShapeDtypeStruct(shape, x.dtype)] * images,
        compiler_params=MID,
        chain=chain,
        name="pack",
    )(rank, x)


def unpack_kernel(rank_ref, *refs):
    ins, o_ref, row_ref = refs[:-2], refs[-2], refs[-1]
    chans = o_ref.shape[2]
    for k, x_ref in enumerate(ins):

        @pl.when(pl.program_id(0) == k)
        def _():
            for i in range(PATCH):
                v = x_ref[i].astype(f32)
                for p in range(v.shape[0] // SIDE):
                    for j in range(PATCH):
                        row_ref[PATCH * p + i, pl.ds(j, SIDE, stride=PATCH), :] = v[
                            p * SIDE : (p + 1) * SIDE, j * chans : (j + 1) * chans
                        ]

    for r in range(o_ref.shape[1]):
        o_ref[0, r] = row_ref[r].T


def unpack(rank, parts, chain=None):
    images = len(parts)
    _, toks, lanes = parts[0].shape
    shape = (images, toks // SIDE * PATCH, lanes // PATCH, SIDE * PATCH)
    return launch(
        unpack_kernel,
        grid_spec=dict(
            num_scalar_prefetch=1,
            grid=(images,),
            in_specs=[pl.BlockSpec(parts[0].shape, lambda b, r: (0, 0, 0))] * images,
            out_specs=pl.BlockSpec((1,) + shape[1:], lambda b, r: (b ^ r[0], 0, 0, 0)),
            scratch_shapes=[pltpu.VMEM((shape[1], shape[3], shape[2]), f32)],
        ),
        out_shape=jax.ShapeDtypeStruct(shape, f32),
        compiler_params=MID,
        chain=chain,
        name="unpack",
    )(rank, *parts).transpose(0, 1, 3, 2)


def prep_kernel(
    rank_ref, group_ref, in_ref, mid_ref, out_ref, skip_ref, gain_ref, bias_ref, cot_ref,
    w_in, w_out, w_skip, b_fwd, b_bwd, g64, g256, vec, keep, edge, *cots,
):
    for k, ref in enumerate(cots):
        ref[...] = cot_ref[rank_ref[0] ^ k]
    def spread(dst, src):
        dst[...] = jnp.zeros_like(dst)
        c, n = src.shape
        for j in range(PATCH):
            dst[j * c : (j + 1) * c, j * n : (j + 1) * n] = src[...]

    spread(w_in, in_ref)
    spread(w_out, out_ref)
    spread(w_skip, skip_ref)
    b_fwd[...] = jnp.zeros_like(b_fwd)
    b_bwd[...] = jnp.zeros_like(b_bwd)
    c = mid_ref.shape[1]
    for di in range(3):
        for k, src in enumerate(SRCS):
            for j in range(PATCH):
                if abs(src - j) <= 1:
                    dj = src - j + 1
                    b_fwd[di, k * c : (k + 1) * c, j * c : (j + 1) * c] = mid_ref[3 * di + dj]
                    b_bwd[di, j * c : (j + 1) * c, k * c : (k + 1) * c] = mid_ref[8 - 3 * di - dj]
    for ref, chans in ((g64, c), (g256, gain_ref.shape[1] - 2 * c)):
        per = chans // GROUPS
        row = (lax.broadcasted_iota(jnp.int32, ref.shape, 0) & (chans - 1)) // per
        col = (lax.broadcasted_iota(jnp.int32, ref.shape, 1) & (chans - 1)) // per
        ref[...] = jnp.where(row == col, 1.0, 0.0)
    vec[...] = jnp.zeros_like(vec)
    for at, (ref, lo, hi) in enumerate(
        (r, lo, hi)
        for lo, hi in ((0, c), (c, 2 * c), (2 * c, gain_ref.shape[1]))
        for r in (gain_ref, bias_ref)
    ):
        part = jnp.concatenate([ref[:, lo:hi]] * PATCH, axis=1)
        vec[at : at + 1, : part.shape[1]] = part
    limit = jnp.where(group_ref[rank_ref[0]] == 1, FULL // PATCH, SMALL // PATCH)
    inverse = 1.0 / (jnp.full((1, vec.shape[1]), PATCH * PATCH, f32) * (limit * limit).astype(f32))
    vec[6:7] = inverse * (GROUPS / c)
    vec[7:8] = inverse * (GROUPS / (gain_ref.shape[1] - 2 * c))
    t = lax.broadcasted_iota(jnp.int32, keep.shape, 0)
    up = ((t.astype(f32) + 0.5) * (1.0 / SIDE)).astype(jnp.int32)
    t = t - SIDE * up
    keep[...] = jnp.where((up < limit) & (t < limit), 1.0, 0.0)
    left = lax.broadcasted_iota(jnp.int32, edge.shape, 1) < c
    edge[...] = jnp.where(t != jnp.where(left, 0, SIDE - 1), 1.0, 0.0)


def prep(rank, group, conv_in, conv_mid, conv_out, conv_skip, norm_gain, norm_bias, cot, chain=None):
    c, n = conv_out.shape
    s = jax.ShapeDtypeStruct
    shapes = [
        s((PATCH * c, PATCH * c), bf16),
        s((PATCH * c, PATCH * n), bf16),
        s((PATCH * c, PATCH * n), bf16),
        s((3, 6 * c, PATCH * c), bf16),
        s((3, PATCH * c, 6 * c), bf16),
        s((PATCH * c, PATCH * c), f32),
        s((PATCH * c, PATCH * c), f32),
        s((8, PATCH * n), f32),
        s((TOK, 128), f32),
        s((TOK, 2 * c), f32),
    ] + [s(cot.shape[1:], bf16)] * cot.shape[0]
    return launch(
        prep_kernel,
        in_specs=[SMEM, SMEM] + [VMEM] * 7,
        out_specs=[VMEM] * len(shapes),
        out_shape=shapes,
        chain=chain,
        name="prep",
    )(
        rank.reshape(1),
        group,
        conv_in,
        conv_mid.transpose(1, 0, 2),
        conv_out,
        conv_skip,
        norm_gain[None],
        norm_bias[None],
        cot,
    )


def ln_stats(h):
    mean = jnp.mean(h, axis=-1, keepdims=True)
    cen = h - mean
    rstd = lax.rsqrt(jnp.mean(cen * cen, axis=-1, keepdims=True) + 1e-05)
    return cen * rstd, rstd


def ln_back(gy, n, rstd, gain):
    gn = gy * gain
    gh = rstd * (
        gn - jnp.mean(gn, axis=-1, keepdims=True) - n * jnp.mean(gn * n, axis=-1, keepdims=True)
    )
    return gh, jnp.sum(gy * n, axis=0), jnp.sum(gy, axis=0)


def slot_of(q, rank):
    rel = q ^ rank
    return rel & 1, rel >> 1


def store_slot(keep_ref, send_ref, core, at, value):
    @pl.when(core == 0)
    def _():
        keep_ref[at] = value

    @pl.when(core == 1)
    def _():
        send_ref[at] = value


def wgrad_cols_kernel(rank_ref, a_ref, g_ref, keep_ref, send_ref):
    total = mm_tn(a_ref[...], g_ref[...]).astype(bf16)
    rows = keep_ref.shape[-2]
    for q in range(total.shape[0] // rows):
        core, over = slot_of(q, rank_ref[0])
        store_slot(keep_ref, send_ref, core, (0, over, 0), total[q * rows : (q + 1) * rows])


def wgrad_cols(rank, a, g, chain=None):
    toks, k = a.shape
    blocks = g.shape[1] // k
    rows = k // 4
    half = blocks // 2
    shape = (2, 2, half, rows, k)
    spec = pl.BlockSpec((1, 2, 1, rows, k), lambda b: (b // half, 0, b % half, 0, 0))
    o = jax.ShapeDtypeStruct(shape, bf16)
    return launch(
        wgrad_cols_kernel,
        grid=(blocks,),
        in_specs=[SMEM, whole(a.shape), pl.BlockSpec((toks, k), lambda b: (0, b))],
        out_specs=[spec, spec],
        out_shape=[o, o],
        compiler_params=MID,
        chain=chain,
        name="wgrad_cols",
    )(rank, a, g)


def wgrad_qkv_kernel(rank_ref, a_ref, g_ref, a2_ref, g2_ref, keep_ref, send_ref):
    last = pl.program_id(0) == pl.num_programs(0) - 1

    @pl.when(jnp.logical_not(last))
    def _():
        wgrad_cols_kernel(rank_ref, a_ref, g_ref, keep_ref, send_ref)

    @pl.when(last)
    def _():
        wgrad_cols_kernel(rank_ref, a2_ref, g2_ref, keep_ref, send_ref)


def wgrad_qkv(rank, a, g, a2, g2, chain=None):
    toks, k = a.shape
    rows = k // 4
    o = jax.ShapeDtypeStruct((2, 2, 2, rows, k), bf16)
    spec = pl.BlockSpec((1, 2, 1, rows, k), lambda b: (b // 2, 0, b % 2, 0, 0))
    return launch(
        wgrad_qkv_kernel,
        grid=(4,),
        in_specs=[
            SMEM, whole(a.shape), pl.BlockSpec((toks, k), lambda b: (0, jnp.minimum(b, 2))),
            whole(a.shape), whole(a.shape),
        ],
        out_specs=[spec, spec],
        out_shape=[o, o],
        compiler_params=MID,
        chain=chain,
        name="wgrad_qkv",
    )(rank, a, g, a2, g2)


def wgrad_rows_kernel(rank_ref, a_ref, g_ref, keep_ref, send_ref):
    total = mm_tn(a_ref[...], g_ref[...]).astype(bf16)
    step = pl.program_id(0)
    rows = total.shape[0] // (1 if len(keep_ref.shape) == 2 else keep_ref.shape[0])

    def put(ref):
        if len(ref.shape) == 2:
            ref[...] = total
        else:
            for h in range(ref.shape[0]):
                ref[h] = total[h * rows : (h + 1) * rows]

    @pl.when(step < 2)
    def _():
        put(send_ref)

    @pl.when(step >= 2)
    def _():
        put(keep_ref)


def wgrad_rows(rank, a, g, outer, chain=None):
    toks, n = g.shape
    rows = a.shape[2] if a.ndim == 3 else a.shape[1] // 4

    def quarter(step, rank_ref):
        rel = (step % 2) * 2 + jnp.where(step < 2, 1, 0)
        return rel ^ rank_ref[0]

    if a.ndim == 3:
        a_spec = pl.BlockSpec((None, toks, rows), lambda s, r: (quarter(s, r), 0, 0))
    else:
        a_spec = pl.BlockSpec((toks, rows), lambda s, r: (0, quarter(s, r)))
    if outer > 1:
        shape = (outer, 2, rows // outer, n)
        block = (outer, None, rows // outer, n)
        specs = [
            pl.BlockSpec(block, lambda s, r: (0, jnp.maximum(s - 2, 0), 0, 0)),
            pl.BlockSpec(block, lambda s, r: (0, jnp.minimum(s, 1), 0, 0)),
        ]
    else:
        shape = (2, rows, n)
        specs = [
            pl.BlockSpec((None, rows, n), lambda s, r: (jnp.maximum(s - 2, 0), 0, 0)),
            pl.BlockSpec((None, rows, n), lambda s, r: (jnp.minimum(s, 1), 0, 0)),
        ]
    o = jax.ShapeDtypeStruct(shape, bf16)
    return launch(
        wgrad_rows_kernel,
        grid_spec=dict(
            num_scalar_prefetch=1,
            grid=(4,),
            in_specs=[a_spec, pl.BlockSpec((toks, n), lambda s, r: (0, 0))],
            out_specs=specs,
        ),
        out_shape=[o, o],
        compiler_params=MID,
        chain=chain,
        name="wgrad_rows",
    )(rank, a, g)


VECS = 6


def collect_kernel(rank_ref, in_ref, mid_ref, cout_ref, skip_ref, co1_ref, co2_ref, co3_ref, *refs):
    vecs, up_ref, (keep_ref, send_ref) = refs[:VECS], refs[VECS], refs[VECS + 1 :]
    c, lanes = cout_ref.shape
    part = c // 4
    norms = []
    for row in (3, 2):
        norms.append(
            jnp.concatenate(
                [fold(co1_ref[row : row + 1]), fold(co2_ref[row : row + 1]), co3_ref[row : row + 1, :lanes]],
                axis=1,
            )
        )

    def full(v):
        gap = lanes - v.shape[1]
        return jnp.concatenate([v, jnp.zeros((v.shape[0], gap), f32)], axis=1) if gap else v

    for q in range(4):
        rows = slice(q * part, (q + 1) * part)
        blocks = [cout_ref[rows], skip_ref[rows]]
        for di in range(3):
            blocks.append(full(jnp.concatenate([mid_ref[3 * di + dj, rows] for dj in range(3)], axis=1)))
        blocks.append(full(in_ref[rows]))

        def quarter(v):
            n = v.shape[1] // 4
            return v[:, q * n : (q + 1) * n]

        small = [full(quarter(v[...])) for v in vecs]
        up = quarter(up_ref[...])
        small += [up[:, k * lanes : (k + 1) * lanes] for k in range(up.shape[1] // lanes)]
        small += [full(quarter(v)) for v in norms]
        small.append(jnp.zeros((16 - len(small), lanes), f32))
        total = jnp.concatenate(blocks + small, axis=0)
        core, over = slot_of(q, rank_ref[0])
        store_slot(keep_ref, send_ref, core, over, total)


def collect(rank, g_in, g_mid, g_cout, g_skip, co1, co2, co3, vecs, up, chain=None):
    c, lanes = g_cout.shape
    rows = 6 * (c // 4) + 16
    o = jax.ShapeDtypeStruct((2, rows, lanes), f32)
    return launch(
        collect_kernel,
        in_specs=[SMEM] + [VMEM] * (8 + VECS),
        out_specs=[VMEM] * 2,
        out_shape=[o, o],
        compiler_params=MID,
        chain=chain,
        name="collect",
    )(rank, g_in, g_mid, g_cout, g_skip, co1, co2, co3, *vecs, up)


def deal_kernel(v_ref, in_ref, mid_ref, cout_ref, skip_ref, gain_ref, bias_ref, *refs):
    vecs, up_ref = refs[:VECS], refs[VECS]
    part, c = in_ref.shape
    lanes = v_ref.shape[1]
    cout_ref[...] = v_ref[:part]
    skip_ref[...] = v_ref[part : 2 * part]
    for di in range(3):
        for dj in range(3):
            mid_ref[3 * di + dj] = v_ref[(2 + di) * part : (3 + di) * part, dj * c : (dj + 1) * c]
    in_ref[...] = v_ref[5 * part : 6 * part, :c]
    at = 6 * part
    for ref in vecs:
        ref[...] = v_ref[at : at + 1, : ref.shape[1]]
        at += 1
    for k in range(up_ref.shape[1] // lanes):
        up_ref[:, k * lanes : (k + 1) * lanes] = v_ref[at : at + 1]
        at += 1
    gain_ref[...] = v_ref[at : at + 1, : gain_ref.shape[1]]
    bias_ref[...] = v_ref[at + 1 : at + 2, : bias_ref.shape[1]]


def deal(v, part, c, n, norms, width, hidden):
    s = jax.ShapeDtypeStruct
    shapes = [s((part, c), f32), s((9, part, c), f32), s((part, n), f32), s((part, n), f32)]
    shapes += [s((1, norms), f32)] * 2 + [s((1, width), f32)] * VECS + [s((1, hidden), f32)]
    return launch(
        deal_kernel,
        in_specs=[VMEM],
        out_specs=[VMEM] * len(shapes),
        out_shape=shapes,
        compiler_params=MID,
        name="deal",
    )(v)


def merge_kernel(bit_ref, a_ref, b_ref, c_ref, d_ref, keep_ref, send_ref):
    keep_ref[...] = (a_ref[...].astype(f32) + b_ref[...].astype(f32)).astype(bf16)
    send_ref[...] = (c_ref[...].astype(f32) + d_ref[...].astype(f32)).astype(bf16)


def merge(bit, kept, got, chain=None):
    rows, n = kept.shape
    half = rows // 2
    tiles = 2 if half >= 512 else 1
    block = (half // tiles, n)
    mine = pl.BlockSpec(block, lambda t, b: (b[0] * tiles + t, 0))
    other = pl.BlockSpec(block, lambda t, b: ((1 - b[0]) * tiles + t, 0))
    out = pl.BlockSpec(block, lambda t, b: (t, 0))
    o = jax.ShapeDtypeStruct((half, n), bf16)
    return launch(
        merge_kernel,
        grid_spec=dict(
            num_scalar_prefetch=1,
            grid=(tiles,),
            in_specs=[mine, mine, other, other],
            out_specs=[out, out],
        ),
        out_shape=[o, o],
        compiler_params=MID,
        chain=chain,
        name="merge",
    )(bit, kept, got, kept, got)


def plus_kernel(a_ref, b_ref, o_ref):
    o_ref[...] = (a_ref[...].astype(f32) + b_ref[...].astype(f32)).astype(o_ref.dtype)


def plus(a, b, chain=None):
    return launch(
        plus_kernel,
        in_specs=[VMEM] * 2,
        out_specs=VMEM,
        out_shape=jax.ShapeDtypeStruct(a.shape, a.dtype),
        compiler_params=MID,
        chain=chain,
        name="plus",
    )(a, b)


def gather_kernel(rank_ref, p0_ref, p1_ref, p2_ref, p3_ref, keep_ref, o_ref, sum_ref):
    total = 0.0
    for k, ref in enumerate((p0_ref, p1_ref, p2_ref, p3_ref)):
        toks, n = ref.shape
        at = pl.ds(pl.multiple_of((rank_ref[0] ^ k) * toks, 16), toks)
        v = ref[...].astype(f32) * tiled(keep_ref[at, :], n)
        total = total + colsum(v)
        o_ref[at, :] = v.astype(bf16)
    sum_ref[...] = total


def gather(rank, parts, keep, chain=None):
    toks, n = parts[0].shape
    return launch(
        gather_kernel,
        in_specs=[SMEM] + [VMEM] * 5,
        out_specs=[VMEM] * 2,
        out_shape=[jax.ShapeDtypeStruct((4 * toks, n), bf16), jax.ShapeDtypeStruct((1, n), f32)],
        compiler_params=MID,
        chain=chain,
        name="gather",
    )(rank, *parts, keep)


def split_kernel(a_ref, b_ref, keep_ref, send_ref):
    half = keep_ref.shape[0]
    keep_ref[...] = a_ref[:half] + b_ref[:half]
    send_ref[...] = a_ref[half:] + b_ref[half:]


def split(a, b, chain=None):
    o = jax.ShapeDtypeStruct((a.shape[0] // 2,) + a.shape[1:], a.dtype)
    return launch(
        split_kernel,
        in_specs=[VMEM] * 2,
        out_specs=[VMEM] * 2,
        out_shape=[o, o],
        compiler_params=MID,
        chain=chain,
        name="split",
    )(a, b)


def merge_two(bit, kept, got, kept2, got2, chain=None):
    def body(bit_ref, a_ref, b_ref, c_ref, d_ref, keep_ref, send_ref):
        def put(first_ref, second_ref):
            first_ref[...] = (a_ref[...].astype(f32) + b_ref[...].astype(f32)).astype(bf16)
            second_ref[...] = (c_ref[...].astype(f32) + d_ref[...].astype(f32)).astype(bf16)

        @pl.when(bit_ref[0] == 0)
        def _():
            put(keep_ref, send_ref)

        @pl.when(bit_ref[0] == 1)
        def _():
            put(send_ref, keep_ref)

    o = jax.ShapeDtypeStruct(kept.shape, bf16)
    return launch(
        body,
        in_specs=[SMEM] + [VMEM] * 4,
        out_specs=[VMEM] * 2,
        out_shape=[o, o],
        compiler_params=MID,
        chain=chain,
        name="merge_two",
    )(bit, kept, got, kept2, got2)


def put_blocks(ref, value, first, rows):
    n = value.shape[1]
    for k in range(value.shape[0] // rows):
        ref[:, pl.ds(pl.multiple_of((first + k) * n, 128), n)] = value[k * rows : (k + 1) * rows]


def finish_mlp(bit, own, got, ranks, chain=None):
    rows, n = own.shape
    half, part = rows // 2, n // ranks

    def body(bit_ref, own_ref, got_ref, down_ref, up_ref):
        for ref, place in ((own_ref, bit_ref[0]), (got_ref, 1 - bit_ref[0])):
            v = ref[...].astype(f32)
            down_ref[pl.ds(pl.multiple_of(place * half, 16), half), :] = v[:half]
            put_blocks(up_ref, v[half:], place * (half // part), part)

    s = jax.ShapeDtypeStruct
    return launch(
        body,
        in_specs=[SMEM, VMEM, VMEM],
        out_specs=[VMEM] * 2,
        out_shape=[s((rows, n), f32), s((part, rows // part * n), f32)],
        compiler_params=MID,
        chain=chain,
        name="finish_mlp",
    )(bit, own, got)


def finish_qkv(bit, own, got, ranks, chain=None):
    rows, n = own.shape
    part = n // ranks

    def body(bit_ref, own_ref, got_ref, qkv_ref, out_ref):
        def put(low_ref, high_ref):
            qkv_ref[:, :n] = low_ref[:part].astype(f32)
            qkv_ref[:, n : 2 * n] = low_ref[part:].astype(f32)
            qkv_ref[:, 2 * n :] = high_ref[:part].astype(f32)
            out_ref[...] = high_ref[part:].astype(f32)

        @pl.when(bit_ref[0] == 0)
        def _():
            put(own_ref, got_ref)

        @pl.when(bit_ref[0] == 1)
        def _():
            put(got_ref, own_ref)

    s = jax.ShapeDtypeStruct
    return launch(
        body,
        in_specs=[SMEM, VMEM, VMEM],
        out_specs=[VMEM] * 2,
        out_shape=[s((part, 3 * n), f32), s((part, n), f32)],
        compiler_params=MID,
        chain=chain,
        name="finish_qkv",
    )(bit, own, got)


def join_kernel(bit_ref, own_ref, got_ref, o_ref):
    o_ref[bit_ref[0]] = own_ref[...].astype(o_ref.dtype)
    o_ref[1 - bit_ref[0]] = got_ref[...].astype(o_ref.dtype)


def join(bit, own, got, dtype, chain=None):
    rows, n = own.shape
    o = launch(
        join_kernel,
        in_specs=[SMEM, VMEM, VMEM],
        out_specs=VMEM,
        out_shape=jax.ShapeDtypeStruct((2, rows, n), dtype),
        compiler_params=MID,
        chain=chain,
        name="join",
    )(bit, own, got)
    return o.reshape(2 * rows, n)


def mlp_back1_kernel(g_ref, w_ref, slope_ref, o_ref, bias_ref):
    g = mm_nt(g_ref[...], w_ref[...]) * slope_ref[...].astype(f32)
    bias_ref[...] = colsum(g)
    o_ref[...] = g.astype(bf16)


def mlp_back1(g, weight, slope, chain=None):
    toks, n = g.shape
    hidden = weight.shape[0]
    s = jax.ShapeDtypeStruct
    return launch(
        mlp_back1_kernel,
        grid=(hidden // n,),
        in_specs=[
            whole(g.shape), pl.BlockSpec((n, n), lambda b: (b, 0)), pl.BlockSpec((toks, n), lambda b: (0, b)),
        ],
        out_specs=[pl.BlockSpec((toks, n), lambda b: (0, b)), pl.BlockSpec((1, n), lambda b: (0, b))],
        out_shape=[s((toks, hidden), bf16), s((1, hidden), f32)],
        compiler_params=MID,
        chain=chain,
        name="mlp_back1",
    )(g, weight, slope)


def norm_back(gy, h, gain):
    n, rstd = ln_stats(h)
    gn = gy * gain
    gh = rstd * (
        gn - jnp.mean(gn, axis=-1, keepdims=True) - n * jnp.mean(gn * n, axis=-1, keepdims=True)
    )
    return gh, colsum(gy * n), colsum(gy)


def mlp_back2_kernel(
    g_ref, w_ref, h_ref, gain_ref, final_ref, out_ref,
    gh_ref, low_ref, att_ref, dgain_ref, dbias_ref, acc_ref,
):
    step = pl.program_id(0)
    add_to(acc_ref, mm_nt(g_ref[...], w_ref[...]), step == 0)

    @pl.when(step == pl.num_programs(0) - 1)
    def _():
        gh, dgain_ref[...], dbias_ref[...] = norm_back(acc_ref[...], h_ref[...], gain_ref[...])
        gh = gh + final_ref[...].astype(f32)
        gh_ref[...] = gh
        low = gh.astype(bf16)
        low_ref[...] = low
        att_ref[...] = mm_nt(low, out_ref[...]).astype(bf16)


def mlp_back2(g, weight, hidden, gain, final, out_weight, chain=None):
    toks, n = hidden.shape
    s = jax.ShapeDtypeStruct
    full = whole((toks, n))
    return launch(
        mlp_back2_kernel,
        grid=(g.shape[1] // n,),
        in_specs=[
            pl.BlockSpec((toks, n), lambda b: (0, b)), pl.BlockSpec((n, n), lambda b: (0, b)),
            full, whole((1, n)), full, whole((n, n)),
        ],
        out_specs=[full, full, full, whole((1, n)), whole((1, n))],
        out_shape=[s((toks, n), f32), s((toks, n), bf16), s((toks, n), bf16), s((1, n), f32), s((1, n), f32)],
        scratch_shapes=[pltpu.VMEM((toks, n), f32)],
        compiler_params=MID,
        chain=chain,
        name="mlp_back2",
    )(g, weight, hidden, gain[None], final, out_weight)


def qkv_back_kernel(g_ref, w_ref, h_ref, gain_ref, gh2_ref, low_ref, dgain_ref, dbias_ref, sum_ref, acc_ref):
    step = pl.program_id(0)
    add_to(acc_ref, mm_nt(g_ref[...], w_ref[...]), step == 0)

    @pl.when(step == pl.num_programs(0) - 1)
    def _():
        gh, dgain_ref[...], dbias_ref[...] = norm_back(acc_ref[...], h_ref[...], gain_ref[...])
        gh = gh + gh2_ref[...]
        sum_ref[...] = colsum(gh)
        low_ref[...] = gh.astype(bf16)


def qkv_back(g, weight, hidden, gain, gh2, chain=None):
    toks, n = hidden.shape
    s = jax.ShapeDtypeStruct
    full, row = whole((toks, n)), whole((1, n))
    return launch(
        qkv_back_kernel,
        grid=(g.shape[1] // n,),
        in_specs=[
            pl.BlockSpec((toks, n), lambda b: (0, b)), pl.BlockSpec((n, n), lambda b: (0, b)), full, row, full,
        ],
        out_specs=[full, row, row, row],
        out_shape=[s((toks, n), bf16)] + [s((1, n), f32)] * 3,
        scratch_shapes=[pltpu.VMEM((toks, n), f32)],
        compiler_params=MID,
        chain=chain,
        name="qkv_back",
    )(g, weight, hidden, gain[None], gh2)


def attend_kernel(keep_ref, q_ref, k_ref, v_ref, o_ref, l_ref):
    scale = HEAD_DIM**-0.5
    valid = keep_ref[...] > 0
    outs = []
    for h in range(2):
        lanes = slice(h * HEAD_DIM, (h + 1) * HEAD_DIM)
        q, k, v = q_ref[:, lanes], k_ref[:, lanes], v_ref[:, lanes]
        s = jnp.where(valid, mm_nt(k, q) * scale, -1000000000.0)
        top = jnp.max(s, axis=0, keepdims=True)
        e = jnp.exp(s - top)
        total = jnp.sum(e, axis=0, keepdims=True)
        outs.append(mm_tn(v, e.astype(bf16)) / total)
        l_ref[0, h : h + 1, :] = top + jnp.log(total)
    o_ref[...] = jnp.concatenate(outs, axis=0).T.astype(bf16)

def attend(qkv, keep, chain=None):
    tok, width3 = qkv.shape
    pairs = HEADS // 2
    two = 2 * HEAD_DIM
    def spec(kind):
        return pl.BlockSpec((tok, two), lambda h: (0, kind * pairs + h))
    return launch(
        attend_kernel, grid=(pairs,),
        in_specs=[pl.BlockSpec((tok, 1), lambda h: (0, 0)), spec(0), spec(1), spec(2)],
        out_specs=[spec(0), pl.BlockSpec((1, 2, tok), lambda h: (h, 0, 0))],
        out_shape=[jax.ShapeDtypeStruct((tok, width3 // 3), bf16), jax.ShapeDtypeStruct((pairs, 2, tok), f32)],
        compiler_params=pltpu.CompilerParams(vmem_limit_bytes=40*1024*1024),
        chain=chain,
        name="attend",
    )(keep, qkv, qkv, qkv)

def attend_back_kernel(keep_ref, q_ref, k_ref, v_ref, g_ref, l_ref, o_ref):
    scale = HEAD_DIM**-0.5
    valid = keep_ref[...] > 0
    gqs, gks, gvs = [], [], []
    for h in range(2):
        lanes = slice(h * HEAD_DIM, (h + 1) * HEAD_DIM)
        q, k, v, g = q_ref[:, lanes], k_ref[:, lanes], v_ref[:, lanes], g_ref[:, lanes]
        s = jnp.where(valid, mm_nt(k, q) * scale, -1000000000.0)
        p = jnp.exp(s - l_ref[0, h : h + 1, :])
        gp = mm_nt(v, g)
        dot = jnp.sum(gp * p, axis=0, keepdims=True)
        gs = (p * (gp - dot)).astype(bf16)
        gvs.append(mm(p.astype(bf16), g))
        gks.append(mm(gs, q) * scale)
        gqs.append(mm_tn(k, gs) * scale)
    width = o_ref.shape[1] // 3
    step = pl.program_id(0)
    for kind, value in enumerate(
        (jnp.concatenate(gqs, axis=0).T, jnp.concatenate(gks, axis=1), jnp.concatenate(gvs, axis=1))
    ):
        lanes = pl.ds(pl.multiple_of(kind * width + step * 2 * HEAD_DIM, 128), 2 * HEAD_DIM)
        o_ref[:, lanes] = value.astype(bf16)


def attend_back(qkv, keep, g, logs, chain=None):
    tok, width3 = qkv.shape
    pairs = HEADS // 2
    two = 2 * HEAD_DIM
    def spec(kind):
        return pl.BlockSpec((tok, two), lambda h: (0, kind * pairs + h))
    return launch(
        attend_back_kernel, grid=(pairs,),
        in_specs=[pl.BlockSpec((tok, 1), lambda h: (0, 0)), spec(0), spec(1), spec(2), spec(0), pl.BlockSpec((1, 2, tok), lambda h: (h, 0, 0))],
        out_specs=whole((tok, width3)),
        out_shape=jax.ShapeDtypeStruct((tok, width3), bf16),
        compiler_params=pltpu.CompilerParams(vmem_limit_bytes=40*1024*1024),
        chain=chain,
        name="attend_back",
    )(keep, qkv, qkv, qkv, g, logs)


def per_image(parts, cots, made, params, flows):
    (
        conv_in,
        conv_mid,
        conv_out,
        conv_skip,
        norm_gain,
        norm_bias,
        patch_weight,
        patch_bias,
        attn_gain,
        attn_bias,
        qkv_weight,
        out_weight,
        mlp_gain,
        mlp_bias,
        up_weight,
        up_bias,
        down_weight,
        down_bias,
    ) = params
    w_in, w_out, w_skip, b_fwd, b_bwd, g64, g256, vec, keep_wide, edge = made
    c0 = conv_in.shape[0]
    c3 = conv_out.shape[1]
    ranks = lax.axis_size("row")
    keep = keep_wide[:, :1]
    chain = flows.chain
    x, wide, d1, p2, d2, n2, st1, st2, st3 = stem_front(
        flows.rank, parts, w_in, b_fwd, w_out, vec, g64, g256, keep_wide, edge, chain
    )
    stem, d3 = stem_last(p2, x, w_out, w_skip, st3, keep_wide, chain)
    pw = patch_weight.reshape(PATCH, PATCH * c3, -1)
    hidden = patch_bias
    for i in range(PATCH):
        hidden = hidden + mm(stem[i], pw[i])
    na, ra = ln_stats(hidden)
    normed = (na * attn_gain + attn_bias).astype(bf16)
    qkv = mm(normed, qkv_weight).astype(bf16)
    attended, logs = attend(qkv, keep, chain)
    hidden2 = hidden + mm(attended, out_weight)
    nm, rm = ln_stats(hidden2)
    normed2 = (nm * mlp_gain + mlp_bias).astype(bf16)
    pre = mm(normed2, up_weight) + up_bias
    act, dact = gelu_both(pre)
    act = act.astype(bf16)
    block_out = ((hidden2 + mm(act, down_weight) + down_bias) * keep).astype(bf16)
    g_low, grad_down_bias = gather(flows.rank, cots, keep_wide, chain)
    rank = flows.rank
    flows.begin("down", wgrad_rows(rank, act, g_low, 1, chain), order_of("x"))
    g_pre, grad_up_bias = mlp_back1(g_low, down_weight, dact.astype(bf16), chain)
    flows.pump("grad")
    flows.begin("up", wgrad_cols(rank, normed2, g_pre, chain), order_of("y"))
    g_h2, g_h2_low, g_att, grad_mlp_gain, grad_mlp_bias = mlp_back2(
        g_pre, up_weight, hidden2, mlp_gain, g_low, out_weight, chain
    )
    flows.pump("mlp")
    g_qkv = attend_back(qkv, keep, g_att, logs, chain)
    flows.pump("att")
    g_h, grad_attn_gain, grad_attn_bias, grad_patch_bias = qkv_back(
        g_qkv, qkv_weight, hidden, attn_gain, g_h2, chain
    )
    flows.begin("patch", wgrad_rows(rank, stem, g_h, 1, chain), order_of("x"))
    flows.pump("patch")
    parts = wgrad_qkv(rank, normed, g_qkv, attended, g_h2_low, chain)
    flows.begin("qkv", parts, order_of("y"), finish_qkv)
    flows.pump("qkv")
    g_z, co3, grad_skip = stem_back1(
        g_h, pw, d3, p2, x, w_out, st3, vec, g256, flows.chain
    )
    flows.pair("mlp", "down", "up", finish_mlp)
    g_2, co2, grad_cout = stem_back2(
        g_z, p2, d2, n2, w_out, st3, co3, vec, g64, keep_wide, flows.chain
    )
    flows.pump("back2")
    g_1, co1, grad_mid = stem_back3(
        g_2, n2, wide, b_bwd, d1, x, w_in, st1, st2, co2, vec, g64, keep_wide, edge, flows.chain
    )
    flows.pump("back3")
    *input_grad, grad_in = stem_back4(
        rank, g_1, x, g_z, w_in, w_skip, st1, co1, vec, keep_wide, ranks, flows.chain
    )
    vecs = (grad_patch_bias, grad_attn_gain, grad_attn_bias, grad_mlp_gain, grad_mlp_bias, grad_down_bias)
    small = collect(
        rank, grad_in, grad_mid, grad_cout, grad_skip, co1, co2, co3,
        vecs, grad_up_bias, flows.chain
    )
    return block_out, input_grad, small


def swap(v, axis, step):
    count = lax.axis_size(axis)
    return lax.ppermute(v, axis, [(i, i ^ step) for i in range(count)])


def steps_of(axis):
    count = lax.axis_size(axis)
    return [1 << b for b in range(count.bit_length() - 1)]


def bit_of(axis, step):
    return ((lax.axis_index(axis) & step) // step).astype(jnp.int32).reshape(1)


class Flow:
    def __init__(self, kept, sent, order, last=None):
        n = kept.shape[-1]
        self.kept = kept.reshape(-1, n)
        self.sent = sent.reshape(-1, n)
        self.todo = list(order)
        self.undo = [s for a, s in reversed(order) if a == "img"]
        self.last = last
        self.done = False
        self.start()

    def start(self):
        if self.todo:
            self.got = swap(self.sent, *self.todo[0])
        elif self.undo:
            self.got = swap(self.kept, "img", self.undo[0])

    def step(self, chain):
        if self.todo:
            self.todo.pop(0)
            if self.todo:
                axis, step = self.todo[0]
                bit = bit_of("img", step) if axis == "img" else jnp.zeros((1,), jnp.int32)
                self.kept, self.sent = merge(bit, self.kept, self.got, chain)
            else:
                self.kept = plus(self.kept, self.got, chain)
        else:
            step = self.undo.pop(0)
            self.done = not self.undo
            bit = bit_of("img", step)
            if self.done and self.last:
                self.kept = self.last(bit, self.kept, self.got, lax.axis_size("row"), chain)
            else:
                self.kept = join(bit, self.kept, self.got, f32 if self.done else bf16, chain)
        self.start()


class Pair(Flow):
    def __init__(self, one, two, last, chain):
        order = [(a, s) for a, s in order_of("x") if a == "img"]
        self.undo = [s for a, s in reversed(order)]
        order = order[1:]
        self.todo = list(order)
        self.last = last
        self.done = False
        bit = bit_of(*order[0])
        self.kept, self.sent = merge_two(bit, one.kept, one.got, two.kept, two.got, chain)
        self.start()


class SmallFlow:
    def __init__(self, kept, sent):
        self.kept, self.sent = kept, sent
        self.todo = order_of("x")
        self.done = False
        self.got = swap(self.sent, *self.todo[0])

    def step(self, chain):
        self.todo.pop(0)
        self.done = not self.todo
        if not self.done and self.todo[0][0] == "row":
            self.kept, self.sent = split(self.kept, self.got, chain)
        else:
            self.kept = self.sent = plus(self.kept, self.got, chain)
        if not self.done:
            self.got = swap(self.sent, *self.todo[0])


class Flows:
    def __init__(self, plan):
        self.plan = plan
        self.live = {}
        self.chain = Chain()
        self.rank = lax.axis_index("row").reshape(1)

    def begin(self, name, parts, order, last=None):
        self.live[name] = Flow(*parts, order, last)

    def wait(self, *names):
        self.chain.tokens += [self.live[name].got for name in names]

    def pair(self, name, one, two, last):
        one, two = self.live.pop(one), self.live.pop(two)
        self.live[name] = Pair(one, two, last, self.chain)

    def pump(self, point):
        for name in self.plan[point]:
            self.live[name].step(self.chain)

    def drain(self):
        while not all(flow.done for flow in self.live.values()):
            for flow in self.live.values():
                if not flow.done:
                    flow.step(self.chain)


def order_of(first):
    row = [("row", s) for s in steps_of("row")]
    img = [("img", s) for s in steps_of("img")]
    if first == "y":
        return row[:1] + img[:1] + row[1:] + img[1:]
    if first == "z":
        return row[:1] + img[1:] + row[1:] + img[:1]
    return row + img


PLAN = {
    "grad": ("down",),
    "mlp": ("up",),
    "att": ("down",),
    "patch": ("up",),
    "qkv": ("patch", "qkv"),
    "back2": ("mlp", "qkv"),
    "back3": ("patch", "mlp"),
    "end0": ("mlp", "qkv", "patch"),
    "end1": ("patch", "mlp", "qkv", "small"),
    "end2": ("patch", "qkv", "small"),
    "end3": ("patch", "qkv", "mlp", "small"),
    "end4": ("patch", "qkv", "small"),
    "end5": ("small", "qkv", "patch"),
}


def exchange(parts):
    return [parts[0]] + [swap(parts[k], "row", k) for k in range(1, len(parts))]


def per_device(stem_input, group, *rest):
    params, cot = rest[:-1], rest[-1]
    images, row_count, col_count, c0 = stem_input.shape
    ranks = lax.axis_size("row")
    assert images == ranks
    flows = Flows(PLAN)
    rank = flows.rank
    front = flows.chain
    parts = pack(rank, stem_input, front)
    made = prep(rank, group, *rest[:6], cot, front)
    parts = exchange(parts)
    made, cots = made[:10], exchange(made[10:])
    block_out, input_grad, small = per_image(parts, cots, made, params, flows)
    block_local = block_out
    block_out = block_out.reshape(images, -1, block_out.shape[-1])
    block_out = lax.all_to_all(block_out, "row", 0, 0, tiled=True)
    came = exchange(input_grad)
    flows.pump("end0")
    ig = unpack(rank, came, flows.chain)
    flows.live["small"] = SmallFlow(*small)
    for point in ("end1", "end2", "end3", "end4", "end5"):
        flows.pump(point)
    flows.drain()
    small = deal(
        flows.live["small"].kept[0], c0 // ranks, c0, rest[2].shape[1],
        rest[4].shape[0] // ranks, rest[6].shape[1] // ranks, rest[15].shape[0] // ranks,
    )
    qkv, out = flows.live["qkv"].kept
    down, up = flows.live["mlp"].kept
    vecs = [v[0] for v in small[4:]]
    shares = [small[0], small[1].transpose(1, 0, 2), small[2], small[3], vecs[0], vecs[1]]
    shares += [flows.live["patch"].kept, vecs[2], vecs[3], vecs[4]]
    shares += [qkv, out, vecs[5], vecs[6]]
    shares += [up, vecs[8], down, vecs[7]]
    return (block_out, ig) + tuple(shares)


def solution(mesh):
    rep = P()
    in_specs = (P("img", "row", None, None), P("img")) + (rep,) * 18 + (P("img", "row", None),)
    dims = (2, 3, 2, 2, 1, 1, 2, 1, 1, 1, 2, 2, 1, 1, 2, 1, 2, 1)
    out_specs = (P("img", "row", None), P("img", "row", None, None)) + tuple(
        P("row", *([None] * (n - 1))) for n in dims
    )
    return jax.shard_map(
        per_device, mesh=mesh, in_specs=in_specs, out_specs=out_specs, check_vma=False
    )
```

```python
import jax
import jax.numpy as jnp
from jax import lax
from jax.experimental import pallas as pl
from jax.experimental.pallas import tpu as pltpu
from jax.sharding import PartitionSpec as P

GROUPS = 32
HEADS = 12
HEAD_DIM = 64
PATCH = 4
FULL = 96
SMALL = 56
SIDE = FULL // PATCH
TOK = SIDE * SIDE
f32 = jnp.float32
bf16 = jnp.bfloat16


def mm(a, b):
    return lax.dot_general(a, b, (((1,), (0,)), ((), ())), preferred_element_type=f32)


def mm_nt(a, b):
    return lax.dot_general(a, b, (((1,), (1,)), ((), ())), preferred_element_type=f32)


def mm_tn(a, b):
    return lax.dot_general(a, b, (((0,), (0,)), ((), ())), preferred_element_type=f32)


def gelu_both(z):
    cdf = 0.5 + 0.5 * lax.erf(z * 0.7071067811865476)
    bell = jnp.exp(-0.5 * z * z)
    return z * cdf, cdf + z * bell * 0.3989422804014327


SRCS = (0, 1, 2, 3, -1, 4)
VMEM = pl.BlockSpec(memory_space=pltpu.VMEM)
SMEM = pl.BlockSpec(memory_space=pltpu.SMEM)


ANY = pl.BlockSpec(memory_space=pl.ANY)
TIMES = {
    "mlp_out": 4,
    "attend": 10, "attend_back": 15, "stem_front": 11, "stem_last": 11, "stem_back1": 13, "stem_back2": 12,
    "stem_back3": 10, "stem_back4": 8, "wgrad_rows": 6, "wgrad_qkv": 6, "mlp_back": 18,
    "qkv_back": 5, "unpack": 4, "pack": 2, "prep": 4,
}


def cost(name):
    flops = int(TIMES.get(name, 1) * 0.3 * 1.1e9)
    return pl.CostEstimate(flops=flops, bytes_accessed=flops // 1000, transcendentals=0)


class Chain:
    def __init__(self):
        self.tokens = []


def launch(kernel, chain=None, in_specs=None, grid_spec=None, out_specs=None, out_shape=None, **options):
    deps = chain.tokens if chain else []
    extra = [ANY] * len(deps)
    single = not isinstance(out_shape, (list, tuple))
    if single:
        out_shape = [out_shape]
    if grid_spec:
        out_specs = grid_spec["out_specs"]
    if not isinstance(out_specs, (list, tuple)):
        out_specs = [out_specs]
    outs = len(out_shape)
    if options.pop("hbm", False):
        out_shape = [pltpu.HBM(o.shape, o.dtype) for o in out_shape]
    count = len(in_specs if in_specs else grid_spec["in_specs"])
    count += grid_spec["num_scalar_prefetch"] if grid_spec else 0
    out_shape, out_specs = list(out_shape), list(out_specs)
    if chain:
        out_shape = out_shape + [jax.ShapeDtypeStruct((8, 128), f32)]
        out_specs = out_specs + [pl.BlockSpec((8, 128), lambda *_: (0, 0))]
    if grid_spec:
        spec = dict(grid_spec, in_specs=grid_spec["in_specs"] + extra, out_specs=out_specs)
        options["grid_spec"] = pltpu.PrefetchScalarGridSpec(**spec)
    else:
        options["in_specs"], options["out_specs"] = in_specs + extra, out_specs

    def body(*refs):
        at = count + len(deps) + outs
        if chain:
            refs[at][...] = jnp.zeros((8, 128), f32)
        return kernel(*refs[:count], *refs[count + len(deps) : at], *refs[at + (1 if chain else 0) :])

    run = pl.pallas_call(body, out_shape=out_shape, cost_estimate=cost(options["name"]), **options)

    def call(*operands):
        out = run(*operands, *deps)
        if chain:
            chain.tokens = [out[-1]]
            out = out[:-1]
        return out[0] if single else out

    return call


MID = pltpu.CompilerParams(vmem_limit_bytes=24 * 1024 * 1024)
BIG = pltpu.CompilerParams(vmem_limit_bytes=56 * 1024 * 1024)


def whole(shape):
    return pl.BlockSpec(shape, lambda i: (0,) * len(shape))


def slab(shape):
    return pl.BlockSpec((1,) + tuple(shape[1:]), lambda i: (i,) + (0,) * (len(shape) - 1))


def exact(row, mat):
    return jnp.dot(row, mat, precision=lax.Precision.HIGHEST, preferred_element_type=f32)


def fold(row):
    n = row.shape[1] // PATCH
    return sum(row[:, j * n : (j + 1) * n] for j in range(PATCH))


def tile4(row):
    return jnp.concatenate([row] * PATCH, axis=1)


def tiled(keep, lanes):
    return jnp.concatenate([keep] * (lanes // keep.shape[1]), axis=1)


def back_coefs(sums, gain, inv, gmat, wide):
    if wide:
        pair = jnp.concatenate([fold(r * gain) for r in sums] + [jnp.zeros((6, 256), f32)], axis=0)
        pair = exact(pair, gmat)
        return tile4(pair[0:1]) * inv, tile4(pair[1:2]) * inv
    pair = jnp.concatenate([r * gain for r in sums] + [jnp.zeros((6, 256), f32)], axis=0)
    pair = exact(pair, gmat)
    return pair[0:1] * inv, pair[1:2] * inv


def add_to(ref, value, first):
    @pl.when(first)
    def _():
        ref[...] = value

    @pl.when(jnp.logical_not(first))
    def _():
        ref[...] += value


def colsum(v):
    return jnp.sum(v, axis=0, keepdims=True)


def stem_back1_kernel(
    gh_ref, pw_ref, d3_ref, p2_ref, x_ref, w_ref, st_ref, vec_ref, g256_ref,
    gz_ref, out_ref, skip_ref, acc_ref, sum_ref,
):
    i = pl.program_id(0)
    gz = mm_nt(gh_ref[...], pw_ref[0]) * d3_ref[0].astype(f32)
    n = mm(p2_ref[0], w_ref[...]) * st_ref[0:1] + st_ref[1:2]
    low = gz.astype(bf16)
    gz_ref[0] = low
    add_to(sum_ref, jnp.concatenate([colsum(gz), colsum(gz * n)] + [jnp.zeros((6, gz.shape[1]), f32)], axis=0), i == 0)
    add_to(acc_ref, mm_tn(x_ref[0], low), i == 0)

    @pl.when(i == PATCH - 1)
    def _():
        c1, c2 = sum_ref[0:1], sum_ref[1:2]
        s1, s2 = back_coefs((c1, c2), vec_ref[4:5], vec_ref[7:8], g256_ref[...], True)
        zero = jnp.zeros_like(c1)
        bias, gain = tile4(fold(c1)), tile4(fold(c2))
        out_ref[...] = jnp.concatenate([s1, s2, bias, gain] + [zero] * 4, axis=0)
        c, n = skip_ref.shape
        skip_ref[...] = sum(
            acc_ref[j * c : (j + 1) * c, j * n : (j + 1) * n] for j in range(PATCH)
        )


def stem_back1(g_h, pw, d3, p2, x, w_out, stat, vec, g256, chain=None):
    lanes = d3.shape[2]
    c = p2.shape[2] // PATCH
    s = jax.ShapeDtypeStruct
    return launch(
        stem_back1_kernel,
        grid=(PATCH,),
        in_specs=[
            whole(g_h.shape), slab(pw.shape), slab(d3.shape), slab(p2.shape), slab(x.shape),
            whole(w_out.shape), whole(stat.shape), whole(vec.shape), whole(g256.shape),
        ],
        out_specs=[slab(d3.shape), whole((8, lanes)), whole((c, lanes // PATCH))],
        out_shape=[s(d3.shape, bf16), s((8, lanes), f32), s((c, lanes // PATCH), f32)],
        scratch_shapes=[pltpu.VMEM((PATCH * c, lanes), f32), pltpu.VMEM((8, lanes), f32)],
        compiler_params=BIG,
        chain=chain,
        name="stem_back1",
    )(g_h, pw, d3, p2, x, w_out, stat, vec, g256)


def stem_back2_kernel(
    gz_ref, p2_ref, d2_ref, n2_ref, w_ref, st_ref, co_ref, vec_ref, g64_ref, keep_ref,
    g2_ref, out_ref, grad_ref, acc_ref, sum_ref,
):
    i = pl.program_id(0)
    lanes = gz_ref.shape[2]
    keep = tiled(keep_ref[...], lanes)
    rstd, gain, s1, s2 = st_ref[0:1], vec_ref[4:5], co_ref[0:1], co_ref[1:2]
    n = mm(p2_ref[0], w_ref[...]) * rstd + st_ref[1:2]
    gv = (rstd * (gz_ref[0].astype(f32) * gain - s1 - n * s2) * keep).astype(bf16)
    add_to(acc_ref, mm_tn(p2_ref[0], gv), i == 0)
    g2 = mm_nt(gv, w_ref[...]) * d2_ref[0].astype(f32)
    g2_ref[0] = g2.astype(bf16)
    add_to(sum_ref, jnp.concatenate([colsum(g2), colsum(g2 * n2_ref[0].astype(f32))] + [jnp.zeros((6, g2.shape[1]), f32)], axis=0), i == 0)

    @pl.when(i == PATCH - 1)
    def _():
        narrow = g2_ref.shape[2]
        c1, c2 = sum_ref[0:1], sum_ref[1:2]
        s1, s2 = back_coefs((c1, c2), vec_ref[2:3, :narrow], vec_ref[6:7, :narrow], g64_ref[...], False)
        out_ref[...] = jnp.concatenate([s1, s2, c1, c2] + [jnp.zeros_like(c1)] * 4, axis=0)
        c, n = grad_ref.shape
        grad_ref[...] = sum(
            acc_ref[j * c : (j + 1) * c, j * n : (j + 1) * n] for j in range(PATCH)
        )


def stem_back2(gz, p2, d2, n2, w_out, stat, coef, vec, g64, keep, chain=None):
    lanes = gz.shape[2]
    narrow = p2.shape[2]
    c = narrow // PATCH
    s = jax.ShapeDtypeStruct
    return launch(
        stem_back2_kernel,
        grid=(PATCH,),
        in_specs=[
            slab(gz.shape), slab(p2.shape), slab(d2.shape), slab(n2.shape), whole(w_out.shape),
            whole(stat.shape), whole(coef.shape), whole(vec.shape), whole(g64.shape), whole(keep.shape),
        ],
        out_specs=[slab(p2.shape), whole((8, narrow)), whole((c, lanes // PATCH))],
        out_shape=[s(p2.shape, bf16), s((8, narrow), f32), s((c, lanes // PATCH), f32)],
        scratch_shapes=[pltpu.VMEM((narrow, lanes), f32), pltpu.VMEM((8, narrow), f32)],
        compiler_params=BIG,
        chain=chain,
        name="stem_back2",
    )(gz, p2, d2, n2, w_out, stat, coef, vec, g64, keep)


def edges(v, edge):
    c = v.shape[1] // PATCH
    toks = v.shape[0]
    left = pltpu.roll(v[:, 3 * c :], 1, 0)
    right = pltpu.roll(v[:, :c], toks - 1, 0)
    return jnp.concatenate([left, right], axis=1) * edge


def fill_wide(wide_ref, i, v, edge):
    lanes = v.shape[1]
    v = jnp.concatenate([v, edges(v, edge)], axis=1)
    wide_ref[i + 1] = v.astype(bf16)
    gap = jnp.zeros((SIDE, v.shape[1]), f32)
    if i == PATCH - 1:
        wide_ref[0] = jnp.concatenate([gap, v[:-SIDE]], axis=0).astype(bf16)
    if i == 0:
        wide_ref[PATCH + 1] = jnp.concatenate([v[SIDE:], gap], axis=0).astype(bf16)


def stem_back3_kernel(
    g2_ref, n2_ref, p1_ref, b_ref, d1_ref, x_ref, w_ref, st1_ref, st2_ref, co_ref, vec_ref, g64_ref,
    keep_ref, edge_ref, g1_ref, out_ref, grad_ref, wide_ref,
):
    narrow = g2_ref.shape[2]
    c = narrow // PATCH
    keep = tiled(keep_ref[...], narrow)
    rstd, gain, s1, s2 = st2_ref[0:1], vec_ref[2:3, :narrow], co_ref[0:1], co_ref[1:2]
    for i in range(PATCH):
        gv = rstd * (g2_ref[i].astype(f32) * gain - s1 - n2_ref[i].astype(f32) * s2) * keep
        fill_wide(wide_ref, i, gv, edge_ref[...])
    for di in range(3):
        total = 0.0
        for i in range(PATCH):
            total = total + mm_tn(p1_ref[i + di], wide_ref[i + 1, :, :narrow])
        for dj in range(3):
            grad_ref[3 * di + dj] = sum(
                total[k * c : (k + 1) * c, j * c : (j + 1) * c]
                for j in range(PATCH)
                for k in (SRCS.index(j + dj - 1),)
            )
    c1 = c2 = 0.0
    for i in range(PATCH):
        g1 = sum(mm_nt(wide_ref[i + di], b_ref[di]) for di in range(3)) * d1_ref[i].astype(f32)
        g1_ref[i] = g1.astype(bf16)
        n = mm(x_ref[i], w_ref[...]) * st1_ref[0:1] + st1_ref[1:2]
        c1 = c1 + colsum(g1)
        c2 = c2 + colsum(g1 * n)
    s1, s2 = back_coefs((c1, c2), vec_ref[0:1, :narrow], vec_ref[6:7, :narrow], g64_ref[...], False)
    out_ref[...] = jnp.concatenate([s1, s2, c1, c2] + [jnp.zeros_like(c1)] * 4, axis=0)


def stem_back3(g2, n2, p1_wide, b_bwd, d1, x, w_in, stat1, stat2, coef, vec, g64, keep, edge, chain=None):
    narrow = g2.shape[2]
    c = narrow // PATCH
    s = jax.ShapeDtypeStruct
    vm = VMEM
    return launch(
        stem_back3_kernel,
        in_specs=[vm] * 14,
        out_specs=[vm] * 3,
        out_shape=[s(g2.shape, bf16), s((8, narrow), f32), s((9, c, c), f32)],
        scratch_shapes=[pltpu.VMEM((PATCH + 2, TOK, 6 * c), bf16)],
        compiler_params=BIG,
        chain=chain,
        name="stem_back3",
    )(g2, n2, p1_wide, b_bwd, d1, x, w_in, stat1, stat2, coef, vec, g64, keep, edge)


def stem_back4_kernel(
    rank_ref, g1_ref, x_ref, gz_ref, win_ref, wskip_ref, st_ref, co_ref, vec_ref, keep_ref,
    o0_ref, o1_ref, o2_ref, o3_ref, grad_ref, acc_ref, ig_ref,
):
    i = pl.program_id(0)
    narrow = g1_ref.shape[2]
    keep = tiled(keep_ref[...], narrow)
    rstd, gain, s1, s2 = st_ref[0:1], vec_ref[0:1, :narrow], co_ref[0:1], co_ref[1:2]
    n = mm(x_ref[0], win_ref[...]) * rstd + st_ref[1:2]
    gv = (rstd * (g1_ref[0].astype(f32) * gain - s1 - n * s2) * keep).astype(bf16)
    add_to(acc_ref, mm_tn(x_ref[0], gv), i == 0)
    ig_ref[...] = (mm_nt(gv, win_ref[...]) + mm_nt(gz_ref[0], wskip_ref[...])) * keep
    for k, o_ref in enumerate((o0_ref, o1_ref, o2_ref, o3_ref)):
        toks = o_ref.shape[1]
        at = pl.ds(pl.multiple_of((rank_ref[0] ^ k) * toks, 16), toks)
        o_ref[0] = ig_ref[at, :].astype(bf16)

    @pl.when(i == PATCH - 1)
    def _():
        c = grad_ref.shape[0]
        grad_ref[...] = sum(
            acc_ref[j * c : (j + 1) * c, j * c : (j + 1) * c] for j in range(PATCH)
        )


def stem_back4(rank, g1, x, gz, w_in, w_skip, stat, coef, vec, keep, ranks, chain=None):
    narrow = g1.shape[2]
    c = narrow // PATCH
    part = jax.ShapeDtypeStruct((PATCH, TOK // ranks, narrow), bf16)
    return launch(
        stem_back4_kernel,
        grid=(PATCH,),
        in_specs=[
            SMEM, slab(g1.shape), slab(x.shape), slab(gz.shape), whole(w_in.shape), whole(w_skip.shape),
            whole(stat.shape), whole(coef.shape), whole(vec.shape), whole(keep.shape),
        ],
        out_specs=[slab(part.shape)] * ranks + [whole((c, c))],
        out_shape=[part] * ranks + [jax.ShapeDtypeStruct((c, c), f32)],
        scratch_shapes=[pltpu.VMEM((narrow, narrow), f32), pltpu.VMEM((TOK, narrow), f32)],
        compiler_params=BIG,
        chain=chain,
        name="stem_back4",
    )(rank, g1, x, gz, w_in, w_skip, stat, coef, vec, keep)


def scale_shift(c1, c2, gain, bias, inv, gmat, wide):
    pair = jnp.concatenate([c1, c2], axis=0)
    if wide:
        pair = fold(pair)
    pair = exact(jnp.concatenate([pair, jnp.zeros((6, pair.shape[1]), f32)], axis=0), gmat)
    if wide:
        pair = tile4(pair)
    mean, square = pair[0:1] * inv, pair[1:2] * inv
    rstd = lax.rsqrt(square - mean * mean + 1e-05)
    shift = -mean * rstd
    return rstd, shift, rstd * gain, bias + shift * gain


def stem_front_kernel(
    rank_ref, x0_ref, x1_ref, x2_ref, x3_ref,
    win_ref, bf_ref, wout_ref, vec_ref, g64_ref, g256_ref, keep_ref, edge_ref,
    x_ref, wide_ref, d1_ref, p2_ref, d2_ref, n2_ref, st1_ref, st2_ref, st3_ref, v_ref,
):
    narrow = x_ref.shape[2]
    for k, part_ref in enumerate((x0_ref, x1_ref, x2_ref, x3_ref)):
        toks = part_ref.shape[1]
        at = pl.ds(pl.multiple_of((rank_ref[0] ^ k) * toks, 16), toks)
        mask = tiled(keep_ref[at, :], narrow)
        for i in range(PATCH):
            x_ref[i, at, :] = (part_ref[i].astype(f32) * mask).astype(bf16)
    keep = tiled(keep_ref[...], narrow)
    inv = vec_ref[6:7, :narrow]
    c1 = c2 = 0.0
    for i in range(PATCH):
        v = mm(x_ref[i], win_ref[...])
        v_ref[i] = v
        c1, c2 = c1 + colsum(v), c2 + colsum(v * v)
    rstd, shift, a, b = scale_shift(c1, c2, vec_ref[0:1, :narrow], vec_ref[1:2, :narrow], inv, g64_ref[...], False)
    st1_ref[...] = jnp.concatenate([rstd, shift], axis=0)
    for i in range(PATCH):
        act, slope = gelu_both(v_ref[i] * a + b)
        d1_ref[i] = (slope * keep).astype(bf16)
        fill_wide(wide_ref, i, act * keep, edge_ref[...])
    c1 = c2 = 0.0
    for i in range(PATCH):
        v = sum(mm(wide_ref[i + di], bf_ref[di]) for di in range(3))
        v_ref[i] = v
        v = v * keep
        c1, c2 = c1 + colsum(v), c2 + colsum(v * v)
    rstd, shift, a, b = scale_shift(c1, c2, vec_ref[2:3, :narrow], vec_ref[3:4, :narrow], inv, g64_ref[...], False)
    st2_ref[...] = jnp.concatenate([rstd, shift], axis=0)
    c1 = c2 = 0.0
    for i in range(PATCH):
        v = v_ref[i]
        act, slope = gelu_both(v * a + b)
        d2_ref[i] = (slope * keep).astype(bf16)
        n2_ref[i] = (v * rstd + shift).astype(bf16)
        low = (act * keep).astype(bf16)
        p2_ref[i] = low
        v = mm(low, wout_ref[...])
        c1, c2 = c1 + colsum(v), c2 + colsum(v * v)
    st3_ref[...] = jnp.concatenate(
        scale_shift(c1, c2, vec_ref[4:5], vec_ref[5:6], vec_ref[7:8], g256_ref[...], True), axis=0
    )


def stem_front(rank, parts, w_in, b_fwd, w_out, vec, g64, g256, keep, edge, chain=None):
    narrow = parts[0].shape[2]
    s = jax.ShapeDtypeStruct
    vm = pl.BlockSpec(memory_space=pltpu.VMEM)
    low = s((PATCH, TOK, narrow), bf16)
    return launch(
        stem_front_kernel,
        in_specs=[SMEM] + [vm] * 12,
        out_specs=[vm] * 9,
        out_shape=[
            low, s((PATCH + 2, TOK, narrow * 3 // 2), bf16), low, low, low, low,
            s((2, narrow), f32), s((2, narrow), f32), s((4, w_out.shape[1]), f32),
        ],
        scratch_shapes=[pltpu.VMEM((PATCH, TOK, narrow), f32)],
        compiler_params=BIG,
        chain=chain,
        name="stem_front",
    )(rank, *parts, w_in, b_fwd, w_out, vec, g64, g256, keep, edge)


def stem_last_kernel(p2_ref, x_ref, wout_ref, wskip_ref, st_ref, keep_ref, stem_ref, d3_ref):
    keep = tiled(keep_ref[...], wout_ref.shape[1])
    z = mm(p2_ref[0], wout_ref[...]) * st_ref[2:3] + st_ref[3:4] + mm(x_ref[0], wskip_ref[...])
    act, slope = gelu_both(z)
    stem_ref[0] = (act * keep).astype(bf16)
    d3_ref[0] = (slope * keep).astype(bf16)


def stem_last(p2, x, w_out, w_skip, stat, keep, chain=None):
    lanes = w_out.shape[1]
    shape = p2.shape[:2] + (lanes,)
    o = jax.ShapeDtypeStruct(shape, bf16)
    return launch(
        stem_last_kernel,
        grid=(PATCH,),
        in_specs=[slab(p2.shape), slab(x.shape), whole(w_out.shape), whole(w_skip.shape), whole(stat.shape), whole(keep.shape)],
        out_specs=[slab(shape)] * 2,
        out_shape=[o, o],
        compiler_params=BIG,
        chain=chain,
        name="stem_last",
    )(p2, x, w_out, w_skip, stat, keep)


def pack_kernel(rank_ref, x_ref, *refs):
    outs, wide_ref = refs[:-1], refs[-1]
    rows, chans, cols = x_ref.shape[1:]
    for r in range(rows):
        wide_ref[r * cols : (r + 1) * cols, :] = x_ref[0, r].astype(f32).T
    for k, o_ref in enumerate(outs):

        @pl.when(pl.program_id(0) == k)
        def _():
            for i in range(PATCH):
                parts = []
                for j in range(PATCH):
                    parts.append(
                        jnp.concatenate(
                            [
                                wide_ref[pl.ds(r * cols + j, SIDE, stride=PATCH), :]
                                for r in range(i, rows, PATCH)
                            ],
                            axis=0,
                        )
                    )
                o_ref[i] = jnp.concatenate(parts, axis=1).astype(o_ref.dtype)


def pack(rank, x, chain):
    images, rows, cols, chans = x.shape
    x = x.transpose(0, 1, 3, 2)
    shape = (PATCH, rows // PATCH * SIDE, PATCH * chans)
    return launch(
        pack_kernel,
        grid_spec=dict(
            num_scalar_prefetch=1,
            grid=(images,),
            in_specs=[pl.BlockSpec((1, rows, chans, cols), lambda b, r: (b ^ r[0], 0, 0, 0))],
            out_specs=[pl.BlockSpec(shape, lambda b, r: (0, 0, 0))] * images,
            scratch_shapes=[pltpu.VMEM((rows * cols, chans), f32)],
        ),
        out_shape=[jax.ShapeDtypeStruct(shape, x.dtype)] * images,
        compiler_params=MID,
        chain=chain,
        name="pack",
    )(rank, x)


def unpack_kernel(rank_ref, *refs):
    ins, o_ref, row_ref = refs[:-2], refs[-2], refs[-1]
    chans = o_ref.shape[2]
    for k, x_ref in enumerate(ins):

        @pl.when(pl.program_id(0) == k)
        def _():
            for i in range(PATCH):
                v = x_ref[i].astype(f32)
                for p in range(v.shape[0] // SIDE):
                    for j in range(PATCH):
                        row_ref[PATCH * p + i, pl.ds(j, SIDE, stride=PATCH), :] = v[
                            p * SIDE : (p + 1) * SIDE, j * chans : (j + 1) * chans
                        ]

    for r in range(o_ref.shape[1]):
        o_ref[0, r] = row_ref[r].T


def unpack(rank, parts, chain=None):
    images = len(parts)
    _, toks, lanes = parts[0].shape
    shape = (images, toks // SIDE * PATCH, lanes // PATCH, SIDE * PATCH)
    return launch(
        unpack_kernel,
        grid_spec=dict(
            num_scalar_prefetch=1,
            grid=(images,),
            in_specs=[pl.BlockSpec(parts[0].shape, lambda b, r: (0, 0, 0))] * images,
            out_specs=pl.BlockSpec((1,) + shape[1:], lambda b, r: (b ^ r[0], 0, 0, 0)),
            scratch_shapes=[pltpu.VMEM((shape[1], shape[3], shape[2]), f32)],
        ),
        out_shape=jax.ShapeDtypeStruct(shape, f32),
        compiler_params=MID,
        chain=chain,
        name="unpack",
    )(rank, *parts).transpose(0, 1, 3, 2)


def prep_kernel(
    rank_ref, group_ref, in_ref, mid_ref, out_ref, skip_ref, gain_ref, bias_ref, cot_ref,
    w_in, w_out, w_skip, b_fwd, b_bwd, g64, g256, vec, keep, edge, *cots,
):
    for k, ref in enumerate(cots):
        ref[...] = cot_ref[rank_ref[0] ^ k]
    def spread(dst, src):
        dst[...] = jnp.zeros_like(dst)
        c, n = src.shape
        for j in range(PATCH):
            dst[j * c : (j + 1) * c, j * n : (j + 1) * n] = src[...]

    spread(w_in, in_ref)
    spread(w_out, out_ref)
    spread(w_skip, skip_ref)
    b_fwd[...] = jnp.zeros_like(b_fwd)
    b_bwd[...] = jnp.zeros_like(b_bwd)
    c = mid_ref.shape[1]
    for di in range(3):
        for k, src in enumerate(SRCS):
            for j in range(PATCH):
                if abs(src - j) <= 1:
                    dj = src - j + 1
                    b_fwd[di, k * c : (k + 1) * c, j * c : (j + 1) * c] = mid_ref[3 * di + dj]
                    b_bwd[di, j * c : (j + 1) * c, k * c : (k + 1) * c] = mid_ref[8 - 3 * di - dj]
    for ref, chans in ((g64, c), (g256, gain_ref.shape[1] - 2 * c)):
        per = chans // GROUPS
        row = (lax.broadcasted_iota(jnp.int32, ref.shape, 0) & (chans - 1)) // per
        col = (lax.broadcasted_iota(jnp.int32, ref.shape, 1) & (chans - 1)) // per
        ref[...] = jnp.where(row == col, 1.0, 0.0)
    vec[...] = jnp.zeros_like(vec)
    for at, (ref, lo, hi) in enumerate(
        (r, lo, hi)
        for lo, hi in ((0, c), (c, 2 * c), (2 * c, gain_ref.shape[1]))
        for r in (gain_ref, bias_ref)
    ):
        part = jnp.concatenate([ref[:, lo:hi]] * PATCH, axis=1)
        vec[at : at + 1, : part.shape[1]] = part
    limit = jnp.where(group_ref[rank_ref[0]] == 1, FULL // PATCH, SMALL // PATCH)
    inverse = 1.0 / (jnp.full((1, vec.shape[1]), PATCH * PATCH, f32) * (limit * limit).astype(f32))
    vec[6:7] = inverse * (GROUPS / c)
    vec[7:8] = inverse * (GROUPS / (gain_ref.shape[1] - 2 * c))
    t = lax.broadcasted_iota(jnp.int32, keep.shape, 0)
    up = ((t.astype(f32) + 0.5) * (1.0 / SIDE)).astype(jnp.int32)
    t = t - SIDE * up
    keep[...] = jnp.where((up < limit) & (t < limit), 1.0, 0.0)
    left = lax.broadcasted_iota(jnp.int32, edge.shape, 1) < c
    edge[...] = jnp.where(t != jnp.where(left, 0, SIDE - 1), 1.0, 0.0)


def prep(rank, group, conv_in, conv_mid, conv_out, conv_skip, norm_gain, norm_bias, cot, chain=None):
    c, n = conv_out.shape
    s = jax.ShapeDtypeStruct
    shapes = [
        s((PATCH * c, PATCH * c), bf16),
        s((PATCH * c, PATCH * n), bf16),
        s((PATCH * c, PATCH * n), bf16),
        s((3, 6 * c, PATCH * c), bf16),
        s((3, PATCH * c, 6 * c), bf16),
        s((PATCH * c, PATCH * c), f32),
        s((PATCH * c, PATCH * c), f32),
        s((8, PATCH * n), f32),
        s((TOK, 128), f32),
        s((TOK, 2 * c), f32),
    ] + [s(cot.shape[1:], bf16)] * cot.shape[0]
    return launch(
        prep_kernel,
        in_specs=[SMEM, SMEM] + [VMEM] * 7,
        out_specs=[VMEM] * len(shapes),
        out_shape=shapes,
        chain=chain,
        name="prep",
    )(
        rank.reshape(1),
        group,
        conv_in,
        conv_mid.transpose(1, 0, 2),
        conv_out,
        conv_skip,
        norm_gain[None],
        norm_bias[None],
        cot,
    )


def ln_stats(h):
    mean = jnp.mean(h, axis=-1, keepdims=True)
    cen = h - mean
    rstd = lax.rsqrt(jnp.mean(cen * cen, axis=-1, keepdims=True) + 1e-05)
    return cen * rstd, rstd


def ln_back(gy, n, rstd, gain):
    gn = gy * gain
    gh = rstd * (
        gn - jnp.mean(gn, axis=-1, keepdims=True) - n * jnp.mean(gn * n, axis=-1, keepdims=True)
    )
    return gh, jnp.sum(gy * n, axis=0), jnp.sum(gy, axis=0)


def slot_of(q, rank):
    rel = q ^ rank
    return rel & 1, rel >> 1


def store_slot(keep_ref, send_ref, core, at, value):
    @pl.when(core == 0)
    def _():
        keep_ref[at] = value

    @pl.when(core == 1)
    def _():
        send_ref[at] = value


def store_quarters(rank_ref, total, keep_ref, send_ref):
    total = total.astype(bf16)
    rows = keep_ref.shape[-2]
    for q in range(total.shape[0] // rows):
        core, over = slot_of(q, rank_ref[0])
        store_slot(keep_ref, send_ref, core, (0, over, 0), total[q * rows : (q + 1) * rows])


def wgrad_qkv_kernel(rank_ref, a_ref, g_ref, a2_ref, g2_ref, keep_ref, send_ref):
    last = pl.program_id(0) == pl.num_programs(0) - 1

    @pl.when(jnp.logical_not(last))
    def _():
        store_quarters(rank_ref, mm_tn(a_ref[...], g_ref[...]), keep_ref, send_ref)

    @pl.when(last)
    def _():
        store_quarters(rank_ref, mm_tn(a2_ref[...], g2_ref[...]), keep_ref, send_ref)


def wgrad_qkv(rank, a, g, a2, g2, chain=None):
    toks, k = a.shape
    rows = k // 4
    o = jax.ShapeDtypeStruct((2, 2, 2, rows, k), bf16)
    spec = pl.BlockSpec((1, 2, 1, rows, k), lambda b: (b // 2, 0, b % 2, 0, 0))
    return launch(
        wgrad_qkv_kernel,
        grid=(4,),
        in_specs=[
            SMEM, whole(a.shape), pl.BlockSpec((toks, k), lambda b: (0, jnp.minimum(b, 2))),
            whole(a.shape), whole(a.shape),
        ],
        out_specs=[spec, spec],
        out_shape=[o, o],
        compiler_params=MID,
        chain=chain,
        name="wgrad_qkv",
    )(rank, a, g, a2, g2)


def wgrad_rows_kernel(rank_ref, a_ref, g_ref, keep_ref, send_ref):
    total = mm_tn(a_ref[...], g_ref[...]).astype(bf16)
    step = pl.program_id(0)
    rows = total.shape[0] // (1 if len(keep_ref.shape) == 2 else keep_ref.shape[0])

    def put(ref):
        if len(ref.shape) == 2:
            ref[...] = total
        else:
            for h in range(ref.shape[0]):
                ref[h] = total[h * rows : (h + 1) * rows]

    @pl.when(step < 2)
    def _():
        put(send_ref)

    @pl.when(step >= 2)
    def _():
        put(keep_ref)


def wgrad_rows(rank, a, g, outer, chain=None):
    toks, n = g.shape
    rows = a.shape[2] if a.ndim == 3 else a.shape[1] // 4

    def quarter(step, rank_ref):
        rel = (step % 2) * 2 + jnp.where(step < 2, 1, 0)
        return rel ^ rank_ref[0]

    if a.ndim == 3:
        a_spec = pl.BlockSpec((None, toks, rows), lambda s, r: (quarter(s, r), 0, 0))
    else:
        a_spec = pl.BlockSpec((toks, rows), lambda s, r: (0, quarter(s, r)))
    if outer > 1:
        shape = (outer, 2, rows // outer, n)
        block = (outer, None, rows // outer, n)
        specs = [
            pl.BlockSpec(block, lambda s, r: (0, jnp.maximum(s - 2, 0), 0, 0)),
            pl.BlockSpec(block, lambda s, r: (0, jnp.minimum(s, 1), 0, 0)),
        ]
    else:
        shape = (2, rows, n)
        specs = [
            pl.BlockSpec((None, rows, n), lambda s, r: (jnp.maximum(s - 2, 0), 0, 0)),
            pl.BlockSpec((None, rows, n), lambda s, r: (jnp.minimum(s, 1), 0, 0)),
        ]
    o = jax.ShapeDtypeStruct(shape, bf16)
    return launch(
        wgrad_rows_kernel,
        grid_spec=dict(
            num_scalar_prefetch=1,
            grid=(4,),
            in_specs=[a_spec, pl.BlockSpec((toks, n), lambda s, r: (0, 0))],
            out_specs=specs,
        ),
        out_shape=[o, o],
        compiler_params=MID,
        chain=chain,
        name="wgrad_rows",
    )(rank, a, g)


VECS = 6


def collect_kernel(rank_ref, in_ref, mid_ref, cout_ref, skip_ref, co1_ref, co2_ref, co3_ref, *refs):
    vecs, up_ref, (keep_ref, send_ref) = refs[:VECS], refs[VECS], refs[VECS + 1 :]
    c, lanes = cout_ref.shape
    part = c // 4
    norms = []
    for row in (3, 2):
        norms.append(
            jnp.concatenate(
                [fold(co1_ref[row : row + 1]), fold(co2_ref[row : row + 1]), co3_ref[row : row + 1, :lanes]],
                axis=1,
            )
        )

    def full(v):
        gap = lanes - v.shape[1]
        return jnp.concatenate([v, jnp.zeros((v.shape[0], gap), f32)], axis=1) if gap else v

    for q in range(4):
        rows = slice(q * part, (q + 1) * part)
        blocks = [cout_ref[rows], skip_ref[rows]]
        for di in range(3):
            blocks.append(full(jnp.concatenate([mid_ref[3 * di + dj, rows] for dj in range(3)], axis=1)))
        blocks.append(full(in_ref[rows]))

        def quarter(v):
            n = v.shape[1] // 4
            return v[:, q * n : (q + 1) * n]

        small = [full(quarter(v[...])) for v in vecs]
        up = quarter(up_ref[...])
        small += [up[:, k * lanes : (k + 1) * lanes] for k in range(up.shape[1] // lanes)]
        small += [full(quarter(v)) for v in norms]
        small.append(jnp.zeros((16 - len(small), lanes), f32))
        total = jnp.concatenate(blocks + small, axis=0)
        core, over = slot_of(q, rank_ref[0])
        store_slot(keep_ref, send_ref, core, over, total)


def collect(rank, g_in, g_mid, g_cout, g_skip, co1, co2, co3, vecs, up, chain=None):
    c, lanes = g_cout.shape
    rows = 6 * (c // 4) + 16
    o = jax.ShapeDtypeStruct((2, rows, lanes), f32)
    return launch(
        collect_kernel,
        in_specs=[SMEM] + [VMEM] * (8 + VECS),
        out_specs=[VMEM] * 2,
        out_shape=[o, o],
        compiler_params=MID,
        chain=chain,
        name="collect",
    )(rank, g_in, g_mid, g_cout, g_skip, co1, co2, co3, *vecs, up)


def deal_kernel(v_ref, in_ref, mid_ref, cout_ref, skip_ref, gain_ref, bias_ref, *refs):
    vecs, up_ref = refs[:VECS], refs[VECS]
    part, c = in_ref.shape
    lanes = v_ref.shape[1]
    cout_ref[...] = v_ref[:part]
    skip_ref[...] = v_ref[part : 2 * part]
    for di in range(3):
        for dj in range(3):
            mid_ref[3 * di + dj] = v_ref[(2 + di) * part : (3 + di) * part, dj * c : (dj + 1) * c]
    in_ref[...] = v_ref[5 * part : 6 * part, :c]
    at = 6 * part
    for ref in vecs:
        ref[...] = v_ref[at : at + 1, : ref.shape[1]]
        at += 1
    for k in range(up_ref.shape[1] // lanes):
        up_ref[:, k * lanes : (k + 1) * lanes] = v_ref[at : at + 1]
        at += 1
    gain_ref[...] = v_ref[at : at + 1, : gain_ref.shape[1]]
    bias_ref[...] = v_ref[at + 1 : at + 2, : bias_ref.shape[1]]


def deal(v, part, c, n, norms, width, hidden):
    s = jax.ShapeDtypeStruct
    shapes = [s((part, c), f32), s((9, part, c), f32), s((part, n), f32), s((part, n), f32)]
    shapes += [s((1, norms), f32)] * 2 + [s((1, width), f32)] * VECS + [s((1, hidden), f32)]
    return launch(
        deal_kernel,
        in_specs=[VMEM],
        out_specs=[VMEM] * len(shapes),
        out_shape=shapes,
        compiler_params=MID,
        name="deal",
    )(v)


def merge_kernel(bit_ref, a_ref, b_ref, c_ref, d_ref, keep_ref, send_ref):
    keep_ref[...] = (a_ref[...].astype(f32) + b_ref[...].astype(f32)).astype(bf16)
    send_ref[...] = (c_ref[...].astype(f32) + d_ref[...].astype(f32)).astype(bf16)


def merge(bit, kept, got, chain=None):
    rows, n = kept.shape
    half = rows // 2
    tiles = 2 if half >= 512 else 1
    block = (half // tiles, n)
    mine = pl.BlockSpec(block, lambda t, b: (b[0] * tiles + t, 0))
    other = pl.BlockSpec(block, lambda t, b: ((1 - b[0]) * tiles + t, 0))
    out = pl.BlockSpec(block, lambda t, b: (t, 0))
    o = jax.ShapeDtypeStruct((half, n), bf16)
    return launch(
        merge_kernel,
        grid_spec=dict(
            num_scalar_prefetch=1,
            grid=(tiles,),
            in_specs=[mine, mine, other, other],
            out_specs=[out, out],
        ),
        out_shape=[o, o],
        compiler_params=MID,
        chain=chain,
        name="merge",
    )(bit, kept, got, kept, got)


def plus_kernel(a_ref, b_ref, o_ref):
    o_ref[...] = (a_ref[...].astype(f32) + b_ref[...].astype(f32)).astype(o_ref.dtype)


def plus(a, b, chain=None):
    return launch(
        plus_kernel,
        in_specs=[VMEM] * 2,
        out_specs=VMEM,
        out_shape=jax.ShapeDtypeStruct(a.shape, a.dtype),
        compiler_params=MID,
        chain=chain,
        name="plus",
    )(a, b)


def gather_kernel(rank_ref, p0_ref, p1_ref, p2_ref, p3_ref, keep_ref, o_ref, sum_ref):
    total = 0.0
    for k, ref in enumerate((p0_ref, p1_ref, p2_ref, p3_ref)):
        toks, n = ref.shape
        at = pl.ds(pl.multiple_of((rank_ref[0] ^ k) * toks, 16), toks)
        v = ref[...].astype(f32) * tiled(keep_ref[at, :], n)
        total = total + colsum(v)
        o_ref[at, :] = v.astype(bf16)
    sum_ref[...] = total


def gather(rank, parts, keep, chain=None):
    toks, n = parts[0].shape
    return launch(
        gather_kernel,
        in_specs=[SMEM] + [VMEM] * 5,
        out_specs=[VMEM] * 2,
        out_shape=[jax.ShapeDtypeStruct((4 * toks, n), bf16), jax.ShapeDtypeStruct((1, n), f32)],
        compiler_params=MID,
        chain=chain,
        name="gather",
    )(rank, *parts, keep)


def split_kernel(a_ref, b_ref, keep_ref, send_ref):
    half = keep_ref.shape[0]
    keep_ref[...] = a_ref[:half] + b_ref[:half]
    send_ref[...] = a_ref[half:] + b_ref[half:]


def split(a, b, chain=None):
    o = jax.ShapeDtypeStruct((a.shape[0] // 2,) + a.shape[1:], a.dtype)
    return launch(
        split_kernel,
        in_specs=[VMEM] * 2,
        out_specs=[VMEM] * 2,
        out_shape=[o, o],
        compiler_params=MID,
        chain=chain,
        name="split",
    )(a, b)


def merge_two(bit, kept, got, kept2, got2, chain=None):
    def body(bit_ref, a_ref, b_ref, c_ref, d_ref, keep_ref, send_ref):
        def put(first_ref, second_ref):
            first_ref[...] = (a_ref[...].astype(f32) + b_ref[...].astype(f32)).astype(bf16)
            second_ref[...] = (c_ref[...].astype(f32) + d_ref[...].astype(f32)).astype(bf16)

        @pl.when(bit_ref[0] == 0)
        def _():
            put(keep_ref, send_ref)

        @pl.when(bit_ref[0] == 1)
        def _():
            put(send_ref, keep_ref)

    o = jax.ShapeDtypeStruct(kept.shape, bf16)
    return launch(
        body,
        in_specs=[SMEM] + [VMEM] * 4,
        out_specs=[VMEM] * 2,
        out_shape=[o, o],
        compiler_params=MID,
        chain=chain,
        name="merge_two",
    )(bit, kept, got, kept2, got2)


def put_blocks(ref, value, first, rows):
    n = value.shape[1]
    for k in range(value.shape[0] // rows):
        ref[:, pl.ds(pl.multiple_of((first + k) * n, 128), n)] = value[k * rows : (k + 1) * rows]


def finish_mlp(bit, own, got, ranks, chain=None):
    rows, n = own.shape
    half, part = rows // 2, n // ranks

    def body(bit_ref, own_ref, got_ref, down_ref, up_ref):
        for ref, place in ((own_ref, bit_ref[0]), (got_ref, 1 - bit_ref[0])):
            v = ref[...].astype(f32)
            down_ref[pl.ds(pl.multiple_of(place * half, 16), half), :] = v[:half]
            put_blocks(up_ref, v[half:], place * (half // part), part)

    s = jax.ShapeDtypeStruct
    return launch(
        body,
        in_specs=[SMEM, VMEM, VMEM],
        out_specs=[VMEM] * 2,
        out_shape=[s((rows, n), f32), s((part, rows // part * n), f32)],
        compiler_params=MID,
        chain=chain,
        name="finish_mlp",
    )(bit, own, got)


def finish_qkv(bit, own, got, ranks, chain=None):
    rows, n = own.shape
    part = n // ranks

    def body(bit_ref, own_ref, got_ref, qkv_ref, out_ref):
        def put(low_ref, high_ref):
            qkv_ref[:, :n] = low_ref[:part].astype(f32)
            qkv_ref[:, n : 2 * n] = low_ref[part:].astype(f32)
            qkv_ref[:, 2 * n :] = high_ref[:part].astype(f32)
            out_ref[...] = high_ref[part:].astype(f32)

        @pl.when(bit_ref[0] == 0)
        def _():
            put(own_ref, got_ref)

        @pl.when(bit_ref[0] == 1)
        def _():
            put(got_ref, own_ref)

    s = jax.ShapeDtypeStruct
    return launch(
        body,
        in_specs=[SMEM, VMEM, VMEM],
        out_specs=[VMEM] * 2,
        out_shape=[s((part, 3 * n), f32), s((part, n), f32)],
        compiler_params=MID,
        chain=chain,
        name="finish_qkv",
    )(bit, own, got)


def join_kernel(bit_ref, own_ref, got_ref, o_ref):
    o_ref[bit_ref[0]] = own_ref[...].astype(o_ref.dtype)
    o_ref[1 - bit_ref[0]] = got_ref[...].astype(o_ref.dtype)


def join(bit, own, got, dtype, chain=None):
    rows, n = own.shape
    o = launch(
        join_kernel,
        in_specs=[SMEM, VMEM, VMEM],
        out_specs=VMEM,
        out_shape=jax.ShapeDtypeStruct((2, rows, n), dtype),
        compiler_params=MID,
        chain=chain,
        name="join",
    )(bit, own, got)
    return o.reshape(2 * rows, n)


def norm_back(gy, h, gain):
    n, rstd = ln_stats(h)
    gn = gy * gain
    gh = rstd * (
        gn - jnp.mean(gn, axis=-1, keepdims=True) - n * jnp.mean(gn * n, axis=-1, keepdims=True)
    )
    return gh, colsum(gy * n), colsum(gy)


def mlp_out_kernel(rank_ref, a_ref, w_ref, h_ref, bias_ref, keep_ref, o0_ref, o1_ref, o2_ref, o3_ref, acc_ref):
    step = pl.program_id(0)
    add_to(acc_ref, mm(a_ref[...], w_ref[...]), step == 0)

    @pl.when(step == pl.num_programs(0) - 1)
    def _():
        keep = tiled(keep_ref[...], acc_ref.shape[1])
        acc_ref[...] = (acc_ref[...] + h_ref[...] + bias_ref[...]) * keep
        for k, o_ref in enumerate((o0_ref, o1_ref, o2_ref, o3_ref)):
            toks = o_ref.shape[0]
            at = pl.ds(pl.multiple_of((rank_ref[0] ^ k) * toks, 16), toks)
            o_ref[...] = acc_ref[at, :].astype(bf16)


def mlp_out(rank, act, weight, hidden, bias, keep, chain=None):
    toks, n = hidden.shape
    part = jax.ShapeDtypeStruct((toks // 4, n), bf16)
    return launch(
        mlp_out_kernel,
        grid=(act.shape[1] // n,),
        in_specs=[
            SMEM, pl.BlockSpec((toks, n), lambda b: (0, b)), pl.BlockSpec((n, n), lambda b: (b, 0)),
            whole((toks, n)), whole((1, n)), whole(keep.shape),
        ],
        out_specs=[whole(part.shape)] * 4,
        out_shape=[part] * 4,
        scratch_shapes=[pltpu.VMEM((toks, n), f32)],
        compiler_params=MID,
        chain=chain,
        name="mlp_out",
    )(rank, act, weight, hidden, bias[None], keep)


def scatter_kernel(rank_ref, *refs):
    for k, ref in enumerate(refs[:-1]):
        refs[-1][rank_ref[0] ^ k] = ref[...]


def scatter(rank, parts, chain=None):
    return launch(
        scatter_kernel,
        in_specs=[SMEM] + [VMEM] * len(parts),
        out_specs=VMEM,
        out_shape=jax.ShapeDtypeStruct((len(parts),) + parts[0].shape, parts[0].dtype),
        compiler_params=MID,
        chain=chain,
        name="scatter",
    )(rank, *parts)


def mlp_back_kernel(
    rank_ref, g_ref, down_ref, slope_ref, n_ref, up_ref, h_ref, gain_ref, out_ref,
    keep_ref, send_ref, bias_ref, gh_ref, low_ref, att_ref, dgain_ref, dbias_ref, acc_ref,
):
    step = pl.program_id(0)
    g = mm_nt(g_ref[...], down_ref[...]) * slope_ref[...].astype(f32)
    bias_ref[...] = colsum(g)
    g = g.astype(bf16)
    store_quarters(rank_ref, mm_tn(n_ref[...], g), keep_ref, send_ref)
    add_to(acc_ref, mm_nt(g, up_ref[...]), step == 0)

    @pl.when(step == pl.num_programs(0) - 1)
    def _():
        gh, dgain_ref[...], dbias_ref[...] = norm_back(acc_ref[...], h_ref[...], gain_ref[...])
        gh = gh + g_ref[...].astype(f32)
        gh_ref[...] = gh
        low = gh.astype(bf16)
        low_ref[...] = low
        att_ref[...] = mm_nt(low, out_ref[...]).astype(bf16)


def mlp_back(rank, g, down, slope, normed, up, hidden, gain, out_weight, chain=None):
    toks, n = hidden.shape
    blocks = up.shape[1] // n
    half = blocks // 2
    rows = n // 4
    s = jax.ShapeDtypeStruct
    full, row = whole((toks, n)), whole((1, n))
    lanes = pl.BlockSpec((toks, n), lambda b: (0, b))
    part = pl.BlockSpec((1, 2, 1, rows, n), lambda b: (b // half, 0, b % half, 0, 0))
    parts = s((2, 2, half, rows, n), bf16)
    keep, send, bias, *rest = launch(
        mlp_back_kernel,
        grid=(blocks,),
        in_specs=[
            SMEM, full, pl.BlockSpec((n, n), lambda b: (b, 0)), lanes, full,
            pl.BlockSpec((n, n), lambda b: (0, b)), full, row, whole((n, n)),
        ],
        out_specs=[part, part, pl.BlockSpec((1, n), lambda b: (0, b)), full, full, full, row, row],
        out_shape=[
            parts, parts, s((1, up.shape[1]), f32), s((toks, n), f32), s((toks, n), bf16), s((toks, n), bf16),
            s((1, n), f32), s((1, n), f32),
        ],
        scratch_shapes=[pltpu.VMEM((toks, n), f32)],
        compiler_params=pltpu.CompilerParams(vmem_limit_bytes=40 * 1024 * 1024),
        chain=chain,
        hbm=True,
        name="mlp_back",
    )(rank, g, down, slope, normed, up, hidden, gain[None], out_weight)
    return (keep, send), bias, *rest


def qkv_back_kernel(g_ref, w_ref, h_ref, gain_ref, gh2_ref, low_ref, dgain_ref, dbias_ref, sum_ref, acc_ref):
    step = pl.program_id(0)
    add_to(acc_ref, mm_nt(g_ref[...], w_ref[...]), step == 0)

    @pl.when(step == pl.num_programs(0) - 1)
    def _():
        gh, dgain_ref[...], dbias_ref[...] = norm_back(acc_ref[...], h_ref[...], gain_ref[...])
        gh = gh + gh2_ref[...]
        sum_ref[...] = colsum(gh)
        low_ref[...] = gh.astype(bf16)


def qkv_back(g, weight, hidden, gain, gh2, chain=None):
    toks, n = hidden.shape
    s = jax.ShapeDtypeStruct
    full, row = whole((toks, n)), whole((1, n))
    return launch(
        qkv_back_kernel,
        grid=(g.shape[1] // n,),
        in_specs=[
            pl.BlockSpec((toks, n), lambda b: (0, b)), pl.BlockSpec((n, n), lambda b: (0, b)), full, row, full,
        ],
        out_specs=[full, row, row, row],
        out_shape=[s((toks, n), bf16)] + [s((1, n), f32)] * 3,
        scratch_shapes=[pltpu.VMEM((toks, n), f32)],
        compiler_params=MID,
        chain=chain,
        name="qkv_back",
    )(g, weight, hidden, gain[None], gh2)


def attend_kernel(keep_ref, q_ref, k_ref, v_ref, o_ref, l_ref):
    scale = HEAD_DIM**-0.5
    valid = keep_ref[...] > 0
    outs = []
    for h in range(2):
        lanes = slice(h * HEAD_DIM, (h + 1) * HEAD_DIM)
        q, k, v = q_ref[:, lanes], k_ref[:, lanes], v_ref[:, lanes]
        s = jnp.where(valid, mm_nt(k, q) * scale, -1000000000.0)
        top = jnp.max(s, axis=0, keepdims=True)
        e = jnp.exp(s - top)
        total = jnp.sum(e, axis=0, keepdims=True)
        outs.append(mm_tn(v, e.astype(bf16)) / total)
        l_ref[0, h : h + 1, :] = top + jnp.log(total)
    o_ref[...] = jnp.concatenate(outs, axis=0).T.astype(bf16)

def attend(qkv, keep, chain=None):
    tok, width3 = qkv.shape
    pairs = HEADS // 2
    two = 2 * HEAD_DIM
    def spec(kind):
        return pl.BlockSpec((tok, two), lambda h: (0, kind * pairs + h))
    return launch(
        attend_kernel, grid=(pairs,),
        in_specs=[pl.BlockSpec((tok, 1), lambda h: (0, 0)), spec(0), spec(1), spec(2)],
        out_specs=[spec(0), pl.BlockSpec((1, 2, tok), lambda h: (h, 0, 0))],
        out_shape=[jax.ShapeDtypeStruct((tok, width3 // 3), bf16), jax.ShapeDtypeStruct((pairs, 2, tok), f32)],
        compiler_params=pltpu.CompilerParams(vmem_limit_bytes=40*1024*1024),
        chain=chain,
        name="attend",
    )(keep, qkv, qkv, qkv)

def attend_back_kernel(keep_ref, q_ref, k_ref, v_ref, g_ref, l_ref, o_ref):
    scale = HEAD_DIM**-0.5
    valid = keep_ref[...] > 0
    gqs, gks, gvs = [], [], []
    for h in range(2):
        lanes = slice(h * HEAD_DIM, (h + 1) * HEAD_DIM)
        q, k, v, g = q_ref[:, lanes], k_ref[:, lanes], v_ref[:, lanes], g_ref[:, lanes]
        s = jnp.where(valid, mm_nt(k, q) * scale, -1000000000.0)
        p = jnp.exp(s - l_ref[0, h : h + 1, :])
        gp = mm_nt(v, g)
        dot = jnp.sum(gp * p, axis=0, keepdims=True)
        gs = (p * (gp - dot)).astype(bf16)
        gvs.append(mm(p.astype(bf16), g))
        gks.append(mm(gs, q) * scale)
        gqs.append(mm_tn(k, gs) * scale)
    width = o_ref.shape[1] // 3
    step = pl.program_id(0)
    for kind, value in enumerate(
        (jnp.concatenate(gqs, axis=0).T, jnp.concatenate(gks, axis=1), jnp.concatenate(gvs, axis=1))
    ):
        lanes = pl.ds(pl.multiple_of(kind * width + step * 2 * HEAD_DIM, 128), 2 * HEAD_DIM)
        o_ref[:, lanes] = value.astype(bf16)


def attend_back(qkv, keep, g, logs, chain=None):
    tok, width3 = qkv.shape
    pairs = HEADS // 2
    two = 2 * HEAD_DIM
    def spec(kind):
        return pl.BlockSpec((tok, two), lambda h: (0, kind * pairs + h))
    return launch(
        attend_back_kernel, grid=(pairs,),
        in_specs=[pl.BlockSpec((tok, 1), lambda h: (0, 0)), spec(0), spec(1), spec(2), spec(0), pl.BlockSpec((1, 2, tok), lambda h: (h, 0, 0))],
        out_specs=whole((tok, width3)),
        out_shape=jax.ShapeDtypeStruct((tok, width3), bf16),
        compiler_params=pltpu.CompilerParams(vmem_limit_bytes=40*1024*1024),
        chain=chain,
        name="attend_back",
    )(keep, qkv, qkv, qkv, g, logs)


def per_image(parts, cots, made, params, flows):
    (
        conv_in,
        conv_mid,
        conv_out,
        conv_skip,
        norm_gain,
        norm_bias,
        patch_weight,
        patch_bias,
        attn_gain,
        attn_bias,
        qkv_weight,
        out_weight,
        mlp_gain,
        mlp_bias,
        up_weight,
        up_bias,
        down_weight,
        down_bias,
    ) = params
    w_in, w_out, w_skip, b_fwd, b_bwd, g64, g256, vec, keep_wide, edge = made
    c0 = conv_in.shape[0]
    c3 = conv_out.shape[1]
    ranks = lax.axis_size("row")
    keep = keep_wide[:, :1]
    chain = flows.chain
    x, wide, d1, p2, d2, n2, st1, st2, st3 = stem_front(
        flows.rank, parts, w_in, b_fwd, w_out, vec, g64, g256, keep_wide, edge, chain
    )
    stem, d3 = stem_last(p2, x, w_out, w_skip, st3, keep_wide, chain)
    pw = patch_weight.reshape(PATCH, PATCH * c3, -1)
    hidden = patch_bias
    for i in range(PATCH):
        hidden = hidden + mm(stem[i], pw[i])
    na, ra = ln_stats(hidden)
    normed = (na * attn_gain + attn_bias).astype(bf16)
    qkv = mm(normed, qkv_weight).astype(bf16)
    attended, logs = attend(qkv, keep, chain)
    hidden2 = hidden + mm(attended, out_weight)
    nm, rm = ln_stats(hidden2)
    normed2 = (nm * mlp_gain + mlp_bias).astype(bf16)
    pre = mm(normed2, up_weight) + up_bias
    act, dact = gelu_both(pre)
    act = act.astype(bf16)
    g_low, grad_down_bias = gather(flows.rank, cots, keep_wide, chain)
    rank = flows.rank
    flows.begin("down", wgrad_rows(rank, act, g_low, 1, chain), order_of("x"))
    parts, grad_up_bias, g_h2, g_h2_low, g_att, grad_mlp_gain, grad_mlp_bias = mlp_back(
        rank, g_low, down_weight, dact.astype(bf16), normed2, up_weight, hidden2, mlp_gain, out_weight, chain
    )
    flows.begin("up", parts, order_of("y"))
    flows.pump()
    flows.pump()
    g_qkv = attend_back(qkv, keep, g_att, logs, chain)
    flows.pump()
    g_h, grad_attn_gain, grad_attn_bias, grad_patch_bias = qkv_back(
        g_qkv, qkv_weight, hidden, attn_gain, g_h2, chain
    )
    flows.begin("patch", wgrad_rows(rank, stem, g_h, 1, chain), order_of("x"))
    flows.pump()
    parts = wgrad_qkv(rank, normed, g_qkv, attended, g_h2_low, chain)
    flows.begin("qkv", parts, order_of("y"), finish_qkv)
    flows.pump()
    g_z, co3, grad_skip = stem_back1(
        g_h, pw, d3, p2, x, w_out, st3, vec, g256, flows.chain
    )
    flows.pump()
    g_2, co2, grad_cout = stem_back2(
        g_z, p2, d2, n2, w_out, st3, co3, vec, g64, keep_wide, flows.chain
    )
    flows.pump()
    g_1, co1, grad_mid = stem_back3(
        g_2, n2, wide, b_bwd, d1, x, w_in, st1, st2, co2, vec, g64, keep_wide, edge, flows.chain
    )
    flows.pump()
    *input_grad, grad_in = stem_back4(
        rank, g_1, x, g_z, w_in, w_skip, st1, co1, vec, keep_wide, ranks, flows.chain
    )
    vecs = (grad_patch_bias, grad_attn_gain, grad_attn_bias, grad_mlp_gain, grad_mlp_bias, grad_down_bias)
    small = collect(
        rank, grad_in, grad_mid, grad_cout, grad_skip, co1, co2, co3,
        vecs, grad_up_bias, flows.chain
    )
    out = (act, down_weight, hidden2, down_bias, keep_wide)
    return out, input_grad, small


def swap(v, axis, step):
    count = lax.axis_size(axis)
    return lax.ppermute(v, axis, [(i, i ^ step) for i in range(count)])


def steps_of(axis):
    count = lax.axis_size(axis)
    return [1 << b for b in range(count.bit_length() - 1)]


def bit_of(axis, step):
    return ((lax.axis_index(axis) & step) // step).astype(jnp.int32).reshape(1)


class Flow:
    def __init__(self, kept, sent, order, last=None):
        n = kept.shape[-1]
        self.kept = kept.reshape(-1, n)
        self.sent = sent.reshape(-1, n)
        self.todo = list(order)
        self.undo = [s for a, s in reversed(order) if a == "img"]
        self.last = last
        self.done = False
        self.start()

    def start(self):
        if self.todo:
            self.got = swap(self.sent, *self.todo[0])
        elif self.undo:
            self.got = swap(self.kept, "img", self.undo[0])

    def step(self, chain):
        if self.todo:
            self.todo.pop(0)
            if self.todo:
                axis, step = self.todo[0]
                bit = bit_of("img", step) if axis == "img" else jnp.zeros((1,), jnp.int32)
                self.kept, self.sent = merge(bit, self.kept, self.got, chain)
            else:
                self.kept = plus(self.kept, self.got, chain)
        else:
            step = self.undo.pop(0)
            self.done = not self.undo
            bit = bit_of("img", step)
            if self.done and self.last:
                self.kept = self.last(bit, self.kept, self.got, lax.axis_size("row"), chain)
            else:
                self.kept = join(bit, self.kept, self.got, f32 if self.done else bf16, chain)
        self.start()


class Pair(Flow):
    def __init__(self, one, two, last, chain):
        order = [(a, s) for a, s in order_of("x") if a == "img"]
        self.undo = [s for a, s in reversed(order)]
        order = order[1:]
        self.todo = list(order)
        self.last = last
        self.done = False
        bit = bit_of(*order[0])
        self.kept, self.sent = merge_two(bit, one.kept, one.got, two.kept, two.got, chain)
        self.start()


class SmallFlow:
    def __init__(self, kept, sent):
        self.kept, self.sent = kept, sent
        self.todo = order_of("x")
        self.done = False
        self.got = swap(self.sent, *self.todo[0])

    def step(self, chain):
        self.todo.pop(0)
        self.done = not self.todo
        if not self.done and self.todo[0][0] == "row":
            self.kept, self.sent = split(self.kept, self.got, chain)
        else:
            self.kept = self.sent = plus(self.kept, self.got, chain)
        if not self.done:
            self.got = swap(self.sent, *self.todo[0])


class Flows:
    def __init__(self, plan):
        self.plan = list(plan)
        self.live = {}
        self.chain = Chain()
        self.rank = lax.axis_index("row").reshape(1)
        self.tasks = {"pair": self.pair}

    def begin(self, name, parts, order, last=None):
        self.live[name] = Flow(*parts, order, last)

    def pair(self):
        one, two = self.live.pop("down"), self.live.pop("up")
        self.live["mlp"] = Pair(one, two, finish_mlp, self.chain)

    def pump(self):
        for name in self.plan.pop(0):
            if name in self.tasks:
                self.tasks.pop(name)()
            else:
                self.live[name].step(self.chain)

    def drain(self):
        while not all(flow.done for flow in self.live.values()):
            for flow in self.live.values():
                if not flow.done:
                    flow.step(self.chain)


def order_of(first):
    row = [("row", s) for s in steps_of("row")]
    img = [("img", s) for s in steps_of("img")]
    if first == "y":
        return row[:1] + img[:1] + row[1:] + img[1:]
    if first == "z":
        return row[:1] + img[1:] + row[1:] + img[:1]
    return row + img


PLAN = (
    ("down", ),
    ("up", ),
    (),
    ("down", "up", ),
    ("patch", "qkv", ),
    ("pair", ),
    ("mlp", "qkv", ),
    ("patch", "mlp", ),
    ("mlp", "qkv", "patch", "mlp", "unpack", "small", "patch", "qkv", "small1", "out", "patch", "qkv", "small1", "patch", "qkv", "mlp", "small1", "patch", "qkv", "scatter", "small1", "small1", "patch", "qkv", ),
)


def exchange(parts):
    return [parts[0]] + [swap(parts[k], "row", k) for k in range(1, len(parts))]


def per_device(stem_input, group, *rest):
    params, cot = rest[:-1], rest[-1]
    images, row_count, col_count, c0 = stem_input.shape
    ranks = lax.axis_size("row")
    assert images == ranks
    flows = Flows(PLAN)
    rank = flows.rank
    front = flows.chain
    parts = pack(rank, stem_input, front)
    made = prep(rank, group, *rest[:6], cot, front)
    parts = exchange(parts)
    made, cots = made[:10], exchange(made[10:])
    out, input_grad, small = per_image(parts, cots, made, params, flows)
    chain = flows.chain
    done = {}

    def start_small():
        flows.live["small1"] = SmallFlow(*small)

    def start_out():
        done["out"] = exchange(mlp_out(rank, *out, chain))

    def end_input():
        done["ig"] = unpack(rank, exchange(input_grad), chain)

    def end_out():
        done["block"] = scatter(rank, done["out"], chain)

    flows.tasks.update(small=start_small, out=start_out, unpack=end_input, scatter=end_out)
    flows.pump()
    for name in list(flows.tasks):
        if name != "pair":
            flows.tasks.pop(name)()
    flows.drain()
    ig, block_out = done["ig"], done["block"]
    small = deal(
        flows.live["small1"].kept[0], c0 // ranks, c0, rest[2].shape[1],
        rest[4].shape[0] // ranks, rest[6].shape[1] // ranks, rest[15].shape[0] // ranks,
    )
    qkv, out = flows.live["qkv"].kept
    down, up = flows.live["mlp"].kept
    vecs = [v[0] for v in small[4:]]
    shares = [small[0], small[1].transpose(1, 0, 2), small[2], small[3], vecs[0], vecs[1]]
    shares += [flows.live["patch"].kept, vecs[2], vecs[3], vecs[4]]
    shares += [qkv, out, vecs[5], vecs[6]]
    shares += [up, vecs[8], down, vecs[7]]
    return (block_out, ig) + tuple(shares)


def solution(mesh):
    rep = P()
    in_specs = (P("img", "row", None, None), P("img")) + (rep,) * 18 + (P("img", "row", None),)
    dims = (2, 3, 2, 2, 1, 1, 2, 1, 1, 1, 2, 2, 1, 1, 2, 1, 2, 1)
    out_specs = (P("img", "row", None), P("img", "row", None, None)) + tuple(
        P("row", *([None] * (n - 1))) for n in dims
    )
    return jax.shard_map(
        per_device, mesh=mesh, in_specs=in_specs, out_specs=out_specs, check_vma=False
    )
```

```python
import jax
import jax.numpy as jnp
from jax import lax
from jax.experimental import pallas as pl
from jax.experimental.pallas import tpu as pltpu
from jax.sharding import PartitionSpec as P

GROUPS = 32
HEADS = 12
HEAD_DIM = 64
PATCH = 4
FULL = 96
SMALL = 56
SIDE = FULL // PATCH
TOK = SIDE * SIDE
f32 = jnp.float32
bf16 = jnp.bfloat16


def mm(a, b):
    return lax.dot_general(a, b, (((1,), (0,)), ((), ())), preferred_element_type=f32)


def mm_nt(a, b):
    return lax.dot_general(a, b, (((1,), (1,)), ((), ())), preferred_element_type=f32)


def mm_tn(a, b):
    return lax.dot_general(a, b, (((0,), (0,)), ((), ())), preferred_element_type=f32)


def gelu_both(z):
    cdf = 0.5 + 0.5 * lax.erf(z * 0.7071067811865476)
    bell = jnp.exp(-0.5 * z * z)
    return z * cdf, cdf + z * bell * 0.3989422804014327


SRCS = (0, 1, 2, 3, -1, 4)
VMEM = pl.BlockSpec(memory_space=pltpu.VMEM)
SMEM = pl.BlockSpec(memory_space=pltpu.SMEM)


ANY = pl.BlockSpec(memory_space=pl.ANY)
TIMES = {
    "mlp_out": 4,
    "attend": 10, "attend_back": 15, "stem_front": 11, "stem_last": 11, "stem_back1": 13, "stem_back2": 12,
    "stem_back3": 10, "stem_back4": 8, "wgrad_rows": 6, "wgrad_qkv": 6, "mlp_back": 18,
    "qkv_back": 5, "unpack": 4, "pack": 2, "prep": 4,
}


def cost(name):
    flops = int(TIMES.get(name, 1) * 0.3 * 1.1e9)
    return pl.CostEstimate(flops=flops, bytes_accessed=flops // 1000, transcendentals=0)


class Chain:
    def __init__(self):
        self.tokens = []


def launch(kernel, chain=None, in_specs=None, grid_spec=None, out_specs=None, out_shape=None, **options):
    deps = chain.tokens if chain else []
    extra = [ANY] * len(deps)
    single = not isinstance(out_shape, (list, tuple))
    if single:
        out_shape = [out_shape]
    if grid_spec:
        out_specs = grid_spec["out_specs"]
    if not isinstance(out_specs, (list, tuple)):
        out_specs = [out_specs]
    outs = len(out_shape)
    if options.pop("hbm", False):
        out_shape = [pltpu.HBM(o.shape, o.dtype) for o in out_shape]
    count = len(in_specs if in_specs else grid_spec["in_specs"])
    count += grid_spec["num_scalar_prefetch"] if grid_spec else 0
    out_shape, out_specs = list(out_shape), list(out_specs)
    if chain:
        out_shape = out_shape + [jax.ShapeDtypeStruct((8, 128), f32)]
        out_specs = out_specs + [pl.BlockSpec((8, 128), lambda *_: (0, 0))]
    if grid_spec:
        spec = dict(grid_spec, in_specs=grid_spec["in_specs"] + extra, out_specs=out_specs)
        options["grid_spec"] = pltpu.PrefetchScalarGridSpec(**spec)
    else:
        options["in_specs"], options["out_specs"] = in_specs + extra, out_specs

    def body(*refs):
        at = count + len(deps) + outs
        if chain:
            refs[at][...] = jnp.zeros((8, 128), f32)
        return kernel(*refs[:count], *refs[count + len(deps) : at], *refs[at + (1 if chain else 0) :])

    run = pl.pallas_call(body, out_shape=out_shape, cost_estimate=cost(options["name"]), **options)

    def call(*operands):
        out = run(*operands, *deps)
        if chain:
            chain.tokens = [out[-1]]
            out = out[:-1]
        return out[0] if single else out

    return call


MID = pltpu.CompilerParams(vmem_limit_bytes=24 * 1024 * 1024)
BIG = pltpu.CompilerParams(vmem_limit_bytes=56 * 1024 * 1024)


def whole(shape):
    return pl.BlockSpec(shape, lambda i: (0,) * len(shape))


def slab(shape):
    return pl.BlockSpec((1,) + tuple(shape[1:]), lambda i: (i,) + (0,) * (len(shape) - 1))


def exact(row, mat):
    return jnp.dot(row, mat, precision=lax.Precision.HIGHEST, preferred_element_type=f32)


def fold(row):
    n = row.shape[1] // PATCH
    return sum(row[:, j * n : (j + 1) * n] for j in range(PATCH))


def tile4(row):
    return jnp.concatenate([row] * PATCH, axis=1)


def tiled(keep, lanes):
    return jnp.concatenate([keep] * (lanes // keep.shape[1]), axis=1)


def back_coefs(sums, gain, inv, gmat, wide):
    if wide:
        pair = jnp.concatenate([fold(r * gain) for r in sums] + [jnp.zeros((6, 256), f32)], axis=0)
        pair = exact(pair, gmat)
        return tile4(pair[0:1]) * inv, tile4(pair[1:2]) * inv
    pair = jnp.concatenate([r * gain for r in sums] + [jnp.zeros((6, 256), f32)], axis=0)
    pair = exact(pair, gmat)
    return pair[0:1] * inv, pair[1:2] * inv


def add_to(ref, value, first):
    @pl.when(first)
    def _():
        ref[...] = value

    @pl.when(jnp.logical_not(first))
    def _():
        ref[...] += value


def colsum(v):
    return jnp.sum(v, axis=0, keepdims=True)


def stem_back1_kernel(
    gh_ref, pw_ref, d3_ref, p2_ref, x_ref, w_ref, st_ref, vec_ref, g256_ref,
    gz_ref, out_ref, skip_ref, acc_ref, sum_ref,
):
    i = pl.program_id(0)
    gz = mm_nt(gh_ref[...], pw_ref[0]) * d3_ref[0].astype(f32)
    n = mm(p2_ref[0], w_ref[...]) * st_ref[0:1] + st_ref[1:2]
    low = gz.astype(bf16)
    gz_ref[0] = low
    add_to(sum_ref, jnp.concatenate([colsum(gz), colsum(gz * n)] + [jnp.zeros((6, gz.shape[1]), f32)], axis=0), i == 0)
    add_to(acc_ref, mm_tn(x_ref[0], low), i == 0)

    @pl.when(i == PATCH - 1)
    def _():
        c1, c2 = sum_ref[0:1], sum_ref[1:2]
        s1, s2 = back_coefs((c1, c2), vec_ref[4:5], vec_ref[7:8], g256_ref[...], True)
        zero = jnp.zeros_like(c1)
        bias, gain = tile4(fold(c1)), tile4(fold(c2))
        out_ref[...] = jnp.concatenate([s1, s2, bias, gain] + [zero] * 4, axis=0)
        c, n = skip_ref.shape
        skip_ref[...] = sum(
            acc_ref[j * c : (j + 1) * c, j * n : (j + 1) * n] for j in range(PATCH)
        )


def stem_back1(g_h, pw, d3, p2, x, w_out, stat, vec, g256, chain=None):
    lanes = d3.shape[2]
    c = p2.shape[2] // PATCH
    s = jax.ShapeDtypeStruct
    return launch(
        stem_back1_kernel,
        grid=(PATCH,),
        in_specs=[
            whole(g_h.shape), slab(pw.shape), slab(d3.shape), slab(p2.shape), slab(x.shape),
            whole(w_out.shape), whole(stat.shape), whole(vec.shape), whole(g256.shape),
        ],
        out_specs=[slab(d3.shape), whole((8, lanes)), whole((c, lanes // PATCH))],
        out_shape=[s(d3.shape, bf16), s((8, lanes), f32), s((c, lanes // PATCH), f32)],
        scratch_shapes=[pltpu.VMEM((PATCH * c, lanes), f32), pltpu.VMEM((8, lanes), f32)],
        compiler_params=BIG,
        chain=chain,
        name="stem_back1",
    )(g_h, pw, d3, p2, x, w_out, stat, vec, g256)


def stem_back2_kernel(
    gz_ref, p2_ref, d2_ref, n2_ref, w_ref, st_ref, co_ref, vec_ref, g64_ref, keep_ref,
    g2_ref, out_ref, grad_ref, acc_ref, sum_ref,
):
    i = pl.program_id(0)
    lanes = gz_ref.shape[2]
    keep = tiled(keep_ref[...], lanes)
    rstd, gain, s1, s2 = st_ref[0:1], vec_ref[4:5], co_ref[0:1], co_ref[1:2]
    n = mm(p2_ref[0], w_ref[...]) * rstd + st_ref[1:2]
    gv = (rstd * (gz_ref[0].astype(f32) * gain - s1 - n * s2) * keep).astype(bf16)
    add_to(acc_ref, mm_tn(p2_ref[0], gv), i == 0)
    g2 = mm_nt(gv, w_ref[...]) * d2_ref[0].astype(f32)
    g2_ref[0] = g2.astype(bf16)
    add_to(sum_ref, jnp.concatenate([colsum(g2), colsum(g2 * n2_ref[0].astype(f32))] + [jnp.zeros((6, g2.shape[1]), f32)], axis=0), i == 0)

    @pl.when(i == PATCH - 1)
    def _():
        narrow = g2_ref.shape[2]
        c1, c2 = sum_ref[0:1], sum_ref[1:2]
        s1, s2 = back_coefs((c1, c2), vec_ref[2:3, :narrow], vec_ref[6:7, :narrow], g64_ref[...], False)
        out_ref[...] = jnp.concatenate([s1, s2, c1, c2] + [jnp.zeros_like(c1)] * 4, axis=0)
        c, n = grad_ref.shape
        grad_ref[...] = sum(
            acc_ref[j * c : (j + 1) * c, j * n : (j + 1) * n] for j in range(PATCH)
        )


def stem_back2(gz, p2, d2, n2, w_out, stat, coef, vec, g64, keep, chain=None):
    lanes = gz.shape[2]
    narrow = p2.shape[2]
    c = narrow // PATCH
    s = jax.ShapeDtypeStruct
    return launch(
        stem_back2_kernel,
        grid=(PATCH,),
        in_specs=[
            slab(gz.shape), slab(p2.shape), slab(d2.shape), slab(n2.shape), whole(w_out.shape),
            whole(stat.shape), whole(coef.shape), whole(vec.shape), whole(g64.shape), whole(keep.shape),
        ],
        out_specs=[slab(p2.shape), whole((8, narrow)), whole((c, lanes // PATCH))],
        out_shape=[s(p2.shape, bf16), s((8, narrow), f32), s((c, lanes // PATCH), f32)],
        scratch_shapes=[pltpu.VMEM((narrow, lanes), f32), pltpu.VMEM((8, narrow), f32)],
        compiler_params=BIG,
        chain=chain,
        name="stem_back2",
    )(gz, p2, d2, n2, w_out, stat, coef, vec, g64, keep)


def edges(v, edge):
    c = v.shape[1] // PATCH
    toks = v.shape[0]
    left = pltpu.roll(v[:, 3 * c :], 1, 0)
    right = pltpu.roll(v[:, :c], toks - 1, 0)
    return jnp.concatenate([left, right], axis=1) * edge


def fill_wide(wide_ref, i, v, edge):
    lanes = v.shape[1]
    v = jnp.concatenate([v, edges(v, edge)], axis=1)
    wide_ref[i + 1] = v.astype(bf16)
    gap = jnp.zeros((SIDE, v.shape[1]), f32)
    if i == PATCH - 1:
        wide_ref[0] = jnp.concatenate([gap, v[:-SIDE]], axis=0).astype(bf16)
    if i == 0:
        wide_ref[PATCH + 1] = jnp.concatenate([v[SIDE:], gap], axis=0).astype(bf16)


def stem_back3_kernel(
    g2_ref, n2_ref, p1_ref, b_ref, d1_ref, x_ref, w_ref, st1_ref, st2_ref, co_ref, vec_ref, g64_ref,
    keep_ref, edge_ref, g1_ref, out_ref, grad_ref, wide_ref,
):
    narrow = g2_ref.shape[2]
    c = narrow // PATCH
    keep = tiled(keep_ref[...], narrow)
    rstd, gain, s1, s2 = st2_ref[0:1], vec_ref[2:3, :narrow], co_ref[0:1], co_ref[1:2]
    for i in range(PATCH):
        gv = rstd * (g2_ref[i].astype(f32) * gain - s1 - n2_ref[i].astype(f32) * s2) * keep
        fill_wide(wide_ref, i, gv, edge_ref[...])
    for di in range(3):
        total = 0.0
        for i in range(PATCH):
            total = total + mm_tn(p1_ref[i + di], wide_ref[i + 1, :, :narrow])
        for dj in range(3):
            grad_ref[3 * di + dj] = sum(
                total[k * c : (k + 1) * c, j * c : (j + 1) * c]
                for j in range(PATCH)
                for k in (SRCS.index(j + dj - 1),)
            )
    c1 = c2 = 0.0
    for i in range(PATCH):
        g1 = sum(mm_nt(wide_ref[i + di], b_ref[di]) for di in range(3)) * d1_ref[i].astype(f32)
        g1_ref[i] = g1.astype(bf16)
        n = mm(x_ref[i], w_ref[...]) * st1_ref[0:1] + st1_ref[1:2]
        c1 = c1 + colsum(g1)
        c2 = c2 + colsum(g1 * n)
    s1, s2 = back_coefs((c1, c2), vec_ref[0:1, :narrow], vec_ref[6:7, :narrow], g64_ref[...], False)
    out_ref[...] = jnp.concatenate([s1, s2, c1, c2] + [jnp.zeros_like(c1)] * 4, axis=0)


def stem_back3(g2, n2, p1_wide, b_bwd, d1, x, w_in, stat1, stat2, coef, vec, g64, keep, edge, chain=None):
    narrow = g2.shape[2]
    c = narrow // PATCH
    s = jax.ShapeDtypeStruct
    vm = VMEM
    return launch(
        stem_back3_kernel,
        in_specs=[vm] * 14,
        out_specs=[vm] * 3,
        out_shape=[s(g2.shape, bf16), s((8, narrow), f32), s((9, c, c), f32)],
        scratch_shapes=[pltpu.VMEM((PATCH + 2, TOK, 6 * c), bf16)],
        compiler_params=BIG,
        chain=chain,
        name="stem_back3",
    )(g2, n2, p1_wide, b_bwd, d1, x, w_in, stat1, stat2, coef, vec, g64, keep, edge)


def stem_back4_kernel(
    rank_ref, g1_ref, x_ref, gz_ref, win_ref, wskip_ref, st_ref, co_ref, vec_ref, keep_ref,
    o0_ref, o1_ref, o2_ref, o3_ref, grad_ref, acc_ref, ig_ref,
):
    i = pl.program_id(0)
    narrow = g1_ref.shape[2]
    keep = tiled(keep_ref[...], narrow)
    rstd, gain, s1, s2 = st_ref[0:1], vec_ref[0:1, :narrow], co_ref[0:1], co_ref[1:2]
    n = mm(x_ref[0], win_ref[...]) * rstd + st_ref[1:2]
    gv = (rstd * (g1_ref[0].astype(f32) * gain - s1 - n * s2) * keep).astype(bf16)
    add_to(acc_ref, mm_tn(x_ref[0], gv), i == 0)
    ig_ref[...] = (mm_nt(gv, win_ref[...]) + mm_nt(gz_ref[0], wskip_ref[...])) * keep
    for k, o_ref in enumerate((o0_ref, o1_ref, o2_ref, o3_ref)):
        toks = o_ref.shape[1]
        at = pl.ds(pl.multiple_of((rank_ref[0] ^ k) * toks, 16), toks)
        o_ref[0] = ig_ref[at, :].astype(bf16)

    @pl.when(i == PATCH - 1)
    def _():
        c = grad_ref.shape[0]
        grad_ref[...] = sum(
            acc_ref[j * c : (j + 1) * c, j * c : (j + 1) * c] for j in range(PATCH)
        )


def stem_back4(rank, g1, x, gz, w_in, w_skip, stat, coef, vec, keep, ranks, chain=None):
    narrow = g1.shape[2]
    c = narrow // PATCH
    part = jax.ShapeDtypeStruct((PATCH, TOK // ranks, narrow), bf16)
    return launch(
        stem_back4_kernel,
        grid=(PATCH,),
        in_specs=[
            SMEM, slab(g1.shape), slab(x.shape), slab(gz.shape), whole(w_in.shape), whole(w_skip.shape),
            whole(stat.shape), whole(coef.shape), whole(vec.shape), whole(keep.shape),
        ],
        out_specs=[slab(part.shape)] * ranks + [whole((c, c))],
        out_shape=[part] * ranks + [jax.ShapeDtypeStruct((c, c), f32)],
        scratch_shapes=[pltpu.VMEM((narrow, narrow), f32), pltpu.VMEM((TOK, narrow), f32)],
        compiler_params=BIG,
        chain=chain,
        name="stem_back4",
    )(rank, g1, x, gz, w_in, w_skip, stat, coef, vec, keep)


def scale_shift(c1, c2, gain, bias, inv, gmat, wide):
    pair = jnp.concatenate([c1, c2], axis=0)
    if wide:
        pair = fold(pair)
    pair = exact(jnp.concatenate([pair, jnp.zeros((6, pair.shape[1]), f32)], axis=0), gmat)
    if wide:
        pair = tile4(pair)
    mean, square = pair[0:1] * inv, pair[1:2] * inv
    rstd = lax.rsqrt(square - mean * mean + 1e-05)
    shift = -mean * rstd
    return rstd, shift, rstd * gain, bias + shift * gain


def stem_front_kernel(
    rank_ref, x0_ref, x1_ref, x2_ref, x3_ref,
    win_ref, bf_ref, wout_ref, vec_ref, g64_ref, g256_ref, keep_ref, edge_ref,
    x_ref, wide_ref, d1_ref, p2_ref, d2_ref, n2_ref, st1_ref, st2_ref, st3_ref, v_ref,
):
    narrow = x_ref.shape[2]
    for k, part_ref in enumerate((x0_ref, x1_ref, x2_ref, x3_ref)):
        toks = part_ref.shape[1]
        at = pl.ds(pl.multiple_of((rank_ref[0] ^ k) * toks, 16), toks)
        mask = tiled(keep_ref[at, :], narrow)
        for i in range(PATCH):
            x_ref[i, at, :] = (part_ref[i].astype(f32) * mask).astype(bf16)
    keep = tiled(keep_ref[...], narrow)
    inv = vec_ref[6:7, :narrow]
    c1 = c2 = 0.0
    for i in range(PATCH):
        v = mm(x_ref[i], win_ref[...])
        v_ref[i] = v
        c1, c2 = c1 + colsum(v), c2 + colsum(v * v)
    rstd, shift, a, b = scale_shift(c1, c2, vec_ref[0:1, :narrow], vec_ref[1:2, :narrow], inv, g64_ref[...], False)
    st1_ref[...] = jnp.concatenate([rstd, shift], axis=0)
    for i in range(PATCH):
        act, slope = gelu_both(v_ref[i] * a + b)
        d1_ref[i] = (slope * keep).astype(bf16)
        fill_wide(wide_ref, i, act * keep, edge_ref[...])
    c1 = c2 = 0.0
    for i in range(PATCH):
        v = sum(mm(wide_ref[i + di], bf_ref[di]) for di in range(3))
        v_ref[i] = v
        v = v * keep
        c1, c2 = c1 + colsum(v), c2 + colsum(v * v)
    rstd, shift, a, b = scale_shift(c1, c2, vec_ref[2:3, :narrow], vec_ref[3:4, :narrow], inv, g64_ref[...], False)
    st2_ref[...] = jnp.concatenate([rstd, shift], axis=0)
    c1 = c2 = 0.0
    for i in range(PATCH):
        v = v_ref[i]
        act, slope = gelu_both(v * a + b)
        d2_ref[i] = (slope * keep).astype(bf16)
        n2_ref[i] = (v * rstd + shift).astype(bf16)
        low = (act * keep).astype(bf16)
        p2_ref[i] = low
        v = mm(low, wout_ref[...])
        c1, c2 = c1 + colsum(v), c2 + colsum(v * v)
    st3_ref[...] = jnp.concatenate(
        scale_shift(c1, c2, vec_ref[4:5], vec_ref[5:6], vec_ref[7:8], g256_ref[...], True), axis=0
    )


def stem_front(rank, parts, w_in, b_fwd, w_out, vec, g64, g256, keep, edge, chain=None):
    narrow = parts[0].shape[2]
    s = jax.ShapeDtypeStruct
    vm = pl.BlockSpec(memory_space=pltpu.VMEM)
    low = s((PATCH, TOK, narrow), bf16)
    return launch(
        stem_front_kernel,
        in_specs=[SMEM] + [vm] * 12,
        out_specs=[vm] * 9,
        out_shape=[
            low, s((PATCH + 2, TOK, narrow * 3 // 2), bf16), low, low, low, low,
            s((2, narrow), f32), s((2, narrow), f32), s((4, w_out.shape[1]), f32),
        ],
        scratch_shapes=[pltpu.VMEM((PATCH, TOK, narrow), f32)],
        compiler_params=BIG,
        chain=chain,
        name="stem_front",
    )(rank, *parts, w_in, b_fwd, w_out, vec, g64, g256, keep, edge)


def stem_last_kernel(p2_ref, x_ref, wout_ref, wskip_ref, st_ref, keep_ref, stem_ref, d3_ref):
    keep = tiled(keep_ref[...], wout_ref.shape[1])
    z = mm(p2_ref[0], wout_ref[...]) * st_ref[2:3] + st_ref[3:4] + mm(x_ref[0], wskip_ref[...])
    act, slope = gelu_both(z)
    stem_ref[0] = (act * keep).astype(bf16)
    d3_ref[0] = (slope * keep).astype(bf16)


def stem_last(p2, x, w_out, w_skip, stat, keep, chain=None):
    lanes = w_out.shape[1]
    shape = p2.shape[:2] + (lanes,)
    o = jax.ShapeDtypeStruct(shape, bf16)
    return launch(
        stem_last_kernel,
        grid=(PATCH,),
        in_specs=[slab(p2.shape), slab(x.shape), whole(w_out.shape), whole(w_skip.shape), whole(stat.shape), whole(keep.shape)],
        out_specs=[slab(shape)] * 2,
        out_shape=[o, o],
        compiler_params=BIG,
        chain=chain,
        name="stem_last",
    )(p2, x, w_out, w_skip, stat, keep)


def pack_kernel(rank_ref, x_ref, *refs):
    outs, wide_ref = refs[:-1], refs[-1]
    rows, chans, cols = x_ref.shape[1:]
    for r in range(rows):
        wide_ref[r * cols : (r + 1) * cols, :] = x_ref[0, r].astype(f32).T
    for k, o_ref in enumerate(outs):

        @pl.when(pl.program_id(0) == k)
        def _():
            for i in range(PATCH):
                parts = []
                for j in range(PATCH):
                    parts.append(
                        jnp.concatenate(
                            [
                                wide_ref[pl.ds(r * cols + j, SIDE, stride=PATCH), :]
                                for r in range(i, rows, PATCH)
                            ],
                            axis=0,
                        )
                    )
                o_ref[i] = jnp.concatenate(parts, axis=1).astype(o_ref.dtype)


def pack(rank, x, chain):
    images, rows, cols, chans = x.shape
    x = x.transpose(0, 1, 3, 2)
    shape = (PATCH, rows // PATCH * SIDE, PATCH * chans)
    return launch(
        pack_kernel,
        grid_spec=dict(
            num_scalar_prefetch=1,
            grid=(images,),
            in_specs=[pl.BlockSpec((1, rows, chans, cols), lambda b, r: (b ^ r[0], 0, 0, 0))],
            out_specs=[pl.BlockSpec(shape, lambda b, r: (0, 0, 0))] * images,
            scratch_shapes=[pltpu.VMEM((rows * cols, chans), f32)],
        ),
        out_shape=[jax.ShapeDtypeStruct(shape, x.dtype)] * images,
        compiler_params=MID,
        chain=chain,
        name="pack",
    )(rank, x)


def unpack_kernel(rank_ref, *refs):
    ins, o_ref, row_ref = refs[:-2], refs[-2], refs[-1]
    chans = o_ref.shape[2]
    for k, x_ref in enumerate(ins):

        @pl.when(pl.program_id(0) == k)
        def _():
            for i in range(PATCH):
                v = x_ref[i].astype(f32)
                for p in range(v.shape[0] // SIDE):
                    for j in range(PATCH):
                        row_ref[PATCH * p + i, pl.ds(j, SIDE, stride=PATCH), :] = v[
                            p * SIDE : (p + 1) * SIDE, j * chans : (j + 1) * chans
                        ]

    for r in range(o_ref.shape[1]):
        o_ref[0, r] = row_ref[r].T


def unpack(rank, parts, chain=None):
    images = len(parts)
    _, toks, lanes = parts[0].shape
    shape = (images, toks // SIDE * PATCH, lanes // PATCH, SIDE * PATCH)
    return launch(
        unpack_kernel,
        grid_spec=dict(
            num_scalar_prefetch=1,
            grid=(images,),
            in_specs=[pl.BlockSpec(parts[0].shape, lambda b, r: (0, 0, 0))] * images,
            out_specs=pl.BlockSpec((1,) + shape[1:], lambda b, r: (b ^ r[0], 0, 0, 0)),
            scratch_shapes=[pltpu.VMEM((shape[1], shape[3], shape[2]), f32)],
        ),
        out_shape=jax.ShapeDtypeStruct(shape, f32),
        compiler_params=MID,
        chain=chain,
        name="unpack",
    )(rank, *parts).transpose(0, 1, 3, 2)


def prep_kernel(
    rank_ref, group_ref, in_ref, mid_ref, out_ref, skip_ref, gain_ref, bias_ref, cot_ref,
    w_in, w_out, w_skip, b_fwd, b_bwd, g64, g256, vec, keep, edge, *cots,
):
    for k, ref in enumerate(cots):
        ref[...] = cot_ref[rank_ref[0] ^ k]
    def spread(dst, src):
        dst[...] = jnp.zeros_like(dst)
        c, n = src.shape
        for j in range(PATCH):
            dst[j * c : (j + 1) * c, j * n : (j + 1) * n] = src[...]

    spread(w_in, in_ref)
    spread(w_out, out_ref)
    spread(w_skip, skip_ref)
    b_fwd[...] = jnp.zeros_like(b_fwd)
    b_bwd[...] = jnp.zeros_like(b_bwd)
    c = mid_ref.shape[1]
    for di in range(3):
        for k, src in enumerate(SRCS):
            for j in range(PATCH):
                if abs(src - j) <= 1:
                    dj = src - j + 1
                    b_fwd[di, k * c : (k + 1) * c, j * c : (j + 1) * c] = mid_ref[3 * di + dj]
                    b_bwd[di, j * c : (j + 1) * c, k * c : (k + 1) * c] = mid_ref[8 - 3 * di - dj]
    for ref, chans in ((g64, c), (g256, gain_ref.shape[1] - 2 * c)):
        per = chans // GROUPS
        row = (lax.broadcasted_iota(jnp.int32, ref.shape, 0) & (chans - 1)) // per
        col = (lax.broadcasted_iota(jnp.int32, ref.shape, 1) & (chans - 1)) // per
        ref[...] = jnp.where(row == col, 1.0, 0.0)
    vec[...] = jnp.zeros_like(vec)
    for at, (ref, lo, hi) in enumerate(
        (r, lo, hi)
        for lo, hi in ((0, c), (c, 2 * c), (2 * c, gain_ref.shape[1]))
        for r in (gain_ref, bias_ref)
    ):
        part = jnp.concatenate([ref[:, lo:hi]] * PATCH, axis=1)
        vec[at : at + 1, : part.shape[1]] = part
    limit = jnp.where(group_ref[rank_ref[0]] == 1, FULL // PATCH, SMALL // PATCH)
    inverse = 1.0 / (jnp.full((1, vec.shape[1]), PATCH * PATCH, f32) * (limit * limit).astype(f32))
    vec[6:7] = inverse * (GROUPS / c)
    vec[7:8] = inverse * (GROUPS / (gain_ref.shape[1] - 2 * c))
    t = lax.broadcasted_iota(jnp.int32, keep.shape, 0)
    up = ((t.astype(f32) + 0.5) * (1.0 / SIDE)).astype(jnp.int32)
    t = t - SIDE * up
    keep[...] = jnp.where((up < limit) & (t < limit), 1.0, 0.0)
    left = lax.broadcasted_iota(jnp.int32, edge.shape, 1) < c
    edge[...] = jnp.where(t != jnp.where(left, 0, SIDE - 1), 1.0, 0.0)


def prep(rank, group, conv_in, conv_mid, conv_out, conv_skip, norm_gain, norm_bias, cot, chain=None):
    c, n = conv_out.shape
    s = jax.ShapeDtypeStruct
    shapes = [
        s((PATCH * c, PATCH * c), bf16),
        s((PATCH * c, PATCH * n), bf16),
        s((PATCH * c, PATCH * n), bf16),
        s((3, 6 * c, PATCH * c), bf16),
        s((3, PATCH * c, 6 * c), bf16),
        s((PATCH * c, PATCH * c), f32),
        s((PATCH * c, PATCH * c), f32),
        s((8, PATCH * n), f32),
        s((TOK, 128), f32),
        s((TOK, 2 * c), f32),
    ] + [s(cot.shape[1:], bf16)] * cot.shape[0]
    return launch(
        prep_kernel,
        in_specs=[SMEM, SMEM] + [VMEM] * 7,
        out_specs=[VMEM] * len(shapes),
        out_shape=shapes,
        chain=chain,
        name="prep",
    )(
        rank.reshape(1),
        group,
        conv_in,
        conv_mid.transpose(1, 0, 2),
        conv_out,
        conv_skip,
        norm_gain[None],
        norm_bias[None],
        cot,
    )


def ln_stats(h):
    mean = jnp.mean(h, axis=-1, keepdims=True)
    cen = h - mean
    rstd = lax.rsqrt(jnp.mean(cen * cen, axis=-1, keepdims=True) + 1e-05)
    return cen * rstd, rstd


def ln_back(gy, n, rstd, gain):
    gn = gy * gain
    gh = rstd * (
        gn - jnp.mean(gn, axis=-1, keepdims=True) - n * jnp.mean(gn * n, axis=-1, keepdims=True)
    )
    return gh, jnp.sum(gy * n, axis=0), jnp.sum(gy, axis=0)


def slot_of(q, rank):
    rel = q ^ rank
    return rel & 1, rel >> 1


def store_slot(keep_ref, send_ref, core, at, value):
    @pl.when(core == 0)
    def _():
        keep_ref[at] = value

    @pl.when(core == 1)
    def _():
        send_ref[at] = value


def store_quarters(rank_ref, total, keep_ref, send_ref):
    total = total.astype(bf16)
    rows = keep_ref.shape[-2]
    for q in range(total.shape[0] // rows):
        core, over = slot_of(q, rank_ref[0])
        store_slot(keep_ref, send_ref, core, (0, over, 0), total[q * rows : (q + 1) * rows])


def wgrad_qkv_kernel(rank_ref, a_ref, g_ref, a2_ref, g2_ref, keep_ref, send_ref):
    last = pl.program_id(0) == pl.num_programs(0) - 1

    @pl.when(jnp.logical_not(last))
    def _():
        store_quarters(rank_ref, mm_tn(a_ref[...], g_ref[...]), keep_ref, send_ref)

    @pl.when(last)
    def _():
        store_quarters(rank_ref, mm_tn(a2_ref[...], g2_ref[...]), keep_ref, send_ref)


def wgrad_qkv(rank, a, g, a2, g2, chain=None):
    toks, k = a.shape
    rows = k // 4
    o = jax.ShapeDtypeStruct((2, 2, 2, rows, k), bf16)
    spec = pl.BlockSpec((1, 2, 1, rows, k), lambda b: (b // 2, 0, b % 2, 0, 0))
    return launch(
        wgrad_qkv_kernel,
        grid=(4,),
        in_specs=[
            SMEM, whole(a.shape), pl.BlockSpec((toks, k), lambda b: (0, jnp.minimum(b, 2))),
            whole(a.shape), whole(a.shape),
        ],
        out_specs=[spec, spec],
        out_shape=[o, o],
        compiler_params=MID,
        chain=chain,
        name="wgrad_qkv",
    )(rank, a, g, a2, g2)


def wgrad_rows_kernel(rank_ref, a_ref, g_ref, keep_ref, send_ref):
    total = mm_tn(a_ref[...], g_ref[...]).astype(bf16)
    step = pl.program_id(0)
    rows = total.shape[0] // (1 if len(keep_ref.shape) == 2 else keep_ref.shape[0])

    def put(ref):
        if len(ref.shape) == 2:
            ref[...] = total
        else:
            for h in range(ref.shape[0]):
                ref[h] = total[h * rows : (h + 1) * rows]

    @pl.when(step < 2)
    def _():
        put(send_ref)

    @pl.when(step >= 2)
    def _():
        put(keep_ref)


def wgrad_rows(rank, a, g, outer, chain=None):
    toks, n = g.shape
    rows = a.shape[2] if a.ndim == 3 else a.shape[1] // 4

    def quarter(step, rank_ref):
        rel = (step % 2) * 2 + jnp.where(step < 2, 1, 0)
        return rel ^ rank_ref[0]

    if a.ndim == 3:
        a_spec = pl.BlockSpec((None, toks, rows), lambda s, r: (quarter(s, r), 0, 0))
    else:
        a_spec = pl.BlockSpec((toks, rows), lambda s, r: (0, quarter(s, r)))
    if outer > 1:
        shape = (outer, 2, rows // outer, n)
        block = (outer, None, rows // outer, n)
        specs = [
            pl.BlockSpec(block, lambda s, r: (0, jnp.maximum(s - 2, 0), 0, 0)),
            pl.BlockSpec(block, lambda s, r: (0, jnp.minimum(s, 1), 0, 0)),
        ]
    else:
        shape = (2, rows, n)
        specs = [
            pl.BlockSpec((None, rows, n), lambda s, r: (jnp.maximum(s - 2, 0), 0, 0)),
            pl.BlockSpec((None, rows, n), lambda s, r: (jnp.minimum(s, 1), 0, 0)),
        ]
    o = jax.ShapeDtypeStruct(shape, bf16)
    return launch(
        wgrad_rows_kernel,
        grid_spec=dict(
            num_scalar_prefetch=1,
            grid=(4,),
            in_specs=[a_spec, pl.BlockSpec((toks, n), lambda s, r: (0, 0))],
            out_specs=specs,
        ),
        out_shape=[o, o],
        compiler_params=MID,
        chain=chain,
        name="wgrad_rows",
    )(rank, a, g)


VECS = 6


def collect_kernel(rank_ref, in_ref, mid_ref, cout_ref, skip_ref, co1_ref, co2_ref, co3_ref, *refs):
    vecs, up_ref, (keep_ref, send_ref) = refs[:VECS], refs[VECS], refs[VECS + 1 :]
    c, lanes = cout_ref.shape
    part = c // 4
    norms = []
    for row in (3, 2):
        norms.append(
            jnp.concatenate(
                [fold(co1_ref[row : row + 1]), fold(co2_ref[row : row + 1]), co3_ref[row : row + 1, :lanes]],
                axis=1,
            )
        )

    def full(v):
        gap = lanes - v.shape[1]
        return jnp.concatenate([v, jnp.zeros((v.shape[0], gap), f32)], axis=1) if gap else v

    for q in range(4):
        rows = slice(q * part, (q + 1) * part)
        blocks = [cout_ref[rows], skip_ref[rows]]
        for di in range(3):
            blocks.append(full(jnp.concatenate([mid_ref[3 * di + dj, rows] for dj in range(3)], axis=1)))
        blocks.append(full(in_ref[rows]))

        def quarter(v):
            n = v.shape[1] // 4
            return v[:, q * n : (q + 1) * n]

        small = [full(quarter(v[...])) for v in vecs]
        up = quarter(up_ref[...])
        small += [up[:, k * lanes : (k + 1) * lanes] for k in range(up.shape[1] // lanes)]
        small += [full(quarter(v)) for v in norms]
        small.append(jnp.zeros((16 - len(small), lanes), f32))
        total = jnp.concatenate(blocks + small, axis=0)
        core, over = slot_of(q, rank_ref[0])
        store_slot(keep_ref, send_ref, core, over, total)


def collect(rank, g_in, g_mid, g_cout, g_skip, co1, co2, co3, vecs, up, chain=None):
    c, lanes = g_cout.shape
    rows = 6 * (c // 4) + 16
    o = jax.ShapeDtypeStruct((2, rows, lanes), f32)
    return launch(
        collect_kernel,
        in_specs=[SMEM] + [VMEM] * (8 + VECS),
        out_specs=[VMEM] * 2,
        out_shape=[o, o],
        compiler_params=MID,
        chain=chain,
        name="collect",
    )(rank, g_in, g_mid, g_cout, g_skip, co1, co2, co3, *vecs, up)


def deal_kernel(v_ref, in_ref, mid_ref, cout_ref, skip_ref, gain_ref, bias_ref, *refs):
    vecs, up_ref = refs[:VECS], refs[VECS]
    part, c = in_ref.shape
    lanes = v_ref.shape[1]
    cout_ref[...] = v_ref[:part]
    skip_ref[...] = v_ref[part : 2 * part]
    for di in range(3):
        for dj in range(3):
            mid_ref[3 * di + dj] = v_ref[(2 + di) * part : (3 + di) * part, dj * c : (dj + 1) * c]
    in_ref[...] = v_ref[5 * part : 6 * part, :c]
    at = 6 * part
    for ref in vecs:
        ref[...] = v_ref[at : at + 1, : ref.shape[1]]
        at += 1
    for k in range(up_ref.shape[1] // lanes):
        up_ref[:, k * lanes : (k + 1) * lanes] = v_ref[at : at + 1]
        at += 1
    gain_ref[...] = v_ref[at : at + 1, : gain_ref.shape[1]]
    bias_ref[...] = v_ref[at + 1 : at + 2, : bias_ref.shape[1]]


def deal(v, part, c, n, norms, width, hidden):
    s = jax.ShapeDtypeStruct
    shapes = [s((part, c), f32), s((9, part, c), f32), s((part, n), f32), s((part, n), f32)]
    shapes += [s((1, norms), f32)] * 2 + [s((1, width), f32)] * VECS + [s((1, hidden), f32)]
    return launch(
        deal_kernel,
        in_specs=[VMEM],
        out_specs=[VMEM] * len(shapes),
        out_shape=shapes,
        compiler_params=MID,
        name="deal",
    )(v)


def merge_kernel(bit_ref, a_ref, b_ref, c_ref, d_ref, keep_ref, send_ref):
    keep_ref[...] = (a_ref[...].astype(f32) + b_ref[...].astype(f32)).astype(bf16)
    send_ref[...] = (c_ref[...].astype(f32) + d_ref[...].astype(f32)).astype(bf16)


def merge(bit, kept, got, chain=None):
    rows, n = kept.shape
    half = rows // 2
    tiles = 2 if half >= 512 else 1
    block = (half // tiles, n)
    mine = pl.BlockSpec(block, lambda t, b: (b[0] * tiles + t, 0))
    other = pl.BlockSpec(block, lambda t, b: ((1 - b[0]) * tiles + t, 0))
    out = pl.BlockSpec(block, lambda t, b: (t, 0))
    o = jax.ShapeDtypeStruct((half, n), bf16)
    return launch(
        merge_kernel,
        grid_spec=dict(
            num_scalar_prefetch=1,
            grid=(tiles,),
            in_specs=[mine, mine, other, other],
            out_specs=[out, out],
        ),
        out_shape=[o, o],
        compiler_params=MID,
        chain=chain,
        name="merge",
    )(bit, kept, got, kept, got)


def plus_kernel(a_ref, b_ref, o_ref):
    o_ref[...] = (a_ref[...].astype(f32) + b_ref[...].astype(f32)).astype(o_ref.dtype)


def plus(a, b, chain=None):
    return launch(
        plus_kernel,
        in_specs=[VMEM] * 2,
        out_specs=VMEM,
        out_shape=jax.ShapeDtypeStruct(a.shape, a.dtype),
        compiler_params=MID,
        chain=chain,
        name="plus",
    )(a, b)


def gather_kernel(rank_ref, p0_ref, p1_ref, p2_ref, p3_ref, keep_ref, o_ref, sum_ref):
    total = 0.0
    for k, ref in enumerate((p0_ref, p1_ref, p2_ref, p3_ref)):
        toks, n = ref.shape
        at = pl.ds(pl.multiple_of((rank_ref[0] ^ k) * toks, 16), toks)
        v = ref[...].astype(f32) * tiled(keep_ref[at, :], n)
        total = total + colsum(v)
        o_ref[at, :] = v.astype(bf16)
    sum_ref[...] = total


def gather(rank, parts, keep, chain=None):
    toks, n = parts[0].shape
    return launch(
        gather_kernel,
        in_specs=[SMEM] + [VMEM] * 5,
        out_specs=[VMEM] * 2,
        out_shape=[jax.ShapeDtypeStruct((4 * toks, n), bf16), jax.ShapeDtypeStruct((1, n), f32)],
        compiler_params=MID,
        chain=chain,
        name="gather",
    )(rank, *parts, keep)


def split_kernel(a_ref, b_ref, keep_ref, send_ref):
    half = keep_ref.shape[0]
    keep_ref[...] = a_ref[:half] + b_ref[:half]
    send_ref[...] = a_ref[half:] + b_ref[half:]


def split(a, b, chain=None):
    o = jax.ShapeDtypeStruct((a.shape[0] // 2,) + a.shape[1:], a.dtype)
    return launch(
        split_kernel,
        in_specs=[VMEM] * 2,
        out_specs=[VMEM] * 2,
        out_shape=[o, o],
        compiler_params=MID,
        chain=chain,
        name="split",
    )(a, b)


def merge_two(bit, kept, got, kept2, got2, chain=None):
    def body(bit_ref, a_ref, b_ref, c_ref, d_ref, keep_ref, send_ref):
        def put(first_ref, second_ref):
            first_ref[...] = (a_ref[...].astype(f32) + b_ref[...].astype(f32)).astype(bf16)
            second_ref[...] = (c_ref[...].astype(f32) + d_ref[...].astype(f32)).astype(bf16)

        @pl.when(bit_ref[0] == 0)
        def _():
            put(keep_ref, send_ref)

        @pl.when(bit_ref[0] == 1)
        def _():
            put(send_ref, keep_ref)

    o = jax.ShapeDtypeStruct(kept.shape, bf16)
    return launch(
        body,
        in_specs=[SMEM] + [VMEM] * 4,
        out_specs=[VMEM] * 2,
        out_shape=[o, o],
        compiler_params=MID,
        chain=chain,
        name="merge_two",
    )(bit, kept, got, kept2, got2)


def put_blocks(ref, value, first, rows):
    n = value.shape[1]
    for k in range(value.shape[0] // rows):
        ref[:, pl.ds(pl.multiple_of((first + k) * n, 128), n)] = value[k * rows : (k + 1) * rows]


def finish_mlp(bit, own, got, ranks, chain=None):
    rows, n = own.shape
    half, part = rows // 2, n // ranks

    def body(bit_ref, own_ref, got_ref, down_ref, up_ref):
        for ref, place in ((own_ref, bit_ref[0]), (got_ref, 1 - bit_ref[0])):
            v = ref[...].astype(f32)
            down_ref[pl.ds(pl.multiple_of(place * half, 16), half), :] = v[:half]
            put_blocks(up_ref, v[half:], place * (half // part), part)

    s = jax.ShapeDtypeStruct
    return launch(
        body,
        in_specs=[SMEM, VMEM, VMEM],
        out_specs=[VMEM] * 2,
        out_shape=[s((rows, n), f32), s((part, rows // part * n), f32)],
        compiler_params=MID,
        chain=chain,
        name="finish_mlp",
    )(bit, own, got)


def finish_qkv(bit, own, got, ranks, chain=None):
    rows, n = own.shape
    part = n // ranks

    def body(bit_ref, own_ref, got_ref, qkv_ref, out_ref):
        def put(low_ref, high_ref):
            qkv_ref[:, :n] = low_ref[:part].astype(f32)
            qkv_ref[:, n : 2 * n] = low_ref[part:].astype(f32)
            qkv_ref[:, 2 * n :] = high_ref[:part].astype(f32)
            out_ref[...] = high_ref[part:].astype(f32)

        @pl.when(bit_ref[0] == 0)
        def _():
            put(own_ref, got_ref)

        @pl.when(bit_ref[0] == 1)
        def _():
            put(got_ref, own_ref)

    s = jax.ShapeDtypeStruct
    return launch(
        body,
        in_specs=[SMEM, VMEM, VMEM],
        out_specs=[VMEM] * 2,
        out_shape=[s((part, 3 * n), f32), s((part, n), f32)],
        compiler_params=MID,
        chain=chain,
        name="finish_qkv",
    )(bit, own, got)


def join_kernel(bit_ref, own_ref, got_ref, o_ref):
    o_ref[bit_ref[0]] = own_ref[...].astype(o_ref.dtype)
    o_ref[1 - bit_ref[0]] = got_ref[...].astype(o_ref.dtype)


def join(bit, own, got, dtype, chain=None):
    rows, n = own.shape
    o = launch(
        join_kernel,
        in_specs=[SMEM, VMEM, VMEM],
        out_specs=VMEM,
        out_shape=jax.ShapeDtypeStruct((2, rows, n), dtype),
        compiler_params=MID,
        chain=chain,
        name="join",
    )(bit, own, got)
    return o.reshape(2 * rows, n)


def norm_back(gy, h, gain):
    n, rstd = ln_stats(h)
    gn = gy * gain
    gh = rstd * (
        gn - jnp.mean(gn, axis=-1, keepdims=True) - n * jnp.mean(gn * n, axis=-1, keepdims=True)
    )
    return gh, colsum(gy * n), colsum(gy)


def mlp_out_kernel(rank_ref, a_ref, w_ref, h_ref, bias_ref, keep_ref, o0_ref, o1_ref, o2_ref, o3_ref, acc_ref):
    step = pl.program_id(0)
    add_to(acc_ref, mm(a_ref[...], w_ref[...]), step == 0)

    @pl.when(step == pl.num_programs(0) - 1)
    def _():
        keep = tiled(keep_ref[...], acc_ref.shape[1])
        acc_ref[...] = (acc_ref[...] + h_ref[...] + bias_ref[...]) * keep
        for k, o_ref in enumerate((o0_ref, o1_ref, o2_ref, o3_ref)):
            toks = o_ref.shape[0]
            at = pl.ds(pl.multiple_of((rank_ref[0] ^ k) * toks, 16), toks)
            o_ref[...] = acc_ref[at, :].astype(bf16)


def mlp_out(rank, act, weight, hidden, bias, keep, chain=None):
    toks, n = hidden.shape
    part = jax.ShapeDtypeStruct((toks // 4, n), bf16)
    return launch(
        mlp_out_kernel,
        grid=(act.shape[1] // n,),
        in_specs=[
            SMEM, pl.BlockSpec((toks, n), lambda b: (0, b)), pl.BlockSpec((n, n), lambda b: (b, 0)),
            whole((toks, n)), whole((1, n)), whole(keep.shape),
        ],
        out_specs=[whole(part.shape)] * 4,
        out_shape=[part] * 4,
        scratch_shapes=[pltpu.VMEM((toks, n), f32)],
        compiler_params=MID,
        chain=chain,
        name="mlp_out",
    )(rank, act, weight, hidden, bias[None], keep)


def scatter_kernel(rank_ref, *refs):
    for k, ref in enumerate(refs[:-1]):
        refs[-1][rank_ref[0] ^ k] = ref[...]


def scatter(rank, parts, chain=None):
    return launch(
        scatter_kernel,
        in_specs=[SMEM] + [VMEM] * len(parts),
        out_specs=VMEM,
        out_shape=jax.ShapeDtypeStruct((len(parts),) + parts[0].shape, parts[0].dtype),
        compiler_params=MID,
        chain=chain,
        name="scatter",
    )(rank, *parts)


def mlp_back_kernel(
    rank_ref, g_ref, down_ref, slope_ref, n_ref, up_ref, h_ref, gain_ref, out_ref,
    keep_ref, send_ref, bias_ref, gh_ref, low_ref, att_ref, dgain_ref, dbias_ref, acc_ref,
):
    step = pl.program_id(0)
    g = mm_nt(g_ref[...], down_ref[...]) * slope_ref[...].astype(f32)
    bias_ref[...] = colsum(g)
    g = g.astype(bf16)
    store_quarters(rank_ref, mm_tn(n_ref[...], g), keep_ref, send_ref)
    add_to(acc_ref, mm_nt(g, up_ref[...]), step == 0)

    @pl.when(step == pl.num_programs(0) - 1)
    def _():
        gh, dgain_ref[...], dbias_ref[...] = norm_back(acc_ref[...], h_ref[...], gain_ref[...])
        gh = gh + g_ref[...].astype(f32)
        gh_ref[...] = gh
        low = gh.astype(bf16)
        low_ref[...] = low
        att_ref[...] = mm_nt(low, out_ref[...]).astype(bf16)


def mlp_back(rank, g, down, slope, normed, up, hidden, gain, out_weight, chain=None):
    toks, n = hidden.shape
    blocks = up.shape[1] // n
    half = blocks // 2
    rows = n // 4
    s = jax.ShapeDtypeStruct
    full, row = whole((toks, n)), whole((1, n))
    lanes = pl.BlockSpec((toks, n), lambda b: (0, b))
    part = pl.BlockSpec((1, 2, 1, rows, n), lambda b: (b // half, 0, b % half, 0, 0))
    parts = s((2, 2, half, rows, n), bf16)
    keep, send, bias, *rest = launch(
        mlp_back_kernel,
        grid=(blocks,),
        in_specs=[
            SMEM, full, pl.BlockSpec((n, n), lambda b: (b, 0)), lanes, full,
            pl.BlockSpec((n, n), lambda b: (0, b)), full, row, whole((n, n)),
        ],
        out_specs=[part, part, pl.BlockSpec((1, n), lambda b: (0, b)), full, full, full, row, row],
        out_shape=[
            parts, parts, s((1, up.shape[1]), f32), s((toks, n), f32), s((toks, n), bf16), s((toks, n), bf16),
            s((1, n), f32), s((1, n), f32),
        ],
        scratch_shapes=[pltpu.VMEM((toks, n), f32)],
        compiler_params=pltpu.CompilerParams(vmem_limit_bytes=40 * 1024 * 1024),
        chain=chain,
        hbm=True,
        name="mlp_back",
    )(rank, g, down, slope, normed, up, hidden, gain[None], out_weight)
    return (keep, send), bias, *rest


def qkv_back_kernel(g_ref, w_ref, h_ref, gain_ref, gh2_ref, low_ref, dgain_ref, dbias_ref, sum_ref, acc_ref):
    step = pl.program_id(0)
    add_to(acc_ref, mm_nt(g_ref[...], w_ref[...]), step == 0)

    @pl.when(step == pl.num_programs(0) - 1)
    def _():
        gh, dgain_ref[...], dbias_ref[...] = norm_back(acc_ref[...], h_ref[...], gain_ref[...])
        gh = gh + gh2_ref[...]
        sum_ref[...] = colsum(gh)
        low_ref[...] = gh.astype(bf16)


def qkv_back(g, weight, hidden, gain, gh2, chain=None):
    toks, n = hidden.shape
    s = jax.ShapeDtypeStruct
    full, row = whole((toks, n)), whole((1, n))
    return launch(
        qkv_back_kernel,
        grid=(g.shape[1] // n,),
        in_specs=[
            pl.BlockSpec((toks, n), lambda b: (0, b)), pl.BlockSpec((n, n), lambda b: (0, b)), full, row, full,
        ],
        out_specs=[full, row, row, row],
        out_shape=[s((toks, n), bf16)] + [s((1, n), f32)] * 3,
        scratch_shapes=[pltpu.VMEM((toks, n), f32)],
        compiler_params=MID,
        chain=chain,
        name="qkv_back",
    )(g, weight, hidden, gain[None], gh2)


def attend_kernel(keep_ref, q_ref, k_ref, v_ref, o_ref, l_ref):
    scale = HEAD_DIM**-0.5
    valid = keep_ref[...] > 0
    outs = []
    for h in range(2):
        lanes = slice(h * HEAD_DIM, (h + 1) * HEAD_DIM)
        q, k, v = q_ref[:, lanes], k_ref[:, lanes], v_ref[:, lanes]
        s = jnp.where(valid, mm_nt(k, q) * scale, -1000000000.0)
        top = jnp.max(s, axis=0, keepdims=True)
        e = jnp.exp(s - top)
        total = jnp.sum(e, axis=0, keepdims=True)
        outs.append(mm_tn(v, e.astype(bf16)) / total)
        l_ref[0, h : h + 1, :] = top + jnp.log(total)
    o_ref[...] = jnp.concatenate(outs, axis=0).T.astype(bf16)

def attend(qkv, keep, chain=None):
    tok, width3 = qkv.shape
    pairs = HEADS // 2
    two = 2 * HEAD_DIM
    def spec(kind):
        return pl.BlockSpec((tok, two), lambda h: (0, kind * pairs + h))
    return launch(
        attend_kernel, grid=(pairs,),
        in_specs=[pl.BlockSpec((tok, 1), lambda h: (0, 0)), spec(0), spec(1), spec(2)],
        out_specs=[spec(0), pl.BlockSpec((1, 2, tok), lambda h: (h, 0, 0))],
        out_shape=[jax.ShapeDtypeStruct((tok, width3 // 3), bf16), jax.ShapeDtypeStruct((pairs, 2, tok), f32)],
        compiler_params=pltpu.CompilerParams(vmem_limit_bytes=40*1024*1024),
        chain=chain,
        name="attend",
    )(keep, qkv, qkv, qkv)

def attend_back_kernel(keep_ref, q_ref, k_ref, v_ref, g_ref, l_ref, o_ref):
    scale = HEAD_DIM**-0.5
    valid = keep_ref[...] > 0
    gqs, gks, gvs = [], [], []
    for h in range(2):
        lanes = slice(h * HEAD_DIM, (h + 1) * HEAD_DIM)
        q, k, v, g = q_ref[:, lanes], k_ref[:, lanes], v_ref[:, lanes], g_ref[:, lanes]
        s = jnp.where(valid, mm_nt(k, q) * scale, -1000000000.0)
        p = jnp.exp(s - l_ref[0, h : h + 1, :])
        gp = mm_nt(v, g)
        dot = jnp.sum(gp * p, axis=0, keepdims=True)
        gs = (p * (gp - dot)).astype(bf16)
        gvs.append(mm(p.astype(bf16), g))
        gks.append(mm(gs, q) * scale)
        gqs.append(mm_tn(k, gs) * scale)
    width = o_ref.shape[1] // 3
    step = pl.program_id(0)
    for kind, value in enumerate(
        (jnp.concatenate(gqs, axis=0).T, jnp.concatenate(gks, axis=1), jnp.concatenate(gvs, axis=1))
    ):
        lanes = pl.ds(pl.multiple_of(kind * width + step * 2 * HEAD_DIM, 128), 2 * HEAD_DIM)
        o_ref[:, lanes] = value.astype(bf16)


def attend_back(qkv, keep, g, logs, chain=None):
    tok, width3 = qkv.shape
    pairs = HEADS // 2
    two = 2 * HEAD_DIM
    def spec(kind):
        return pl.BlockSpec((tok, two), lambda h: (0, kind * pairs + h))
    return launch(
        attend_back_kernel, grid=(pairs,),
        in_specs=[pl.BlockSpec((tok, 1), lambda h: (0, 0)), spec(0), spec(1), spec(2), spec(0), pl.BlockSpec((1, 2, tok), lambda h: (h, 0, 0))],
        out_specs=whole((tok, width3)),
        out_shape=jax.ShapeDtypeStruct((tok, width3), bf16),
        compiler_params=pltpu.CompilerParams(vmem_limit_bytes=40*1024*1024),
        chain=chain,
        name="attend_back",
    )(keep, qkv, qkv, qkv, g, logs)


def per_image(parts, cots, made, params, flows):
    (
        conv_in,
        conv_mid,
        conv_out,
        conv_skip,
        norm_gain,
        norm_bias,
        patch_weight,
        patch_bias,
        attn_gain,
        attn_bias,
        qkv_weight,
        out_weight,
        mlp_gain,
        mlp_bias,
        up_weight,
        up_bias,
        down_weight,
        down_bias,
    ) = params
    w_in, w_out, w_skip, b_fwd, b_bwd, g64, g256, vec, keep_wide, edge = made
    c0 = conv_in.shape[0]
    c3 = conv_out.shape[1]
    ranks = lax.axis_size("row")
    keep = keep_wide[:, :1]
    chain = flows.chain
    x, wide, d1, p2, d2, n2, st1, st2, st3 = stem_front(
        flows.rank, parts, w_in, b_fwd, w_out, vec, g64, g256, keep_wide, edge, chain
    )
    stem, d3 = stem_last(p2, x, w_out, w_skip, st3, keep_wide, chain)
    pw = patch_weight.reshape(PATCH, PATCH * c3, -1)
    hidden = patch_bias
    for i in range(PATCH):
        hidden = hidden + mm(stem[i], pw[i])
    na, ra = ln_stats(hidden)
    normed = (na * attn_gain + attn_bias).astype(bf16)
    qkv = mm(normed, qkv_weight).astype(bf16)
    attended, logs = attend(qkv, keep, chain)
    hidden2 = hidden + mm(attended, out_weight)
    nm, rm = ln_stats(hidden2)
    normed2 = (nm * mlp_gain + mlp_bias).astype(bf16)
    pre = mm(normed2, up_weight) + up_bias
    act, dact = gelu_both(pre)
    act = act.astype(bf16)
    g_low, grad_down_bias = gather(flows.rank, cots, keep_wide, chain)
    rank = flows.rank
    flows.begin("down", wgrad_rows(rank, act, g_low, 1, chain), order_of("x"))
    parts, grad_up_bias, g_h2, g_h2_low, g_att, grad_mlp_gain, grad_mlp_bias = mlp_back(
        rank, g_low, down_weight, dact.astype(bf16), normed2, up_weight, hidden2, mlp_gain, out_weight, chain
    )
    flows.begin("up", parts, order_of("y"))
    flows.pump()
    flows.pump()
    g_qkv = attend_back(qkv, keep, g_att, logs, chain)
    flows.pump()
    g_h, grad_attn_gain, grad_attn_bias, grad_patch_bias = qkv_back(
        g_qkv, qkv_weight, hidden, attn_gain, g_h2, chain
    )
    flows.begin("patch", wgrad_rows(rank, stem, g_h, 1, chain), order_of("x"))
    flows.pump()
    parts = wgrad_qkv(rank, normed, g_qkv, attended, g_h2_low, chain)
    flows.begin("qkv", parts, order_of("y"), finish_qkv)
    flows.pump()
    g_z, co3, grad_skip = stem_back1(
        g_h, pw, d3, p2, x, w_out, st3, vec, g256, flows.chain
    )
    flows.pump()
    g_2, co2, grad_cout = stem_back2(
        g_z, p2, d2, n2, w_out, st3, co3, vec, g64, keep_wide, flows.chain
    )
    flows.pump()
    g_1, co1, grad_mid = stem_back3(
        g_2, n2, wide, b_bwd, d1, x, w_in, st1, st2, co2, vec, g64, keep_wide, edge, flows.chain
    )
    flows.pump()
    *input_grad, grad_in = stem_back4(
        rank, g_1, x, g_z, w_in, w_skip, st1, co1, vec, keep_wide, ranks, flows.chain
    )
    vecs = (grad_patch_bias, grad_attn_gain, grad_attn_bias, grad_mlp_gain, grad_mlp_bias, grad_down_bias)
    small = collect(
        rank, grad_in, grad_mid, grad_cout, grad_skip, co1, co2, co3,
        vecs, grad_up_bias, flows.chain
    )
    out = (act, down_weight, hidden2, down_bias, keep_wide)
    return out, input_grad, small


def swap(v, axis, step):
    count = lax.axis_size(axis)
    return lax.ppermute(v, axis, [(i, i ^ step) for i in range(count)])


def steps_of(axis):
    count = lax.axis_size(axis)
    return [1 << b for b in range(count.bit_length() - 1)]


def bit_of(axis, step):
    return ((lax.axis_index(axis) & step) // step).astype(jnp.int32).reshape(1)


class Flow:
    def __init__(self, kept, sent, order, last=None):
        n = kept.shape[-1]
        self.kept = kept.reshape(-1, n)
        self.sent = sent.reshape(-1, n)
        self.todo = list(order)
        self.undo = [s for a, s in reversed(order) if a == "img"]
        self.last = last
        self.done = False
        self.start()

    def start(self):
        if self.todo:
            self.got = swap(self.sent, *self.todo[0])
        elif self.undo:
            self.got = swap(self.kept, "img", self.undo[0])

    def step(self, chain):
        if self.todo:
            self.todo.pop(0)
            if self.todo:
                axis, step = self.todo[0]
                bit = bit_of("img", step) if axis == "img" else jnp.zeros((1,), jnp.int32)
                self.kept, self.sent = merge(bit, self.kept, self.got, chain)
            else:
                self.kept = plus(self.kept, self.got, chain)
        else:
            step = self.undo.pop(0)
            self.done = not self.undo
            bit = bit_of("img", step)
            if self.done and self.last:
                self.kept = self.last(bit, self.kept, self.got, lax.axis_size("row"), chain)
            else:
                self.kept = join(bit, self.kept, self.got, f32 if self.done else bf16, chain)
        self.start()


class Pair(Flow):
    def __init__(self, one, two, last, chain):
        order = [(a, s) for a, s in order_of("x") if a == "img"]
        self.undo = [s for a, s in reversed(order)]
        order = order[1:]
        self.todo = list(order)
        self.last = last
        self.done = False
        bit = bit_of(*order[0])
        self.kept, self.sent = merge_two(bit, one.kept, one.got, two.kept, two.got, chain)
        self.start()


class SmallFlow:
    def __init__(self, kept, sent):
        self.kept, self.sent = kept, sent
        self.todo = order_of("x")
        self.done = False
        self.got = swap(self.sent, *self.todo[0])

    def step(self, chain):
        self.todo.pop(0)
        self.done = not self.todo
        if not self.done and self.todo[0][0] == "row":
            self.kept, self.sent = split(self.kept, self.got, chain)
        else:
            self.kept = self.sent = plus(self.kept, self.got, chain)
        if not self.done:
            self.got = swap(self.sent, *self.todo[0])


class Flows:
    def __init__(self, plan):
        self.plan = list(plan)
        self.live = {}
        self.chain = Chain()
        self.rank = lax.axis_index("row").reshape(1)
        self.tasks = {"pair": self.pair}

    def begin(self, name, parts, order, last=None):
        self.live[name] = Flow(*parts, order, last)

    def pair(self):
        one, two = self.live.pop("down"), self.live.pop("up")
        self.live["mlp"] = Pair(one, two, finish_mlp, self.chain)

    def pump(self):
        for name in self.plan.pop(0):
            if name in self.tasks:
                self.tasks.pop(name)()
            else:
                self.live[name].step(self.chain)

    def drain(self):
        while not all(flow.done for flow in self.live.values()):
            for flow in self.live.values():
                if not flow.done:
                    flow.step(self.chain)


def order_of(first):
    row = [("row", s) for s in steps_of("row")]
    img = [("img", s) for s in steps_of("img")]
    if first == "y":
        return row[:1] + img[:1] + row[1:] + img[1:]
    if first == "z":
        return row[:1] + img[1:] + row[1:] + img[:1]
    return row + img


PLAN = (
    ("down", ),
    ("up", ),
    (),
    ("down", "up", ),
    ("patch", "qkv", ),
    ("pair", ),
    ("mlp", "qkv", ),
    ("patch", "mlp", ),
    ("mlp", "qkv", "patch", "mlp", "unpack", "small", "patch", "out", "qkv", "small1", "patch", "qkv", "small1", "patch", "qkv", "small1", "patch", "qkv", "mlp", "scatter", "small1", "small1", "patch", "qkv", ),
)


def exchange(parts):
    return [parts[0]] + [swap(parts[k], "row", k) for k in range(1, len(parts))]


def per_device(stem_input, group, *rest):
    params, cot = rest[:-1], rest[-1]
    images, row_count, col_count, c0 = stem_input.shape
    ranks = lax.axis_size("row")
    assert images == ranks
    flows = Flows(PLAN)
    rank = flows.rank
    front = flows.chain
    parts = pack(rank, stem_input, front)
    made = prep(rank, group, *rest[:6], cot, front)
    parts = exchange(parts)
    made, cots = made[:10], exchange(made[10:])
    out, input_grad, small = per_image(parts, cots, made, params, flows)
    chain = flows.chain
    done = {}

    def start_small():
        flows.live["small1"] = SmallFlow(*small)

    def start_out():
        done["out"] = exchange(mlp_out(rank, *out, chain))

    def end_input():
        done["ig"] = unpack(rank, exchange(input_grad), chain)

    def end_out():
        done["block"] = scatter(rank, done["out"], chain)

    flows.tasks.update(small=start_small, out=start_out, unpack=end_input, scatter=end_out)
    flows.pump()
    for name in list(flows.tasks):
        if name != "pair":
            flows.tasks.pop(name)()
    flows.drain()
    ig, block_out = done["ig"], done["block"]
    small = deal(
        flows.live["small1"].kept[0], c0 // ranks, c0, rest[2].shape[1],
        rest[4].shape[0] // ranks, rest[6].shape[1] // ranks, rest[15].shape[0] // ranks,
    )
    qkv, out = flows.live["qkv"].kept
    down, up = flows.live["mlp"].kept
    vecs = [v[0] for v in small[4:]]
    shares = [small[0], small[1].transpose(1, 0, 2), small[2], small[3], vecs[0], vecs[1]]
    shares += [flows.live["patch"].kept, vecs[2], vecs[3], vecs[4]]
    shares += [qkv, out, vecs[5], vecs[6]]
    shares += [up, vecs[8], down, vecs[7]]
    return (block_out, ig) + tuple(shares)


def solution(mesh):
    rep = P()
    in_specs = (P("img", "row", None, None), P("img")) + (rep,) * 18 + (P("img", "row", None),)
    dims = (2, 3, 2, 2, 1, 1, 2, 1, 1, 1, 2, 2, 1, 1, 2, 1, 2, 1)
    out_specs = (P("img", "row", None), P("img", "row", None, None)) + tuple(
        P("row", *([None] * (n - 1))) for n in dims
    )
    return jax.shard_map(
        per_device, mesh=mesh, in_specs=in_specs, out_specs=out_specs, check_vma=False
    )
```
